32 devices in a mesh: batch: 16 (over z, y, x), mp: 2 (over core).
Axes of the slice: x: 2, y: 2, z: 4, core: 2. Of those that a mesh axis runs over, the one named last changes fastest.
Arguments:
- hidden_in: bfloat16 [32, 1024, 768], P('batch', 'mp'), may hold values from -6 to 6
- memory_flags: int32 [32], P('batch'), may hold values 0 or 1
- memory_coeffs: bfloat16 [32, 256, 768], P('batch', 'mp'), may hold values from -6 to 6
- first_gain: float32 [768], replicated, may hold values from 0.25 to 1.75
- first_bias: float32 [768], replicated, may hold values from -1.5 to 1.5
- query_key_value_matrix: bfloat16 [768, 3, 768], P(None, None, 'mp'), may hold values from -0.21875 to 0.21875
- qv_bias: bfloat16 [2, 768], P(None, 'mp'), may hold values from -1.5 to 1.5
- memory_weight: bfloat16 [2, 12, 256], P(None, 'mp'), may hold values from -0.1875 to 0.1875
- memory_bias: bfloat16 [2, 12], P(None, 'mp'), may hold values from -1.5 to 1.5
- output_matrix: bfloat16 [768, 768], P('mp'), may hold values from -1.25 to 1.25
- out_bias: float32 [768], replicated, may hold values from -1.5 to 1.5
- second_gain: float32 [768], replicated, may hold values from 0.25 to 1.75
- second_bias: float32 [768], replicated, may hold values from -1.5 to 1.5
- up_matrix: bfloat16 [768, 3072], P(None, 'mp'), may hold values from -0.21875 to 0.21875
- up_bias_vector: bfloat16 [3072], P('mp'), may hold values from -1.5 to 1.5
- down_matrix: bfloat16 [3072, 768], P('mp'), may hold values from -0.109375 to 0.109375
- down_bias: float32 [768], replicated, may hold values from -1.5 to 1.5
- out_grad: bfloat16 [32, 1024, 768], P('batch', 'mp'), may hold values from -6 to 6
Outputs:
- block_out: bfloat16 [32, 1024, 768], P('batch', 'mp')
- input_grad: float32 [32, 1024, 768], P('batch', 'mp')
- coeff_grad: float32 [32, 256, 768], P('batch', 'mp')
- first_gain_grad: float32 [768], replicated
- first_bias_grad: float32 [768], replicated
- query_key_value_matrix_grad: float32 [768, 3, 768], P(None, None, 'mp')
- qv_bias_grad: float32 [2, 768], P(None, 'mp')
- memory_weight_grad: float32 [2, 12, 256], P(None, 'mp')
- memory_bias_grad: float32 [2, 12], P(None, 'mp')
- output_matrix_grad: float32 [768, 768], P('mp')
- out_bias_grad: float32 [768], replicated
- second_gain_grad: float32 [768], replicated
- second_bias_grad: float32 [768], replicated
- up_weight_grad: float32 [768, 3072], P(None, 'mp')
- up_bias_grad: float32 [3072], P('mp')
- down_weight_grad: float32 [3072, 768], P('mp')
- down_bias_grad: float32 [768], replicated
The draws below stay inside these ranges and needn't reach their ends.
Inputs may be any that keep to these rules, and one draw needn't show every extreme that they name: memory_flags holds one flag per sequence.
All inputs are finite; a program needn't handle non-finite values. No bound on the sum of `memory_flags` on one device may be relied on, other than what follows from the above.
Results may differ from the reference program's by a relative error of at most 0.013.
The reference program's roundings to bfloat16 on the way count: a program that leaves them out, or rounds other values in their place, can miss the bound.
Values may be sent and summed in bfloat16 or wider, within the bound.
No kernel may reach another device: no remote copies, remote signals or barrier semaphores. Data moves between devices by JAX's collectives and lax.ppermute only.
A program may use at most 320 MiB of HBM per device.

```python
import math
import jax
import jax.numpy as jnp
from jax import lax

D = 768
H = 12
HD = 64
FF = 3072
LEN = 1024
NB = 256
SEQS = 32


def plant(values, own_key, smallest, high):
    longest = values.shape.index(max(values.shape))
    spots = []
    for shift in (0, 1):
        where = [jax.random.randint(jax.random.fold_in(own_key, axis), (), 0, length) for axis, length in enumerate(values.shape)]
        where[longest] = (where[longest] + shift) % values.shape[longest]
        spots.append(tuple(where))
    return values.at[spots[0]].set(smallest).at[spots[1]].set(high)


def steps_of(own_key, extent, cuts, least, top_value):
    factor_of = 1.0
    for dim, parts in cuts:
        draws = jax.random.uniform(jax.random.fold_in(jax.random.fold_in(own_key, 6), dim), (parts,), jnp.float32, least / len(cuts), top_value / len(cuts))
        factor_of = factor_of * jnp.repeat(jnp.exp(draws), extent[dim] // parts).reshape((-1,) + (1,) * (len(extent) - 1 - dim))
    return factor_of


def bell_draw(own_key, shape, width, bound, cuts=(), kind=jnp.bfloat16):
    loudness = steps_of(own_key, shape, cuts, -0.22, 0.18) if cuts else 1.0
    values = jax.random.normal(own_key, shape, jnp.float32) * width * loudness
    return jnp.minimum(jnp.maximum(values, -bound), bound).astype(kind)


def setup_inputs(seed: int = 0) -> dict:
    streams_of = jax.random.split(jax.random.key(seed), 19)
    return {
        "hidden_in": bell_draw(streams_of[0], (SEQS, LEN, D), 1.0, 6.0, ((0, 16), (1, 2))),
        "memory_flags": plant((jax.random.randint(streams_of[1], (SEQS,), 0, 2) < 1).astype(jnp.int32), jax.random.fold_in(streams_of[1], 1), 0, 1),
        "memory_coeffs": bell_draw(streams_of[2], (SEQS, NB, D), 1.0, 6.0, ((0, 16), (1, 2))),
        "first_gain": jnp.clip(1.0 + 0.15 * jax.random.normal(streams_of[3], (D,), jnp.float32), 0.25, 1.75),
        "first_bias": bell_draw(streams_of[4], (D,), 0.3, 1.5, (), jnp.float32),
        "query_key_value_matrix": bell_draw(streams_of[5], (D, 3, D), D ** -0.5, 0.21875, ((2, 2),)),
        "qv_bias": bell_draw(streams_of[6], (2, D), 0.3, 1.5, ((1, 2),)),
        "memory_weight": bell_draw(streams_of[7], (2, H, NB), (4 * NB) ** -0.5, 0.1875, ((1, 2),)),
        "memory_bias": bell_draw(streams_of[8], (2, H), 0.5, 1.5, ((1, 2),)),
        "output_matrix": bell_draw(streams_of[9], (D, D), (D // 32) ** -0.5, 1.25, ((0, 2),)),
        "out_bias": bell_draw(streams_of[10], (D,), 0.3, 1.5, (), jnp.float32),
        "second_gain": jnp.clip(1.0 + 0.15 * jax.random.normal(streams_of[11], (D,), jnp.float32), 0.25, 1.75),
        "second_bias": bell_draw(streams_of[12], (D,), 0.3, 1.5, (), jnp.float32),
        "up_matrix": bell_draw(streams_of[13], (D, FF), D ** -0.5, 0.21875, ((1, 2),)),
        "up_bias_vector": bell_draw(streams_of[14], (FF,), 0.3, 1.5, ((0, 2),)),
        "down_matrix": bell_draw(streams_of[15], (FF, D), FF ** -0.5, 0.109375, ((0, 2),)),
        "down_bias": bell_draw(streams_of[16], (D,), 0.3, 1.5, (), jnp.float32),
        "out_grad": bell_draw(streams_of[17], (SEQS, LEN, D), 1.0, 6.0, ((0, 16), (1, 2))),
    }


@jax.custom_vjp
def low(v):
    return lax.optimization_barrier(v.astype(jnp.bfloat16)).astype(jnp.float32)

@jax.custom_vjp
def low_back(v):
    return v

def low_keep(v):
    return (low(v), None)

def low_pass(kept, grad):
    return (grad,)

def back_keep(v):
    return (v, None)

def back_low(kept, grad):
    return (low(grad),)
low.defvjp(low_keep, low_pass)
low_back.defvjp(back_keep, back_low)

def product(form, left_side, right_side):
    return jnp.einsum(form, left_side, right_side, precision=lax.Precision.HIGHEST)

def layer_norm(values, gain_vec, bias_vec):
    row_mean = lax.optimization_barrier(jnp.mean(values, axis=-1, keepdims=True))
    centred = values - row_mean
    row_var = lax.optimization_barrier(jnp.mean(centred * centred, axis=-1, keepdims=True))
    return centred * lax.rsqrt(row_var + 1e-05) * gain_vec + bias_vec

def basis_weights(memory_scores, weight_pair, bias_pair):
    basis_count = memory_scores.shape[-1]
    mean_logit = product('glhn,hn->glh', memory_scores, weight_pair[0]) + bias_pair[0]
    var_logit = product('glhn,hn->glh', memory_scores, weight_pair[1]) + bias_pair[1]
    centre = jax.nn.sigmoid(mean_logit)
    spread = 0.05 * jax.nn.softplus(var_logit) + (8.0 / basis_count) ** 2
    places = (jnp.arange(basis_count, dtype=jnp.float32) + 0.5) / basis_count
    offset = places - centre[..., None]
    return jnp.exp(-offset * offset / (2.0 * spread[..., None])) * lax.rsqrt(2.0 * math.pi * spread[..., None]) / basis_count

def layer(hidden, coeffs, flag_vec, params):
    first_gain, first_bias, query_key_value_matrix, qv_bias, memory_weight, memory_bias, output_matrix, out_bias, second_gain, second_bias, up_matrix, up_bias_vector, down_matrix, down_bias = params
    groups, length, model_width = hidden.shape
    head_count = model_width // HD
    head_shape = (groups, length, head_count, HD)
    norm_output = low(layer_norm(hidden, first_gain, first_bias))
    projected_rows = product('gld,dcf->glcf', norm_output, query_key_value_matrix)
    queries = low(low_back(projected_rows[:, :, 0] + qv_bias[0])).reshape(head_shape)
    key_rows = low(low_back(projected_rows[:, :, 1])).reshape(head_shape)
    values = low(low_back(projected_rows[:, :, 2] + qv_bias[1])).reshape(head_shape)
    memory = product('gnd,dcf->gncf', coeffs, query_key_value_matrix[:, 1:])
    memory_keys = low(low_back(memory[:, :, 0])).reshape(groups, NB, head_count, HD)
    memory_values = low(low_back(memory[:, :, 1])).reshape(groups, NB, head_count, HD)
    scores = low_back(0.125 * product('glhd,gmhd->ghlm', queries, key_rows))
    causal = jnp.arange(length)[:, None] >= jnp.arange(length)[None, :]
    weights = jax.nn.softmax(jnp.where(causal, scores, -1e+30), axis=-1)
    attended = product('ghlm,gmhd->glhd', low(weights), values)
    memory_scores = low_back(0.125 * product('glhd,gnhd->glhn', queries, memory_keys))
    basis_mass = low(basis_weights(memory_scores, memory_weight, memory_bias))
    recalled = product('glhn,gnhd->glhd', basis_mass, memory_values)
    combined_heads = low(low_back(attended + flag_vec[:, None, None, None] * recalled)).reshape(groups, length, model_width)
    branch = low_back(product('glf,fd->gld', combined_heads, output_matrix) + out_bias)
    middle = hidden + branch
    normed_two = low(layer_norm(middle, second_gain, second_bias))
    input_rows = product('gld,df->glf', normed_two, up_matrix) + up_bias_vector
    gelu_output = low(jax.nn.gelu(low_back(input_rows), approximate=True))
    return middle + product('glf,fd->gld', gelu_output, down_matrix) + down_bias

def reference(hidden_in, memory_flags, memory_coeffs, first_gain, first_bias, query_key_value_matrix, qv_bias, memory_weight, memory_bias, output_matrix, out_bias, second_gain, second_bias, up_matrix, up_bias_vector, down_matrix, down_bias, out_grad):
    params = tuple((param_item.astype(jnp.float32) for param_item in (first_gain, first_bias, query_key_value_matrix, qv_bias, memory_weight, memory_bias, output_matrix, out_bias, second_gain, second_bias, up_matrix, up_bias_vector, down_matrix, down_bias)))
    group_count = SEQS // 2
    hidden_all = hidden_in.astype(jnp.float32).reshape(group_count, 2, LEN, D)
    coeffs_all = memory_coeffs.astype(jnp.float32).reshape(group_count, 2, NB, D)
    flags_all = memory_flags.astype(jnp.float32).reshape(group_count, 2)
    grads_all = out_grad.astype(jnp.float32).reshape(group_count, 2, LEN, D)

    def one_group(totals, pieces):
        group_in, group_coeffs, group_flags, group_grad = pieces

        def forward(hidden, coeffs, layer_params):
            return layer(hidden, coeffs, group_flags, layer_params)
        result, pullback = jax.vjp(forward, group_in, group_coeffs, params)
        grad_in, grad_coeffs, grad_params = pullback(group_grad)
        totals = jax.tree.map(lambda running, fresh_term: running + fresh_term, totals, grad_params)
        return (totals, (result, grad_in, grad_coeffs))
    zero_grads = jax.tree.map(jnp.zeros_like, params)
    totals, (results, grads_in, grads_coeffs) = lax.scan(one_group, zero_grads, (hidden_all, coeffs_all, flags_all, grads_all))
    return (results.reshape(SEQS, LEN, D).astype(jnp.bfloat16), grads_in.reshape(SEQS, LEN, D), grads_coeffs.reshape(SEQS, NB, D), totals[0], totals[1], totals[2], totals[3], totals[4], totals[5], totals[6], totals[7], totals[8], totals[9], totals[10], totals[11], totals[12], totals[13])
```

```python
import functools
import math

import jax
import jax.numpy as jnp
from jax import lax
from jax.experimental import pallas as pl
from jax.experimental.pallas import tpu as pltpu
from jax.sharding import PartitionSpec as P

HD = 64
BLOCK = 256
BF16 = jnp.bfloat16
F32 = jnp.float32
VMEM_BYTES = 56 * 2**20


def dot_nn(left, right):
    return lax.dot_general(left, right, (((1,), (0,)), ((), ())), preferred_element_type=F32)


def dot_nt(left, right):
    return lax.dot_general(left, right, (((1,), (1,)), ((), ())), preferred_element_type=F32)


def dot_tn(left, right):
    return lax.dot_general(left, right, (((0,), (0,)), ((), ())), preferred_element_type=F32)


def dot_tn_exact(left, right):
    return lax.dot_general(
        left,
        right,
        (((0,), (0,)), ((), ())),
        precision=lax.Precision.HIGHEST,
        preferred_element_type=F32,
    )


def three_parts(values):
    high = values.astype(BF16).astype(F32)
    rest = values - high
    middle = rest.astype(BF16).astype(F32)
    return jnp.concatenate([high, middle, rest - middle], axis=0).astype(BF16)


def add_parts(stacked):
    rows = stacked.shape[0] // 3
    return stacked[:rows] + stacked[rows : 2 * rows] + stacked[2 * rows :]


def scaled_rows(values):
    row_mean = jnp.mean(values, axis=-1, keepdims=True)
    centred = values - row_mean
    row_var = jnp.mean(centred * centred, axis=-1, keepdims=True)
    inverse = lax.rsqrt(row_var + 1e-05)
    return centred * inverse, inverse


def norm_back(grad_out, scaled, inverse, gain_vec):
    grad_scaled = grad_out * gain_vec
    first_mean = jnp.mean(grad_scaled, axis=-1, keepdims=True)
    second_mean = jnp.mean(grad_scaled * scaled, axis=-1, keepdims=True)
    return inverse * (grad_scaled - first_mean - scaled * second_mean)


def whole(shape):
    return pl.BlockSpec(shape, lambda *_: (0,) * len(shape))


def call(kernel, grid, in_specs, out_specs, out_shape, flops, name, scratch=()):
    bytes_accessed = sum(math.prod(s.shape) * jnp.dtype(s.dtype).itemsize for s in out_shape)
    return pl.pallas_call(
        kernel,
        grid=grid,
        in_specs=in_specs,
        out_specs=out_specs,
        out_shape=out_shape,
        scratch_shapes=list(scratch),
        compiler_params=pltpu.CompilerParams(
            vmem_limit_bytes=VMEM_BYTES, dimension_semantics=("arbitrary",) * len(grid)
        ),
        cost_estimate=pl.CostEstimate(
            flops=int(flops), bytes_accessed=2 * bytes_accessed, transcendentals=0
        ),
        name=name,
    )


def shape_of(shape, dtype):
    return jax.ShapeDtypeStruct(shape, dtype)


def project_kernel(
    hid, gain, bias, w_own, w_far, qb, coeffs, norm_t, q, k, v, mem_k, mem_v, coeffs_t
):
    scaled, _ = scaled_rows(hid[...].astype(F32))
    normed_f = scaled * gain[...] + bias[...]
    normed = normed_f.astype(BF16)
    norm_t[...] = normed.T
    half = w_own.shape[2]
    for side, weight in enumerate((w_own, w_far)):
        cols = slice(side * half, (side + 1) * half)
        q[:, cols] = (dot_nn(normed, weight[0]) + qb[0:1, cols]).astype(BF16)
        k[:, cols] = dot_nn(normed, weight[1]).astype(BF16)
        v[:, cols] = (dot_nn(normed, weight[2]) + qb[1:2, cols]).astype(BF16)

    @pl.when(pl.program_id(0) == 0)
    def _():
        rows = coeffs[...]
        coeffs_t[...] = rows.T
        for side, weight in enumerate((w_own, w_far)):
            cols = slice(side * half, (side + 1) * half)
            mem_k[:, cols] = dot_nn(rows, weight[1]).astype(BF16)
            mem_v[:, cols] = dot_nn(rows, weight[2]).astype(BF16)


def project(hid, gain, bias, w_own, w_far, qb, coeffs):
    length, width = hid.shape
    basis = coeffs.shape[0]
    rows = pl.BlockSpec((BLOCK, width), lambda i: (i, 0))
    return call(
        project_kernel,
        (length // BLOCK,),
        [
            rows,
            whole(gain.shape),
            whole(bias.shape),
            whole(w_own.shape),
            whole(w_far.shape),
            whole(qb.shape),
            whole(coeffs.shape),
        ],
        [
            pl.BlockSpec((width, BLOCK), lambda i: (0, i)),
            rows,
            rows,
            rows,
            whole((basis, width)),
            whole((basis, width)),
            whole((width, basis)),
        ],
        [
            shape_of((width, length), BF16),
            shape_of((length, width), BF16),
            shape_of((length, width), BF16),
            shape_of((length, width), BF16),
            shape_of((basis, width), BF16),
            shape_of((basis, width), BF16),
            shape_of((width, basis), BF16),
        ],
        2 * length * width * width * 3,
        "project",
    )(hid, gain, bias, w_own, w_far, qb, coeffs)


def head_rows(values_t, head):
    part = values_t[head * HD : (head + 1) * HD]
    zeros = jnp.zeros_like(part)
    return jnp.concatenate([part, zeros] if head == 0 else [zeros, part], axis=0)


def pair_maps(mw, mem_k):
    maps = dot_nn(mw, mem_k)
    row = lax.broadcasted_iota(jnp.int32, maps.shape, 0)
    lane = lax.broadcasted_iota(jnp.int32, maps.shape, 1)
    return jnp.where((row // 2) == (lane // HD), maps, 0.0)


def basis_of(logits, basis_count):
    centre = jax.nn.sigmoid(logits)
    softplus = jnp.maximum(logits, 0.0) + jnp.log(1.0 + jnp.exp(-jnp.abs(logits)))
    spread = 0.05 * softplus + (8.0 / basis_count) ** 2
    rate = -0.5 / spread
    level = lax.rsqrt(2.0 * math.pi * spread) / basis_count
    return centre, rate, level


def places_of(basis_count):
    steps = lax.broadcasted_iota(jnp.int32, (basis_count, BLOCK), 0).astype(F32)
    return (steps + 0.5) / basis_count


def attend_kernel(flag, q, k, v, mem_k, mem_v, mw, mb, att_t, mix_t, mix, stat):
    length = q.shape[0]
    basis = mem_k.shape[0]
    flag_value = flag[0, 0].astype(F32)
    q_t = (q[...].astype(F32) * 0.125).astype(BF16).T
    v_t = v[...].T
    mem_v_t = mem_v[...].T
    maps = pair_maps(mw[0].astype(BF16), mem_k[...])
    logits = add_parts(dot_nn(three_parts(maps), q_t)) + mb[0][:, 0:1]
    centre, rate, level = basis_of(logits, basis)
    places = places_of(basis)
    allowed = lax.broadcasted_iota(jnp.int32, (BLOCK, BLOCK), 0) <= lax.broadcasted_iota(
        jnp.int32, (BLOCK, BLOCK), 1
    )
    stat[4:8, :] = logits[0:4]
    for head in range(2):
        rows = slice(head * HD, (head + 1) * HD)
        q_head = head_rows(q_t, head)
        v_ones = jnp.concatenate([v_t[rows], jnp.ones((16, length), BF16)], axis=0)
        for index in range(length // BLOCK):
            start, stop = index * BLOCK, (index + 1) * BLOCK
            q_block = q_head[:, start:stop]
            near = jnp.where(allowed, dot_nn(k[start:stop, :], q_block), -1e30)
            top = jnp.max(near, axis=0, keepdims=True)
            if index:
                far = dot_nn(k[:start, :], q_block)
                top = jnp.maximum(top, jnp.max(far, axis=0, keepdims=True))
            total = dot_nn(v_ones[:, start:stop], jnp.exp(near - top).astype(BF16))
            if index:
                total += dot_nn(v_ones[:, :start], jnp.exp(far - top).astype(BF16))
            denominator = total[HD : HD + 1]
            attended = total[:HD] / denominator
            att_t[rows, start:stop] = attended
            stat[head : head + 1, start:stop] = top + jnp.log(denominator)
            offset = places - centre[2 * head : 2 * head + 1, start:stop]
            mass = (
                jnp.exp(offset * offset * rate[2 * head + 1 : 2 * head + 2, start:stop])
                * level[2 * head + 1 : 2 * head + 2, start:stop]
            )
            recalled = dot_nn(mem_v_t[rows], mass.astype(BF16))
            mix_t[rows, start:stop] = (attended + flag_value * recalled).astype(BF16)
    mix[...] = mix_t[...].T


def attend(flag, q, k, v, mem_k, mem_v, mw, mb):
    length, width = q.shape
    basis = mem_k.shape[0]
    pairs = width // 128
    rows = pl.BlockSpec((length, 128), lambda p: (0, p))
    mem_rows = pl.BlockSpec((basis, 128), lambda p: (0, p))
    cols = pl.BlockSpec((128, length), lambda p: (p, 0))
    return call(
        attend_kernel,
        (pairs,),
        [
            pl.BlockSpec(memory_space=pltpu.SMEM),
            rows,
            rows,
            rows,
            mem_rows,
            mem_rows,
            pl.BlockSpec((1, 8, basis), lambda p: (p, 0, 0)),
            pl.BlockSpec((1, 8, 128), lambda p: (p, 0, 0)),
        ],
        [cols, cols, rows, pl.BlockSpec((8, length), lambda p: (p, 0))],
        [
            shape_of((width, length), F32),
            shape_of((width, length), BF16),
            shape_of((length, width), BF16),
            shape_of((pairs * 8, length), F32),
        ],
        12 * length * length * width,
        "attend",
    )(flag, q, k, v, mem_k, mem_v, mw, mb)


def attend_back_kernel(
    flag, q, k, v, mem_k, mem_v, mw, grad, att_t, stat, dq, dk, dv, dmem_k, dmem_v, dmw, sums
):
    length = q.shape[0]
    basis = mem_k.shape[0]
    flag_value = flag[0, 0].astype(F32)
    q_t = (q[...].astype(F32) * 0.125).astype(BF16).T
    k_t = k[...].T
    grad_t = grad[...].T
    lane = lax.broadcasted_iota(jnp.int32, (length, 128), 1)
    maps = pair_maps(mw[0].astype(BF16), mem_k[...])
    logits = stat[4:8, :]
    logits = jnp.concatenate([logits, jnp.zeros_like(logits)], axis=0)
    centre, rate, level = basis_of(logits, basis)
    places = places_of(basis)
    allowed = lax.broadcasted_iota(jnp.int32, (BLOCK, BLOCK), 0) <= lax.broadcasted_iota(
        jnp.int32, (BLOCK, BLOCK), 1
    )
    q_lanes = []
    dk_lanes = []
    dv_lanes = []
    dmv_lanes = []
    mass_grads = []
    for head in range(2):
        rows = slice(head * HD, (head + 1) * HD)
        mine = (lane // HD) == head
        q_head_t = head_rows(q_t, head)
        grad_head_t = head_rows(grad_t, head)
        q_head = jnp.where(mine, q[...].astype(F32), 0.0).astype(BF16)
        grad_head = jnp.where(mine, grad[...].astype(F32), 0.0).astype(BF16)
        log_total = stat[head : head + 1, :]
        inner = jnp.sum(grad_t[rows].astype(F32) * att_t[rows], axis=0, keepdims=True)
        query_parts = [None] * (length // BLOCK)
        dk_parts = []
        dv_parts = []
        for index in range(length // BLOCK):
            start, stop = index * BLOCK, (index + 1) * BLOCK
            scores = dot_nn(k[start:stop, :], q_head_t[:, start:])
            weights = jnp.exp(scores - log_total[:, start:])
            diagonal = jnp.where(allowed, weights[:, :BLOCK], 0.0)
            if stop < length:
                weights = jnp.concatenate([diagonal, weights[:, BLOCK:]], axis=1)
            else:
                weights = diagonal
            weights_grad = dot_nn(v[start:stop, :], grad_head_t[:, start:])
            scores_grad = (weights * (weights_grad - inner[:, start:])).astype(BF16)
            dv_parts.append(dot_nn(weights.astype(BF16), grad_head[start:]))
            dk_parts.append(dot_nn(scores_grad, q_head[start:]))
            query = dot_nn(k_t[rows, start:stop], scores_grad)
            for later in range(index, length // BLOCK):
                piece = query[:, (later - index) * BLOCK : (later - index + 1) * BLOCK]
                kept = query_parts[later]
                query_parts[later] = piece if kept is None else kept + piece
        q_lanes.append(jnp.concatenate(query_parts, axis=1))
        dk_lanes.append(jnp.concatenate(dk_parts, axis=0))
        dv_lanes.append(jnp.concatenate(dv_parts, axis=0))
        sum_parts = []
        mem_total = None
        for index in range(length // BLOCK):
            start, stop = index * BLOCK, (index + 1) * BLOCK
            rate_row = rate[2 * head + 1 : 2 * head + 2, start:stop]
            offset = places - centre[2 * head : 2 * head + 1, start:stop]
            mass = (
                jnp.exp(offset * offset * rate_row) * level[2 * head + 1 : 2 * head + 2, start:stop]
            )
            basis_grad = dot_nn(mem_v[...], grad_head_t[:, start:stop])
            zeroth = basis_grad * mass
            first = zeroth * offset
            second = first * offset
            sum_parts.append(
                jnp.concatenate(
                    [
                        jnp.sum(first, axis=0, keepdims=True) * (-2.0 * rate_row),
                        jnp.sum(second, axis=0, keepdims=True) * (2.0 * rate_row * rate_row)
                        + jnp.sum(zeroth, axis=0, keepdims=True) * rate_row,
                    ],
                    axis=0,
                )
            )
            piece = dot_nn(mass.astype(BF16), grad_head[start:stop])
            mem_total = piece if mem_total is None else mem_total + piece
        dmv_lanes.append(mem_total)
        mass_grads.append(jnp.concatenate(sum_parts, axis=1))
    parity = lax.broadcasted_iota(jnp.int32, logits.shape, 0) % 2
    basis_grads = jnp.concatenate(
        mass_grads + [jnp.zeros((4, length), F32)], axis=0
    )
    slope = jnp.where(parity == 0, centre * (1.0 - centre), 0.05 * centre)
    logits_grad = basis_grads * slope * flag_value
    query_total = jnp.concatenate(q_lanes, axis=0) + dot_tn_exact(maps, logits_grad)
    dq[...] = (0.125 * query_total).T.astype(BF16)
    dk[...] = (0.125 * (dk_lanes[0] + dk_lanes[1])).astype(BF16)
    dv[...] = (dv_lanes[0] + dv_lanes[1]).astype(BF16)
    dmem_v[...] = (flag_value * (dmv_lanes[0] + dmv_lanes[1])).astype(BF16)
    row = lax.broadcasted_iota(jnp.int32, maps.shape, 0)
    lanes = lax.broadcasted_iota(jnp.int32, maps.shape, 1)
    outer = jnp.where(
        (row // 2) == (lanes // HD), add_parts(dot_nn(three_parts(logits_grad), q[...])) * 0.125, 0.0
    )
    dmem_k[...] = dot_tn_exact(mw[0], outer).astype(BF16)
    dmw[0] = add_parts(dot_nt(three_parts(outer), mem_k[...]))
    ones = jnp.ones((16, length), BF16)
    sums[0, 0:8] = jnp.broadcast_to(jnp.sum(logits_grad, axis=1, keepdims=True), (8, 128))
    sums[0, 8:9] = dot_nn(ones, dq[...])[0:1]
    sums[0, 9:10] = dot_nn(ones, dv[...])[0:1]
    sums[0, 10:16] = jnp.zeros((6, 128), F32)


def attend_back(side, flag, q, k, v, mem_k, mem_v, mw, grad, att_t, stat):
    length, width = q.shape
    basis = mem_k.shape[0]
    pairs = width // 256
    base = side * pairs
    rows = pl.BlockSpec((length, 128), lambda p: (0, base + p))
    mem_rows = pl.BlockSpec((basis, 128), lambda p: (0, base + p))
    out_rows = pl.BlockSpec((length, 128), lambda p: (0, p))
    out_mem_rows = pl.BlockSpec((basis, 128), lambda p: (0, p))
    return call(
        attend_back_kernel,
        (pairs,),
        [
            pl.BlockSpec(memory_space=pltpu.SMEM),
            rows,
            rows,
            rows,
            mem_rows,
            mem_rows,
            pl.BlockSpec((1, 8, basis), lambda p: (base + p, 0, 0)),
            rows,
            pl.BlockSpec((128, length), lambda p: (base + p, 0)),
            pl.BlockSpec((8, length), lambda p: (base + p, 0)),
        ],
        [
            out_rows,
            out_rows,
            out_rows,
            out_mem_rows,
            out_mem_rows,
            pl.BlockSpec((1, 8, basis), lambda p: (p, 0, 0)),
            pl.BlockSpec((1, 16, 128), lambda p: (p, 0, 0)),
        ],
        [
            shape_of((length, width // 2), BF16),
            shape_of((length, width // 2), BF16),
            shape_of((length, width // 2), BF16),
            shape_of((basis, width // 2), BF16),
            shape_of((basis, width // 2), BF16),
            shape_of((pairs, 8, basis), F32),
            shape_of((pairs, 16, 128), F32),
        ],
        14 * length * length * width,
        "attend_back",
    )(flag, q, k, v, mem_k, mem_v, mw, grad, att_t, stat)


def residual_kernel(mix, hid, w_own, w_far, out_bias, gain, bias, middle, normed, normed_t):
    half = w_own.shape[0]
    branch = dot_nn(mix[:, :half], w_own[...]) + dot_nn(mix[:, half:], w_far[...])
    rows = hid[...].astype(F32) + (branch + out_bias[...])
    middle[...] = rows
    scaled, _ = scaled_rows(rows)
    result = (scaled * gain[...] + bias[...]).astype(BF16)
    normed[...] = result
    normed_t[...] = result.T


def residual(mix, hid, w_own, w_far, out_bias, gain, bias):
    length, width = hid.shape
    rows = pl.BlockSpec((BLOCK, width), lambda i: (i, 0))
    return call(
        residual_kernel,
        (length // BLOCK,),
        [
            rows,
            rows,
            whole(w_own.shape),
            whole(w_far.shape),
            whole(out_bias.shape),
            whole(gain.shape),
            whole(bias.shape),
        ],
        [rows, rows, pl.BlockSpec((width, BLOCK), lambda i: (0, i))],
        [
            shape_of((length, width), F32),
            shape_of((length, width), BF16),
            shape_of((width, length), BF16),
        ],
        2 * length * width * width,
        "residual",
    )(mix, hid, w_own, w_far, out_bias, gain, bias)


def branch_back_kernel(
    normed_grad, out_grad, middle, mix_t, w_own, w_far, gain, mid_grad, mix_grad, dw_own, dw_far, sums, total
):
    index = pl.program_id(0)
    scaled, inverse = scaled_rows(middle[...])
    grad_rows = normed_grad[...]
    out_rows = out_grad[...].astype(F32)
    result = out_rows + norm_back(grad_rows, scaled, inverse, gain[...])
    mid_grad[...] = result
    branch = result.astype(BF16)
    half = w_own.shape[0]
    mix_grad[:, :half] = dot_nt(branch, w_own[...]).astype(BF16)
    mix_grad[:, half:] = dot_nt(branch, w_far[...]).astype(BF16)
    fresh = dot_nn(mix_t[...], branch)
    added = jnp.concatenate(
        [
            jnp.sum(branch.astype(F32), axis=0, keepdims=True),
            jnp.sum(grad_rows * scaled, axis=0, keepdims=True),
            jnp.sum(grad_rows, axis=0, keepdims=True),
            jnp.sum(out_rows, axis=0, keepdims=True),
            jnp.zeros((4, grad_rows.shape[1]), F32),
        ],
        axis=0,
    )

    @pl.when(index == 0)
    def _():
        total[...] = fresh
        sums[...] = added

    @pl.when(index > 0)
    def _():
        total[...] += fresh
        sums[...] += added

    @pl.when(index == pl.num_programs(0) - 1)
    def _():
        dw_own[...] = total[:half].astype(BF16)
        dw_far[...] = total[half:].astype(BF16)


def branch_back(normed_grad, out_grad, middle, mix_t, w_own, w_far, gain):
    length, width = middle.shape
    rows = pl.BlockSpec((BLOCK, width), lambda i: (i, 0))
    return call(
        branch_back_kernel,
        (length // BLOCK,),
        [
            rows,
            rows,
            rows,
            pl.BlockSpec((width, BLOCK), lambda i: (0, i)),
            whole(w_own.shape),
            whole(w_far.shape),
            whole(gain.shape),
        ],
        [rows, rows, whole(w_own.shape), whole(w_far.shape), whole((8, width))],
        [
            shape_of((length, width), F32),
            shape_of((length, width), BF16),
            shape_of(w_own.shape, BF16),
            shape_of(w_far.shape, BF16),
            shape_of((8, width), F32),
        ],
        4 * length * width * width,
        "branch_back",
        scratch=[pltpu.VMEM((width, width), F32)],
    )(normed_grad, out_grad, middle, mix_t, w_own, w_far, gain)


def feed_step(normed, normed_t, out_grad, up, up_bias, down, d_up, d_up_bias, d_down):
    weight_up = up[...]
    weight_down = down[...]
    before = dot_nn(normed[...], weight_up) + up_bias[...]
    out_rows = out_grad[...]
    hidden_grad = dot_nt(out_rows, weight_down)
    root = math.sqrt(2.0 / math.pi)
    square = before * before
    angle = jnp.tanh(before * (root + (root * 0.044715) * square))
    half_sum = 0.5 + 0.5 * angle
    activated = (before * half_sum).astype(BF16)
    slope = half_sum + before * (0.5 - 0.5 * angle * angle) * (
        root + (3.0 * 0.044715 * root) * square
    )
    before_grad = (hidden_grad * slope).astype(BF16)
    d_down[...] = dot_tn(activated, out_rows).astype(BF16)
    d_up[...] = dot_nn(normed_t[...], before_grad).astype(BF16)
    d_up_bias[...] = dot_nn(jnp.ones((8, before.shape[0]), BF16), before_grad)
    return dot_nn(activated, weight_down), dot_nt(before_grad, weight_up)


def feed_kernel(carried, steps, *refs):
    normed, normed_t, out_grad, up_far, up_own, ub_far, ub_own, down_far, down_own = refs[:9]
    refs = refs[9:]
    if carried:
        out_in, grad_in = refs[:2]
        refs = refs[2:]
    out_sum, grad_sum, du_far, du_own, dub_far, dub_own, dd_far, dd_own = refs
    index = pl.program_id(0)

    @pl.when(index == 0)
    def _():
        forward, backward = feed_step(
            normed, normed_t, out_grad, up_far, ub_far, down_far, du_far, dub_far, dd_far
        )
        if carried:
            forward += out_in[...]
            backward += grad_in[...]
        out_sum[...] = forward
        grad_sum[...] = backward

    @pl.when((index > 0) & (index < steps))
    def _():
        forward, backward = feed_step(
            normed, normed_t, out_grad, up_far, ub_far, down_far, du_far, dub_far, dd_far
        )
        out_sum[...] += forward
        grad_sum[...] += backward

    @pl.when(index >= steps)
    def _():
        forward, backward = feed_step(
            normed, normed_t, out_grad, up_own, ub_own, down_own, du_own, dub_own, dd_own
        )
        out_sum[...] += forward
        grad_sum[...] += backward


def feed(part, parts, normed, normed_t, out_grad, up_far, up_own, ub_far, ub_own, down_far, down_own, carry):
    length, width = normed.shape
    hidden = up_own.shape[1] // parts
    steps = hidden // BLOCK
    base = part * steps

    def far_block(i):
        return jnp.minimum(i, steps - 1)

    def own_block(i):
        return jnp.maximum(i - steps, 0)

    def up_spec(block, first):
        return pl.BlockSpec((width, BLOCK), lambda i: (0, first + block(i)))

    def bias_spec(block, first, rows):
        return pl.BlockSpec((rows, BLOCK), lambda i: (0, first + block(i)))

    def down_spec(block, first):
        return pl.BlockSpec((BLOCK, width), lambda i: (first + block(i), 0))

    keep = whole((length, width))
    carried = carry is not None
    specs = [
        keep,
        whole((width, length)),
        keep,
        up_spec(far_block, base),
        up_spec(own_block, base),
        bias_spec(far_block, base, 1),
        bias_spec(own_block, base, 1),
        down_spec(far_block, base),
        down_spec(own_block, base),
    ] + ([keep, keep] if carried else [])
    operands = (normed, normed_t, out_grad, up_far, up_own, ub_far, ub_own, down_far, down_own)
    return call(
        functools.partial(feed_kernel, carried, steps),
        (2 * steps,),
        specs,
        [
            keep,
            keep,
            up_spec(far_block, 0),
            up_spec(own_block, 0),
            bias_spec(far_block, 0, 8),
            bias_spec(own_block, 0, 8),
            down_spec(far_block, 0),
            down_spec(own_block, 0),
        ],
        [
            shape_of((length, width), F32),
            shape_of((length, width), F32),
            shape_of((width, hidden), BF16),
            shape_of((width, hidden), BF16),
            shape_of((8, hidden), F32),
            shape_of((8, hidden), F32),
            shape_of((hidden, width), BF16),
            shape_of((hidden, width), BF16),
        ],
        24 * length * width * hidden,
        "feed",
    )(*operands, *(carry or ()))


def weights_back_kernel(norm_t, coeffs_t, dq, dk, dv, dmem_k, dmem_v, out):
    out[0] = dot_nn(norm_t[...], dq[...]).astype(BF16)
    out[1] = (dot_nn(norm_t[...], dk[...]) + dot_nn(coeffs_t[...], dmem_k[...])).astype(BF16)
    out[2] = (dot_nn(norm_t[...], dv[...]) + dot_nn(coeffs_t[...], dmem_v[...])).astype(BF16)


def weights_back(norm_t, coeffs_t, dq, dk, dv, dmem_k, dmem_v):
    width, length = norm_t.shape
    half = dq.shape[1]
    operands = (norm_t, coeffs_t, dq, dk, dv, dmem_k, dmem_v)
    return call(
        weights_back_kernel,
        (1,),
        [whole(o.shape) for o in operands],
        [whole((3, width, half))],
        [shape_of((3, width, half), BF16)],
        6 * length * width * half,
        "weights_back",
    )(*operands)[0]


def input_back_kernel(
    hid, mid_grad, gain, w_own, w_far, dq_own, dk_own, dv_own, dq_far, dk_far, dv_far,
    dmk_own, dmv_own, dmk_far, dmv_far, in_grad, coeff_grad, sums,
):
    index = pl.program_id(0)
    grad_rows = (
        dot_nt(dq_own[...], w_own[0])
        + dot_nt(dk_own[...], w_own[1])
        + dot_nt(dv_own[...], w_own[2])
        + dot_nt(dq_far[...], w_far[0])
        + dot_nt(dk_far[...], w_far[1])
        + dot_nt(dv_far[...], w_far[2])
    )
    scaled, inverse = scaled_rows(hid[...].astype(F32))
    in_grad[...] = mid_grad[...] + norm_back(grad_rows, scaled, inverse, gain[...])
    added = jnp.concatenate(
        [
            jnp.sum(grad_rows * scaled, axis=0, keepdims=True),
            jnp.sum(grad_rows, axis=0, keepdims=True),
            jnp.zeros((6, grad_rows.shape[1]), F32),
        ],
        axis=0,
    )

    @pl.when(index == 0)
    def _():
        sums[...] = added
        coeff_grad[...] = (
            dot_nt(dmk_own[...], w_own[1])
            + dot_nt(dmv_own[...], w_own[2])
            + dot_nt(dmk_far[...], w_far[1])
            + dot_nt(dmv_far[...], w_far[2])
        )

    @pl.when(index > 0)
    def _():
        sums[...] += added


def input_back(hid, mid_grad, gain, w_own, w_far, own, far):
    length, width = hid.shape
    half = w_own.shape[2]
    basis = own[3].shape[0]
    rows = pl.BlockSpec((BLOCK, width), lambda i: (i, 0))
    half_rows = pl.BlockSpec((BLOCK, half), lambda i: (i, 0))
    return call(
        input_back_kernel,
        (length // BLOCK,),
        [rows, rows, whole(gain.shape), whole(w_own.shape), whole(w_far.shape)]
        + [half_rows] * 6
        + [whole((basis, half))] * 4,
        [rows, whole((basis, width)), whole((8, width))],
        [
            shape_of((length, width), F32),
            shape_of((basis, width), F32),
            shape_of((8, width), F32),
        ],
        6 * length * width * width,
        "input_back",
    )(hid, mid_grad, gain, w_own, w_far, *own[:3], *far[:3], *own[3:5], *far[3:5])


def to_peer(values):
    return jax.tree.map(lambda v: lax.ppermute(v, "mp", [(0, 1), (1, 0)]), values)


def across(values, offset, count):
    return lax.ppermute(values, "batch", [(i, i ^ offset) for i in range(count)])


def added(left, right):
    return (left.astype(F32) + right.astype(F32)).astype(BF16)


def halved(values, bit):
    parts = values.reshape(2, values.shape[0] // 2, values.shape[1])
    return (
        lax.dynamic_index_in_dim(parts, bit, 0, keepdims=False),
        lax.dynamic_index_in_dim(parts, 1 - bit, 0, keepdims=False),
    )


def joined(mine, theirs, bit):
    low = jnp.where(bit == 0, mine, theirs)
    high = jnp.where(bit == 0, theirs, mine)
    return jnp.concatenate([low, high], axis=0)


def sum_pair(first, second, position, count):
    bits = (position & 1, (position >> 1) & 1)
    kept = [first, second]
    for step in range(2):
        halves = [halved(kept[which], bits[step ^ which]) for which in range(2)]
        kept = [
            added(halves[which][0], across(halves[which][1], 1 << (step ^ which), count))
            for which in range(2)
        ]
    group = min(4, count // 4)
    place = (position >> 2) % group
    results = []
    for values in kept:
        parts = values.reshape(group, values.shape[0] // group, values.shape[1])
        total = lax.dynamic_index_in_dim(parts, place, 0, keepdims=False).astype(F32)
        for offset in range(1, group):
            share = lax.dynamic_index_in_dim(parts, place ^ offset, 0, keepdims=False)
            total += across(share, offset << 2, count).astype(F32)
        total = total.astype(BF16)
        offset = 4 * group
        while offset < count:
            total = added(total, across(total, offset, count))
            offset *= 2
        pieces = [total] + [across(total, offset << 2, count) for offset in range(1, group)]
        level = 1
        while level < group:
            bit = (place // level) & 1
            pieces = [
                jnp.where(bit == 0, pieces[index], pieces[index ^ level]) for index in range(group)
            ]
            level *= 2
        results.append(jnp.concatenate(pieces, axis=0))
    for step in (1, 0):
        results = [
            joined(
                results[which],
                across(results[which], 1 << (step ^ which), count),
                bits[step ^ which],
            )
            for which in range(2)
        ]
    return results


def sum_small(values, count):
    near = [across(values, offset, count) for offset in (1, 2, 3)]
    values = (values + near[0]) + (near[1] + near[2])
    offset = 4
    while offset < count:
        if offset * 2 < count:
            more = [across(values, offset * times, count) for times in (1, 2, 3)]
            values = (values + more[0]) + (more[1] + more[2])
            offset *= 4
        else:
            values = values + across(values, offset, count)
            offset *= 2
    return values


def pair_rows(values):
    heads = values.shape[1]
    rows = jnp.transpose(values, (1, 0, 2)).reshape(heads // 2, 4, values.shape[2])
    return jnp.concatenate([rows, jnp.zeros_like(rows)], axis=1)


def per_device(
    count,
    hidden_in,
    memory_flags,
    memory_coeffs,
    first_gain,
    first_bias,
    query_key_value_matrix,
    qv_bias,
    memory_weight,
    memory_bias,
    output_matrix,
    out_bias,
    second_gain,
    second_bias,
    up_matrix,
    up_bias_vector,
    down_matrix,
    down_bias,
    out_grad,
):
    me = lax.axis_index("mp")
    position = lax.axis_index("batch")
    _, tokens, width = hidden_in.shape
    first = me == 0

    def sequence(values):
        mine = lax.dynamic_index_in_dim(values, me, 0, keepdims=False)
        theirs = to_peer(lax.dynamic_index_in_dim(values, 1 - me, 0, keepdims=False))
        low = jnp.where(first, mine, theirs)
        high = jnp.where(first, theirs, mine)
        return jnp.concatenate([low, high], axis=0)

    hid = sequence(hidden_in)
    w_own = jnp.transpose(query_key_value_matrix, (1, 0, 2))
    w_far = to_peer(w_own)
    coeffs = sequence(memory_coeffs)
    small_own = (qv_bias, memory_weight, memory_bias, up_bias_vector)
    small_far = to_peer(small_own)
    wo_far = to_peer(output_matrix)
    out_rows = sequence(out_grad)
    up_far = to_peer(up_matrix)
    down_far = to_peer(down_matrix)
    flag = lax.dynamic_index_in_dim(memory_flags, me, 0, keepdims=True).reshape(1, 1)

    query_bias = jnp.concatenate([small_own[0], small_far[0]], axis=1).astype(F32)
    mem_maps = jnp.concatenate([pair_rows(small_own[1]), pair_rows(small_far[1])], axis=0)
    mem_maps = mem_maps.astype(F32)
    mem_biases = jnp.concatenate(
        [pair_rows(small_own[2][:, :, None]), pair_rows(small_far[2][:, :, None])], axis=0
    ).astype(F32)
    mem_biases = jnp.broadcast_to(mem_biases, mem_biases.shape[:2] + (128,))
    ub_own = small_own[3].astype(F32)[None]
    ub_far = small_far[3].astype(F32)[None]
    gain_one, bias_one = first_gain[None], first_bias[None]
    gain_two, bias_two = second_gain[None], second_bias[None]

    norm_t, q, k, v, mem_k, mem_v, coeffs_t = project(
        hid, gain_one, bias_one, w_own, w_far, query_bias, coeffs
    )
    att_t, mix_t, mix, stat = attend(flag, q, k, v, mem_k, mem_v, mem_maps, mem_biases)
    middle, normed, normed_t = residual(
        mix, hid, output_matrix, wo_far, out_bias[None], gain_two, bias_two
    )
    parts = 2
    carry = None
    feed_sums = []
    up_bias_far, up_bias_own = [], []
    for part in range(parts):
        out_sum, grad_sum, du_far, du_own, dub_far, dub_own, dd_far, dd_own = feed(
            part,
            parts,
            normed,
            normed_t,
            out_rows,
            up_far,
            up_matrix,
            ub_far,
            ub_own,
            down_far,
            down_matrix,
            carry,
        )
        carry = (out_sum, grad_sum)
        du_peer, dd_peer = to_peer((du_far, dd_far))
        feed_sums.append(
            sum_pair(added(du_own, du_peer), added(dd_own, dd_peer), position, count)
        )
        up_bias_far.append(dub_far[0])
        up_bias_own.append(dub_own[0])
    block_rows = (middle + carry[0] + down_bias).astype(BF16)
    mid_grad, mix_grad, dwo_own, dwo_far, mid_sums = branch_back(
        carry[1], out_rows, middle, mix_t, output_matrix, wo_far, gain_two
    )
    far = attend_back(1, flag, q, k, v, mem_k, mem_v, mem_maps, mix_grad, att_t, stat)
    dqkv_far = weights_back(norm_t, coeffs_t, *far[:5])
    own = attend_back(0, flag, q, k, v, mem_k, mem_v, mem_maps, mix_grad, att_t, stat)
    dqkv_own = weights_back(norm_t, coeffs_t, *own[:5])
    dwo_peer, dqkv_peer = to_peer((dwo_far, dqkv_far))
    half = width // 2
    bucket_far = None
    dqkv = added(dqkv_own, dqkv_peer).reshape(3 * width, half)
    dwo = added(dwo_own, dwo_peer)
    dwo = jnp.concatenate([dwo[:, :half], dwo[:, half:]], axis=0)
    bucket = jnp.concatenate([dqkv, dwo], axis=0)
    split = bucket.shape[0] // 2
    low, high = sum_pair(bucket[:split], bucket[split:], position, count)
    bucket = jnp.concatenate([low, high], axis=0).astype(F32)
    query_key_value_grad = jnp.transpose(bucket[: 3 * width].reshape(3, width, half), (1, 0, 2))
    dwo = bucket[3 * width :]
    output_matrix_grad = jnp.concatenate([dwo[:half], dwo[half:]], axis=1)
    in_rows, coeff_rows, first_sums = input_back(
        hid, mid_grad, gain_one, w_own, w_far, own, far
    )

    def own_tokens(values):
        parts_of = values.reshape(2, values.shape[0] // 2, width)
        mine = lax.dynamic_index_in_dim(parts_of, me, 0, keepdims=False)
        theirs = lax.dynamic_index_in_dim(parts_of, 1 - me, 0, keepdims=False)
        theirs = to_peer(theirs.astype(BF16)).astype(values.dtype)
        low = jnp.where(first, mine, theirs)
        high = jnp.where(first, theirs, mine)
        return jnp.stack([low, high], axis=0)

    block_out = own_tokens(block_rows)
    input_grad = own_tokens(in_rows)
    coeff_grad = own_tokens(coeff_rows)

    def flat_small(group, up_bias):
        maps, sums = group[5], group[6]
        return [
            maps[:, :4].reshape(-1),
            sums[:, :4, 0].reshape(-1),
            sums[:, 8].reshape(-1),
            sums[:, 9].reshape(-1),
            jnp.concatenate(up_bias).reshape(-1),
        ]

    shared = [mid_sums[:4].reshape(-1), first_sums[:2].reshape(-1)]
    own_small = flat_small(own, up_bias_own)
    sizes = [v.shape[0] for v in own_small + shared]
    own_flat = jnp.concatenate(own_small + shared)
    far_flat = jnp.concatenate(flat_small(far, up_bias_far) + shared)
    padding = -own_flat.shape[0] % 1024
    own_flat = jnp.pad(own_flat, (0, padding)).reshape(-1, 128)
    far_flat = jnp.pad(far_flat, (0, padding)).reshape(-1, 128)
    small = sum_small(own_flat + to_peer(far_flat), count).reshape(-1)
    pieces = []
    start = 0
    for size in sizes:
        pieces.append(small[start : start + size])
        start += size
    heads = memory_weight.shape[1]
    basis = memory_weight.shape[2]
    memory_weight_grad = jnp.transpose(pieces[0].reshape(heads, 2, basis), (1, 0, 2))
    memory_bias_grad = jnp.transpose(pieces[1].reshape(heads, 2), (1, 0))
    qv_bias_grad = jnp.stack([pieces[2], pieces[3]], axis=0)
    up_bias_grad = pieces[4]
    mid_rows = pieces[5].reshape(4, width)
    first_rows = pieces[6].reshape(2, width)
    up_weight_grad = jnp.concatenate([s[0] for s in feed_sums], axis=1).astype(F32)
    down_weight_grad = jnp.concatenate([s[1] for s in feed_sums], axis=0).astype(F32)
    return (
        block_out,
        input_grad,
        coeff_grad,
        first_rows[0],
        first_rows[1],
        query_key_value_grad,
        qv_bias_grad,
        memory_weight_grad,
        memory_bias_grad,
        output_matrix_grad,
        mid_rows[0],
        mid_rows[1],
        mid_rows[2],
        up_weight_grad,
        up_bias_grad,
        down_weight_grad,
        mid_rows[3],
    )


def solution(mesh):
    tokens = P("batch", "mp", None)
    return jax.shard_map(
        functools.partial(per_device, mesh.shape["batch"]),
        mesh=mesh,
        in_specs=(
            tokens,
            P("batch"),
            tokens,
            P(),
            P(),
            P(None, None, "mp"),
            P(None, "mp"),
            P(None, "mp", None),
            P(None, "mp"),
            P("mp", None),
            P(),
            P(),
            P(),
            P(None, "mp"),
            P("mp"),
            P("mp", None),
            P(),
            tokens,
        ),
        out_specs=(
            tokens,
            tokens,
            tokens,
            P(),
            P(),
            P(None, None, "mp"),
            P(None, "mp"),
            P(None, "mp", None),
            P(None, "mp"),
            P("mp", None),
            P(),
            P(),
            P(),
            P(None, "mp"),
            P("mp"),
            P("mp", None),
            P(),
        ),
        check_vma=False,
    )
```

```python
import functools
import math

import jax
import jax.numpy as jnp
from jax import lax
from jax.experimental import pallas as pl
from jax.experimental.pallas import tpu as pltpu
from jax.sharding import PartitionSpec as P

HD = 64
BLOCK = 256
ROWS = 512
FEED_BLOCK = 512
BF16 = jnp.bfloat16
F32 = jnp.float32
VMEM_BYTES = 56 * 2**20


def dot_nn(left, right):
    return lax.dot_general(left, right, (((1,), (0,)), ((), ())), preferred_element_type=F32)


def dot_nt(left, right):
    return lax.dot_general(left, right, (((1,), (1,)), ((), ())), preferred_element_type=F32)


def dot_tn(left, right):
    return lax.dot_general(left, right, (((0,), (0,)), ((), ())), preferred_element_type=F32)


def dot_tn_exact(left, right):
    return lax.dot_general(
        left,
        right,
        (((0,), (0,)), ((), ())),
        precision=lax.Precision.HIGHEST,
        preferred_element_type=F32,
    )


def three_parts(values):
    high = values.astype(BF16).astype(F32)
    rest = values - high
    middle = rest.astype(BF16).astype(F32)
    return jnp.concatenate([high, middle, rest - middle], axis=0).astype(BF16)


def add_parts(stacked):
    rows = stacked.shape[0] // 3
    return stacked[:rows] + stacked[rows : 2 * rows] + stacked[2 * rows :]


def scaled_rows(values):
    row_mean = jnp.mean(values, axis=-1, keepdims=True)
    centred = values - row_mean
    row_var = jnp.mean(centred * centred, axis=-1, keepdims=True)
    inverse = lax.rsqrt(row_var + 1e-05)
    return centred * inverse, inverse


def norm_back(grad_out, scaled, inverse, gain_vec):
    grad_scaled = grad_out * gain_vec
    first_mean = jnp.mean(grad_scaled, axis=-1, keepdims=True)
    second_mean = jnp.mean(grad_scaled * scaled, axis=-1, keepdims=True)
    return inverse * (grad_scaled - first_mean - scaled * second_mean)


def whole(shape):
    return pl.BlockSpec(shape, lambda *_: (0,) * len(shape))


class Order:
    def __init__(self):
        self.token = None

    def call(
        self, kernel, grid, in_specs, out_specs, out_shape, flops, name, operands, scratch=(), scalars=(),
        aliases=None,
    ):
        count = len(operands)
        prefetched = len(scalars)
        token = () if self.token is None else (self.token,)

        def body(*refs):
            kernel(*refs[: prefetched + count], *refs[prefetched + count + len(token) :])

        bytes_accessed = sum(math.prod(s.shape) * jnp.dtype(s.dtype).itemsize for s in out_shape)
        results = pl.pallas_call(
            body,
            grid_spec=pltpu.PrefetchScalarGridSpec(
                num_scalar_prefetch=prefetched,
                grid=grid,
                in_specs=list(in_specs) + [pl.BlockSpec(memory_space=pl.ANY)] * len(token),
                out_specs=list(out_specs),
                scratch_shapes=list(scratch),
            ),
            out_shape=out_shape,
            input_output_aliases=aliases or {},
            compiler_params=pltpu.CompilerParams(
                vmem_limit_bytes=VMEM_BYTES, dimension_semantics=("arbitrary",) * len(grid)
            ),
            cost_estimate=pl.CostEstimate(
                flops=int(flops), bytes_accessed=2 * bytes_accessed, transcendentals=0
            ),
            name=name,
        )(*scalars, *operands, *token)
        self.token = results[-1]
        return results


def shape_of(shape, dtype):
    return jax.ShapeDtypeStruct(shape, dtype)


def project_kernel(
    scalars, mine, theirs, vectors, w_own, w_far, qb, coeffs_mine, coeffs_theirs,
    hid, norm_t, q, k, v, mem_k, mem_v, coeffs_t,
):
    me = scalars[0]
    index = pl.program_id(0)

    @pl.when(index == me)
    def _():
        hid[...] = mine[0]

    @pl.when(index != me)
    def _():
        hid[...] = theirs[...]

    scaled, _ = scaled_rows(hid[...].astype(F32))
    normed = (scaled * vectors[0:1] + vectors[1:2]).astype(BF16)
    norm_t[...] = normed.T

    def weight(part):
        return jnp.concatenate([w_own[part], w_far[part]], axis=1)

    q[...] = (dot_nn(normed, weight(0)) + qb[0:1]).astype(BF16)
    k[...] = dot_nn(normed, weight(1)).astype(BF16)
    v[...] = (dot_nn(normed, weight(2)) + qb[1:2]).astype(BF16)

    @pl.when(index == 0)
    def _():
        first = coeffs_mine[0].astype(F32)
        second = coeffs_theirs[...].astype(F32)
        rows = jnp.concatenate(
            [jnp.where(me == 0, first, second), jnp.where(me == 0, second, first)], axis=0
        ).astype(BF16)
        coeffs_t[...] = rows.T
        mem_k[...] = dot_nn(rows, weight(1)).astype(BF16)
        mem_v[...] = dot_nn(rows, weight(2)).astype(BF16)


def project(order, scalars, hidden_in, hidden_come, vectors, w_own, w_far, qb, coeffs, coeffs_come):
    tokens, width = hidden_come.shape
    length = 2 * tokens
    part = coeffs_come.shape[0]
    basis = 2 * part
    rows = pl.BlockSpec((tokens, width), lambda i, s: (i, 0))
    return order.call(
        project_kernel,
        (2,),
        [
            pl.BlockSpec((1, tokens, width), lambda i, s: (s[0], 0, 0)),
            whole((tokens, width)),
            whole(vectors.shape),
            whole(w_own.shape),
            whole(w_far.shape),
            whole(qb.shape),
            pl.BlockSpec((1, part, width), lambda i, s: (s[0], 0, 0)),
            whole((part, width)),
        ],
        [
            rows,
            pl.BlockSpec((width, tokens), lambda i, s: (0, i)),
            rows,
            rows,
            rows,
            whole((basis, width)),
            whole((basis, width)),
            whole((width, basis)),
        ],
        [
            shape_of((length, width), BF16),
            shape_of((width, length), BF16),
            shape_of((length, width), BF16),
            shape_of((length, width), BF16),
            shape_of((length, width), BF16),
            shape_of((basis, width), BF16),
            shape_of((basis, width), BF16),
            shape_of((width, basis), BF16),
        ],
        2 * length * width * width * 3,
        "project",
        (hidden_in, hidden_come, vectors, w_own, w_far, qb, coeffs, coeffs_come),
        scalars=(scalars,),
    )


def head_rows(values_t, head):
    part = values_t[head * HD : (head + 1) * HD]
    zeros = jnp.zeros_like(part)
    return jnp.concatenate([part, zeros] if head == 0 else [zeros, part], axis=0)


def map_rows(mw, pair):
    return jnp.concatenate(
        [mw[2 * pair], mw[2 * pair + 1], jnp.zeros((4, mw.shape[2]), F32)], axis=0
    )


def pair_maps(rows, mem_k):
    maps = dot_nn(rows.astype(BF16), mem_k)
    row = lax.broadcasted_iota(jnp.int32, maps.shape, 0)
    lane = lax.broadcasted_iota(jnp.int32, maps.shape, 1)
    return jnp.where((row // 2) == (lane // HD), maps, 0.0)


def bias_rows(mb, pair):
    row = lax.broadcasted_iota(jnp.int32, (8, 1), 0)
    column = jnp.zeros((8, 1), F32)
    for head in range(2):
        for which in range(2):
            column = jnp.where(row == 2 * head + which, mb[which, 2 * pair + head], column)
    return column


def basis_of(logits, basis_count):
    centre = jax.nn.sigmoid(logits)
    softplus = jnp.maximum(logits, 0.0) + jnp.log(1.0 + jnp.exp(-jnp.abs(logits)))
    spread = 0.05 * softplus + (8.0 / basis_count) ** 2
    rate = -0.5 / spread
    level = lax.rsqrt(2.0 * math.pi * spread) / basis_count
    return centre, rate, level


def places_of(basis_count):
    steps = lax.broadcasted_iota(jnp.int32, (basis_count, BLOCK), 0).astype(F32)
    return (steps + 0.5) / basis_count


def attend_kernel(scalars, flags, q, k, v, mem_k, mem_v, mw, mb, att_t, mix_t, mix, stat):
    length = q.shape[0]
    basis = mem_k.shape[0]
    flag_value = flags[scalars[0]].astype(F32)
    q_t = (q[...].astype(F32) * 0.125).astype(BF16).T
    v_t = v[...].T
    mem_v_t = mem_v[...].T
    pair = pl.program_id(0)
    maps = pair_maps(map_rows(mw, pair), mem_k[...])
    logits = add_parts(dot_nn(three_parts(maps), q_t)) + bias_rows(mb, pair)
    centre, rate, level = basis_of(logits, basis)
    places = places_of(basis)
    allowed = lax.broadcasted_iota(jnp.int32, (BLOCK, BLOCK), 0) <= lax.broadcasted_iota(
        jnp.int32, (BLOCK, BLOCK), 1
    )
    stat[4:8, :] = logits[0:4]
    for head in range(2):
        rows = slice(head * HD, (head + 1) * HD)
        q_head = head_rows(q_t, head)
        v_ones = jnp.concatenate([v_t[rows], jnp.ones((16, length), BF16)], axis=0)
        for index in range(length // BLOCK):
            start, stop = index * BLOCK, (index + 1) * BLOCK
            q_block = q_head[:, start:stop]
            near = jnp.where(allowed, dot_nn(k[start:stop, :], q_block), -1e30)
            top = jnp.max(near, axis=0, keepdims=True)
            if index:
                far = dot_nn(k[:start, :], q_block)
                top = jnp.maximum(top, jnp.max(far, axis=0, keepdims=True))
            total = dot_nn(v_ones[:, start:stop], jnp.exp(near - top).astype(BF16))
            if index:
                total += dot_nn(v_ones[:, :start], jnp.exp(far - top).astype(BF16))
            denominator = total[HD : HD + 1]
            attended = total[:HD] / denominator
            att_t[rows, start:stop] = attended
            stat[head : head + 1, start:stop] = top + jnp.log(denominator)
            offset = places - centre[2 * head : 2 * head + 1, start:stop]
            mass = (
                jnp.exp(offset * offset * rate[2 * head + 1 : 2 * head + 2, start:stop])
                * level[2 * head + 1 : 2 * head + 2, start:stop]
            )
            recalled = dot_nn(mem_v_t[rows], mass.astype(BF16))
            mix_t[rows, start:stop] = (attended + flag_value * recalled).astype(BF16)
    mix[...] = mix_t[...].T


def attend(order, scalars, flags, q, k, v, mem_k, mem_v, mw, mb):
    length, width = q.shape
    basis = mem_k.shape[0]
    pairs = width // 128
    rows = pl.BlockSpec((length, 128), lambda p, *_: (0, p))
    mem_rows = pl.BlockSpec((basis, 128), lambda p, *_: (0, p))
    cols = pl.BlockSpec((128, length), lambda p, *_: (p, 0))
    return order.call(
        attend_kernel,
        (pairs,),
        [
            rows,
            rows,
            rows,
            mem_rows,
            mem_rows,
            whole(mw.shape),
            pl.BlockSpec(memory_space=pltpu.SMEM),
        ],
        [cols, cols, rows, pl.BlockSpec((8, length), lambda p, *_: (p, 0))],
        [
            shape_of((width, length), F32),
            shape_of((width, length), BF16),
            shape_of((length, width), BF16),
            shape_of((pairs * 8, length), F32),
        ],
        12 * length * length * width,
        "attend",
        (q, k, v, mem_k, mem_v, mw, mb),
        scalars=(scalars, flags),
    )


def attend_back_kernel(
    base, scalars, flags, q, k, v, mem_k, mem_v, mw, grad, att_t, stat, norm_t, coeffs_t, *refs
):
    dq, dk, dv, dmem_k, dmem_v, dqkv, dmw, sums = refs[-8:]
    length = q.shape[0]
    basis = mem_k.shape[0]
    flag_value = flags[scalars[0]].astype(F32)
    q_t = (q[...].astype(F32) * 0.125).astype(BF16).T
    k_t = k[...].T
    grad_t = grad[...].T
    lane = lax.broadcasted_iota(jnp.int32, (length, 128), 1)
    mem_rows = map_rows(mw, base + pl.program_id(0))
    maps = pair_maps(mem_rows, mem_k[...])
    logits = stat[4:8, :]
    logits = jnp.concatenate([logits, jnp.zeros_like(logits)], axis=0)
    centre, rate, level = basis_of(logits, basis)
    places = places_of(basis)
    allowed = lax.broadcasted_iota(jnp.int32, (BLOCK, BLOCK), 0) <= lax.broadcasted_iota(
        jnp.int32, (BLOCK, BLOCK), 1
    )
    q_lanes = []
    dk_lanes = []
    dv_lanes = []
    dmv_lanes = []
    mass_grads = []
    for head in range(2):
        rows = slice(head * HD, (head + 1) * HD)
        mine = (lane // HD) == head
        q_head_t = head_rows(q_t, head)
        grad_head_t = head_rows(grad_t, head)
        q_head = jnp.where(mine, q[...].astype(F32), 0.0).astype(BF16)
        grad_head = jnp.where(mine, grad[...].astype(F32), 0.0).astype(BF16)
        log_total = stat[head : head + 1, :]
        inner = jnp.sum(grad_t[rows].astype(F32) * att_t[rows], axis=0, keepdims=True)
        query_parts = [None] * (length // BLOCK)
        dk_parts = []
        dv_parts = []
        for index in range(length // BLOCK):
            start, stop = index * BLOCK, (index + 1) * BLOCK
            scores = dot_nn(k[start:stop, :], q_head_t[:, start:])
            weights = jnp.exp(scores - log_total[:, start:])
            diagonal = jnp.where(allowed, weights[:, :BLOCK], 0.0)
            if stop < length:
                weights = jnp.concatenate([diagonal, weights[:, BLOCK:]], axis=1)
            else:
                weights = diagonal
            weights_grad = dot_nn(v[start:stop, :], grad_head_t[:, start:])
            scores_grad = (weights * (weights_grad - inner[:, start:])).astype(BF16)
            dv_parts.append(dot_nn(weights.astype(BF16), grad_head[start:]))
            dk_parts.append(dot_nn(scores_grad, q_head[start:]))
            query = dot_nn(k_t[rows, start:stop], scores_grad)
            for later in range(index, length // BLOCK):
                piece = query[:, (later - index) * BLOCK : (later - index + 1) * BLOCK]
                kept = query_parts[later]
                query_parts[later] = piece if kept is None else kept + piece
        q_lanes.append(jnp.concatenate(query_parts, axis=1))
        dk_lanes.append(jnp.concatenate(dk_parts, axis=0))
        dv_lanes.append(jnp.concatenate(dv_parts, axis=0))
        sum_parts = []
        mem_total = None
        for index in range(length // BLOCK):
            start, stop = index * BLOCK, (index + 1) * BLOCK
            rate_row = rate[2 * head + 1 : 2 * head + 2, start:stop]
            offset = places - centre[2 * head : 2 * head + 1, start:stop]
            mass = (
                jnp.exp(offset * offset * rate_row) * level[2 * head + 1 : 2 * head + 2, start:stop]
            )
            basis_grad = dot_nn(mem_v[...], grad_head_t[:, start:stop])
            zeroth = basis_grad * mass
            first = zeroth * offset
            second = first * offset
            sum_parts.append(
                jnp.concatenate(
                    [
                        jnp.sum(first, axis=0, keepdims=True) * (-2.0 * rate_row),
                        jnp.sum(second, axis=0, keepdims=True) * (2.0 * rate_row * rate_row)
                        + jnp.sum(zeroth, axis=0, keepdims=True) * rate_row,
                    ],
                    axis=0,
                )
            )
            piece = dot_nn(mass.astype(BF16), grad_head[start:stop])
            mem_total = piece if mem_total is None else mem_total + piece
        dmv_lanes.append(mem_total)
        mass_grads.append(jnp.concatenate(sum_parts, axis=1))
    parity = lax.broadcasted_iota(jnp.int32, logits.shape, 0) % 2
    basis_grads = jnp.concatenate(
        mass_grads + [jnp.zeros((4, length), F32)], axis=0
    )
    slope = jnp.where(parity == 0, centre * (1.0 - centre), 0.05 * centre)
    logits_grad = basis_grads * slope * flag_value
    query_total = jnp.concatenate(q_lanes, axis=0) + dot_tn_exact(maps, logits_grad)
    dq[...] = (0.125 * query_total).T.astype(BF16)
    dk[...] = (0.125 * (dk_lanes[0] + dk_lanes[1])).astype(BF16)
    dv[...] = (dv_lanes[0] + dv_lanes[1]).astype(BF16)
    dmem_v[...] = (flag_value * (dmv_lanes[0] + dmv_lanes[1])).astype(BF16)
    row = lax.broadcasted_iota(jnp.int32, maps.shape, 0)
    lanes = lax.broadcasted_iota(jnp.int32, maps.shape, 1)
    outer = jnp.where(
        (row // 2) == (lanes // HD), add_parts(dot_nn(three_parts(logits_grad), q[...])) * 0.125, 0.0
    )
    dmem_k[...] = dot_tn_exact(mem_rows, outer).astype(BF16)
    dmw[0] = add_parts(dot_nt(three_parts(outer), mem_k[...]))
    ones = jnp.ones((16, length), BF16)
    sums[0, 0:8] = jnp.broadcast_to(jnp.sum(logits_grad, axis=1, keepdims=True), (8, 128))
    sums[0, 8:9] = dot_nn(ones, dq[...])[0:1]
    sums[0, 9:10] = dot_nn(ones, dv[...])[0:1]
    sums[0, 10:16] = jnp.zeros((6, 128), F32)
    width = norm_t.shape[0]
    rows_grad = dot_nn(norm_t[...], jnp.concatenate([dq[...], dk[...], dv[...]], axis=1))
    mem_grad = dot_nn(coeffs_t[...], jnp.concatenate([dmem_k[...], dmem_v[...]], axis=1))
    dqkv[:width] = rows_grad[:, :128].astype(BF16)
    dqkv[width : 2 * width] = (rows_grad[:, 128:256] + mem_grad[:, :128]).astype(BF16)
    dqkv[2 * width :] = (rows_grad[:, 256:] + mem_grad[:, 128:]).astype(BF16)


def attend_back(
    order, side, first, pairs, earlier, scalars, flags, q, k, v, mem_k, mem_v, mw, grad, att_t, stat, norm_t, coeffs_t
):
    length, width = q.shape
    basis = mem_k.shape[0]
    side_pairs = width // 256
    base = side * side_pairs + first
    half = width // 2
    rows = pl.BlockSpec((length, 128), lambda p, *_: (0, base + p))
    mem_rows = pl.BlockSpec((basis, 128), lambda p, *_: (0, base + p))
    out_rows = pl.BlockSpec((length, 128), lambda p, *_: (0, first + p))
    out_mem_rows = pl.BlockSpec((basis, 128), lambda p, *_: (0, first + p))
    operands = (q, k, v, mem_k, mem_v, mw, grad, att_t, stat, norm_t, coeffs_t)
    earlier = () if earlier is None else tuple(earlier)
    return order.call(
        functools.partial(attend_back_kernel, base),
        (pairs,),
        [
            rows,
            rows,
            rows,
            mem_rows,
            mem_rows,
            whole(mw.shape),
            rows,
            pl.BlockSpec((128, length), lambda p, *_: (base + p, 0)),
            pl.BlockSpec((8, length), lambda p, *_: (base + p, 0)),
            whole(norm_t.shape),
            whole(coeffs_t.shape),
        ]
        + [pl.BlockSpec(memory_space=pl.ANY)] * len(earlier),
        [
            out_rows,
            out_rows,
            out_rows,
            out_mem_rows,
            out_mem_rows,
            pl.BlockSpec((3 * width, 128), lambda p, *_: (0, first + p)),
            pl.BlockSpec((1, 8, basis), lambda p, *_: (first + p, 0, 0)),
            pl.BlockSpec((1, 16, 128), lambda p, *_: (first + p, 0, 0)),
        ],
        [shape_of((length, half), BF16)] * 3
        + [shape_of((basis, half), BF16)] * 2
        + [
            shape_of((3 * width, half), BF16),
            shape_of((side_pairs, 8, basis), F32),
            shape_of((side_pairs, 16, 128), F32),
        ],
        pairs * (28 * length * length * 128 + 6 * length * width * 128),
        "attend_back",
        operands + earlier,
        scalars=(scalars, flags),
        aliases={2 + len(operands) + index: index for index in range(len(earlier))},
    )


def residual_kernel(
    scalars, mix, hid, w_own, w_far, vectors, mine, theirs, middle, normed, normed_t, out_grad
):
    branch = dot_nn(mix[...], jnp.concatenate([w_own[...], w_far[...]], axis=0))
    rows = hid[...].astype(F32) + (branch + vectors[2:3])
    middle[...] = rows
    scaled, _ = scaled_rows(rows)
    result = (scaled * vectors[3:4] + vectors[4:5]).astype(BF16)
    normed[...] = result
    normed_t[...] = result.T
    index = pl.program_id(0)

    @pl.when(index == scalars[0])
    def _():
        out_grad[...] = mine[0]

    @pl.when(index != scalars[0])
    def _():
        out_grad[...] = theirs[...]


def residual(order, scalars, mix, hid, w_own, w_far, vectors, out_grad, out_grad_come):
    length, width = hid.shape
    tokens = length // 2
    rows = pl.BlockSpec((tokens, width), lambda i, s: (i, 0))
    return order.call(
        residual_kernel,
        (2,),
        [
            rows,
            rows,
            whole(w_own.shape),
            whole(w_far.shape),
            whole(vectors.shape),
            pl.BlockSpec((1, tokens, width), lambda i, s: (s[0], 0, 0)),
            whole((tokens, width)),
        ],
        [rows, rows, pl.BlockSpec((width, tokens), lambda i, s: (0, i)), rows],
        [
            shape_of((length, width), F32),
            shape_of((length, width), BF16),
            shape_of((width, length), BF16),
            shape_of((length, width), BF16),
        ],
        2 * length * width * width,
        "residual",
        (mix, hid, w_own, w_far, vectors, out_grad, out_grad_come),
        scalars=(scalars,),
    )


def branch_back_kernel(
    normed_grad, out_grad, middle, mix_t, w_own, w_far, vectors, mid_grad, mix_grad, dw_own, dw_far, sums, total
):
    index = pl.program_id(0)
    scaled, inverse = scaled_rows(middle[...])
    grad_rows = normed_grad[...]
    out_rows = out_grad[...].astype(F32)
    result = out_rows + norm_back(grad_rows, scaled, inverse, vectors[3:4])
    mid_grad[...] = result
    branch = result.astype(BF16)
    half = w_own.shape[0]
    mix_grad[...] = dot_nt(branch, jnp.concatenate([w_own[...], w_far[...]], axis=0)).astype(BF16)
    fresh = dot_nn(mix_t[...], branch)
    added = jnp.concatenate(
        [
            jnp.sum(branch.astype(F32), axis=0, keepdims=True),
            jnp.sum(grad_rows * scaled, axis=0, keepdims=True),
            jnp.sum(grad_rows, axis=0, keepdims=True),
            jnp.sum(out_rows, axis=0, keepdims=True),
            jnp.zeros((4, grad_rows.shape[1]), F32),
        ],
        axis=0,
    )

    @pl.when(index == 0)
    def _():
        total[...] = fresh
        sums[...] = added

    @pl.when(index > 0)
    def _():
        total[...] += fresh
        sums[...] += added

    @pl.when(index == pl.num_programs(0) - 1)
    def _():
        for side, out in enumerate((dw_own, dw_far)):
            rows = slice(side * half, (side + 1) * half)
            out[:half] = total[rows, :half].astype(BF16)
            out[half:] = total[rows, half:].astype(BF16)


def branch_back(order, normed_grad, out_grad, middle, mix_t, w_own, w_far, vectors):
    length, width = middle.shape
    rows = pl.BlockSpec((ROWS, width), lambda i: (i, 0))
    return order.call(
        branch_back_kernel,
        (length // ROWS,),
        [
            rows,
            rows,
            rows,
            pl.BlockSpec((width, ROWS), lambda i: (0, i)),
            whole(w_own.shape),
            whole(w_far.shape),
            whole(vectors.shape),
        ],
        [rows, rows, whole((width, width // 2)), whole((width, width // 2)), whole((8, width))],
        [
            shape_of((length, width), F32),
            shape_of((length, width), BF16),
            shape_of((width, width // 2), BF16),
            shape_of((width, width // 2), BF16),
            shape_of((8, width), F32),
        ],
        4 * length * width * width,
        "branch_back",
        (normed_grad, out_grad, middle, mix_t, w_own, w_far, vectors),
        scratch=[pltpu.VMEM((width, width), F32)],
    )


def feed_step(normed, normed_t, out_grad, up, up_bias, down, d_up, d_up_bias, d_down):
    weight_up = up[...]
    weight_down = down[...]
    before = dot_nn(normed[...], weight_up) + up_bias[...]
    out_rows = out_grad[...]
    hidden_grad = dot_nt(out_rows, weight_down)
    root = math.sqrt(2.0 / math.pi)
    square = before * before
    angle = jnp.tanh(before * (root + (root * 0.044715) * square))
    half_sum = 0.5 + 0.5 * angle
    activated = (before * half_sum).astype(BF16)
    slope = half_sum + before * (0.5 - 0.5 * angle * angle) * (
        root + (3.0 * 0.044715 * root) * square
    )
    before_grad = (hidden_grad * slope).astype(BF16)
    d_down[...] = dot_tn(activated, out_rows).astype(BF16)
    d_up[...] = dot_nn(normed_t[...], before_grad).astype(BF16)
    d_up_bias[...] = dot_nn(jnp.ones((8, before.shape[0]), BF16), before_grad)
    return dot_nn(activated, weight_down), dot_nt(before_grad, weight_up)


def feed_kernel(
    steps, scalars, normed, normed_t, out_grad, middle, vectors, up_far, up_own, ub_far, ub_own, down_far,
    down_own, grad_sum, du_far, du_own, dub_far, dub_own, dd_far, dd_own, mine, theirs,
    out_sum, up, ub, down, du, dub, dd,
):
    index = pl.program_id(0)

    @pl.when(index == 0)
    def _():
        out_sum[...] = jnp.zeros_like(out_sum)
        grad_sum[...] = jnp.zeros_like(grad_sum)

    for side, weights in ((0, (up_far, ub_far, down_far)), (1, (up_own, ub_own, down_own))):

        @pl.when((index >= steps) == (side == 1))
        def _():
            for held, source in zip((up, ub, down), weights):
                held[...] = source[...]

    forward, backward = feed_step(normed, normed_t, out_grad, up, ub, down, du, dub, dd)
    out_sum[...] += forward
    grad_sum[...] += backward
    for side, grads in ((0, (du_far, dub_far, dd_far)), (1, (du_own, dub_own, dd_own))):

        @pl.when((index >= steps) == (side == 1))
        def _():
            for target, held in zip(grads, (du, dub, dd)):
                target[...] = held[...]

    @pl.when(index == 2 * steps - 1)
    def _():
        tokens = theirs.shape[0]
        for target, half in ((mine.at[0], scalars[0]), (theirs, 1 - scalars[0])):
            at = pl.ds(pl.multiple_of(half * tokens, tokens), tokens)
            target[...] = (middle[at, :] + out_sum[at, :] + vectors[5:6]).astype(BF16)


def feed(order, scalars, normed, normed_t, out_grad, middle, vectors, up_far, up_own, ub_far, ub_own, down_far, down_own):
    length, width = normed.shape
    tokens = length // 2
    hidden = up_own.shape[1]
    steps = hidden // FEED_BLOCK

    def far_block(i):
        return jnp.minimum(i, steps - 1)

    def own_block(i):
        return jnp.maximum(i - steps, 0)

    def up_spec(block):
        return pl.BlockSpec((width, FEED_BLOCK), lambda i, s: (0, block(i)))

    def bias_spec(block, rows):
        return pl.BlockSpec((rows, FEED_BLOCK), lambda i, s: (0, block(i)))

    def down_spec(block):
        return pl.BlockSpec((FEED_BLOCK, width), lambda i, s: (block(i), 0))

    keep = whole((length, width))
    return order.call(
        functools.partial(feed_kernel, steps),
        (2 * steps,),
        [
            keep,
            whole((width, length)),
            keep,
            keep,
            whole(vectors.shape),
            up_spec(far_block),
            up_spec(own_block),
            bias_spec(far_block, 1),
            bias_spec(own_block, 1),
            down_spec(far_block),
            down_spec(own_block),
        ],
        [
            keep,
            up_spec(far_block),
            up_spec(own_block),
            bias_spec(far_block, 8),
            bias_spec(own_block, 8),
            down_spec(far_block),
            down_spec(own_block),
            pl.BlockSpec((1, tokens, width), lambda i, s: (s[0], 0, 0)),
            whole((tokens, width)),
        ],
        [
            shape_of((length, width), F32),
            shape_of((width, hidden), BF16),
            shape_of((width, hidden), BF16),
            shape_of((8, hidden), F32),
            shape_of((8, hidden), F32),
            shape_of((hidden, width), BF16),
            shape_of((hidden, width), BF16),
            shape_of((2, tokens, width), BF16),
            shape_of((tokens, width), BF16),
        ],
        24 * length * width * hidden,
        "feed",
        (normed, normed_t, out_grad, middle, vectors, up_far, up_own, ub_far, ub_own, down_far, down_own),
        scratch=[
            pltpu.VMEM((length, width), F32),
            pltpu.VMEM((width, FEED_BLOCK), BF16),
            pltpu.VMEM((1, FEED_BLOCK), F32),
            pltpu.VMEM((FEED_BLOCK, width), BF16),
            pltpu.VMEM((width, FEED_BLOCK), BF16),
            pltpu.VMEM((8, FEED_BLOCK), F32),
            pltpu.VMEM((FEED_BLOCK, width), BF16),
        ],
        scalars=(scalars,),
    )


def input_back_kernel(
    scalars, hid, mid_grad, vectors, w_own, w_far, dq_own, dk_own, dv_own, dq_far, dk_far, dv_far,
    dmk_own, dmv_own, dmk_far, dmv_far, mine, theirs, coeff_mine, coeff_theirs, sums, total,
):
    me = scalars[0]
    index = pl.program_id(0)

    def back(own, far, part):
        return dot_nt(
            jnp.concatenate([own[...], far[...]], axis=1),
            jnp.concatenate([w_own[part], w_far[part]], axis=1),
        )

    grad_rows = back(dq_own, dq_far, 0) + back(dk_own, dk_far, 1) + back(dv_own, dv_far, 2)
    scaled, inverse = scaled_rows(hid[...].astype(F32))
    result = mid_grad[...] + norm_back(grad_rows, scaled, inverse, vectors[0:1])

    @pl.when(index == me)
    def _():
        mine[0] = result

    @pl.when(index != me)
    def _():
        theirs[...] = result.astype(BF16)

    fresh = jnp.concatenate(
        [
            jnp.sum(grad_rows * scaled, axis=0, keepdims=True),
            jnp.sum(grad_rows, axis=0, keepdims=True),
            jnp.zeros((6, grad_rows.shape[1]), F32),
        ],
        axis=0,
    )

    @pl.when(index == 0)
    def _():
        sums[...] = fresh
        total[...] = back(dmk_own, dmk_far, 1) + back(dmv_own, dmv_far, 2)
        part = coeff_theirs.shape[0]
        coeff_mine[0] = total[pl.ds(pl.multiple_of(me * part, part), part), :]
        coeff_theirs[...] = total[
            pl.ds(pl.multiple_of((1 - me) * part, part), part), :
        ].astype(BF16)

    @pl.when(index > 0)
    def _():
        sums[...] += fresh


def input_back(order, scalars, hid, mid_grad, vectors, w_own, w_far, own, far):
    length, width = hid.shape
    tokens = length // 2
    basis, half = own[3].shape
    rows = pl.BlockSpec((tokens, width), lambda i, s: (i, 0))
    half_rows = pl.BlockSpec((tokens, half), lambda i, s: (i, 0))
    return order.call(
        input_back_kernel,
        (2,),
        [rows, rows, whole(vectors.shape), whole(w_own.shape), whole(w_far.shape)]
        + [half_rows] * 6
        + [whole((basis, half))] * 4,
        [
            pl.BlockSpec((1, tokens, width), lambda i, s: (s[0], 0, 0)),
            whole((tokens, width)),
            pl.BlockSpec((1, basis // 2, width), lambda i, s: (s[0], 0, 0)),
            whole((basis // 2, width)),
            whole((8, width)),
        ],
        [
            shape_of((2, tokens, width), F32),
            shape_of((tokens, width), BF16),
            shape_of((2, basis // 2, width), F32),
            shape_of((basis // 2, width), BF16),
            shape_of((8, width), F32),
        ],
        6 * length * width * width,
        "input_back",
        (hid, mid_grad, vectors, w_own, w_far, *own[:3], *far[:3], *own[3:5], *far[3:5]),
        scratch=[pltpu.VMEM((basis, width), F32)],
        scalars=(scalars,),
    )


def tokens_place_kernel(scalars, *refs):
    for come, out in zip(refs[:3], refs[6:]):
        out[0] = come[...].astype(out.dtype)


def tokens_place(order, scalars, filled, come):
    return order.call(
        tokens_place_kernel,
        (1,),
        [whole(c.shape) for c in come] + [pl.BlockSpec(memory_space=pl.ANY)] * 3,
        [pl.BlockSpec((1,) + f.shape[1:], lambda i, s: (1 - s[0], 0, 0)) for f in filled],
        [shape_of(f.shape, f.dtype) for f in filled],
        0,
        "tokens_place",
        tuple(come) + tuple(filled),
        scalars=(scalars,),
        aliases={4 + index: index for index in range(3)},
    )


def pack_kernel(own_maps, own_sums, own_bias, far_maps, far_sums, far_bias, mid_sums, first_sums, own, far):
    for maps, sums, bias, out in (
        (own_maps, own_sums, own_bias, own),
        (far_maps, far_sums, far_bias, far),
    ):
        row = 0

        def put(values):
            nonlocal row
            for start in range(0, values.shape[1], 128):
                out[row : row + 1] = values[:, start : start + 128]
                row += 1

        for pair in range(maps.shape[0]):
            for index in range(4):
                put(maps[pair, index : index + 1])
        for index in (8, 9):
            for pair in range(maps.shape[0]):
                put(sums[pair, index : index + 1])
        put(bias[0:1])
        for index in range(4):
            put(mid_sums[index : index + 1])
        for index in range(2):
            put(first_sums[index : index + 1])
        for pair in range(maps.shape[0]):
            for index in range(4):
                put(sums[pair, index : index + 1])
        out[row:] = jnp.zeros((out.shape[0] - row, 128), F32)


def pack(order, own, own_bias, far, far_bias, mid_sums, first_sums):
    operands = (own[6], own[7], own_bias, far[6], far[7], far_bias, mid_sums, first_sums)
    pairs, _, basis = own[6].shape
    width = mid_sums.shape[1]
    count = pairs * 4 * (basis // 128) + 6 * pairs + own_bias.shape[1] // 128 + 6 * width // 128
    count += -count % 8
    return order.call(
        pack_kernel,
        (1,),
        [whole(o.shape) for o in operands],
        [whole((count, 128))] * 2,
        [shape_of((count, 128), F32)] * 2,
        0,
        "pack",
        operands,
    )


def to_peer(values):
    return jax.tree.map(lambda v: lax.ppermute(v, "mp", [(0, 1), (1, 0)]), values)


def across(values, offset, count):
    return lax.ppermute(values, "batch", [(i, i ^ offset) for i in range(count)])


def added(left, right):
    return left + right


def halve_kernel(flip, scalars, *refs):
    for chunk in range(2):
        low, high, low_more, high_more = refs[4 * chunk : 4 * chunk + 4]
        keep, send = refs[8 + 2 * chunk : 10 + 2 * chunk]
        bit = scalars[1 + (chunk ^ flip)]

        @pl.when(bit == 0)
        def _():
            keep[...] = added(low[...], low_more[...])
            send[...] = added(high[...], high_more[...])

        @pl.when(bit != 0)
        def _():
            keep[...] = added(high[...], high_more[...])
            send[...] = added(low[...], low_more[...])


def share_kernel(group, scalars, keep_a, more_a, keep_b, more_b, *outs):
    rows_a = keep_a.shape[0] // group
    rows_b = keep_b.shape[0] // group
    width = keep_b.shape[1]
    for offset in range(group):
        place = scalars[3 + offset]
        at = pl.ds(pl.multiple_of(place * rows_a, rows_a), rows_a)
        share = added(keep_a[at, :], more_a[at, :])
        for part in range(keep_a.shape[1] // width):
            outs[offset][part * rows_a : (part + 1) * rows_a] = share[
                :, part * width : (part + 1) * width
            ]
        at = pl.ds(pl.multiple_of(place * rows_b, rows_b), rows_b)
        outs[offset][outs[offset].shape[0] - rows_b :] = added(keep_b[at, :], more_b[at, :])


def total_kernel(*refs):
    total = refs[0][...].astype(F32)
    for ref in refs[1:-1]:
        total += ref[...].astype(F32)
    refs[-1][...] = total.astype(BF16)


def spread_kernel(group, scalars, *refs):
    out = refs[group]
    rows = out.shape[0] // group
    for offset in range(group):
        at = pl.ds(pl.multiple_of(scalars[3 + offset] * rows, rows), rows)
        out[at, :] = refs[offset][...]


def small_kernel(left, right, out):
    out[...] = left[...] + right[...]


def small_add(order, left, right):
    return order.call(
        small_kernel,
        (1,),
        [whole(left.shape)] * 2,
        [whole(left.shape)],
        [shape_of(left.shape, F32)],
        0,
        "small_add",
        (left, right),
    )[0]


class BatchSum:
    def __init__(self, order, scalars, count):
        self.order = order
        self.scalars = scalars
        self.count = count
        self.group = min(4, count // 4)

    def halve(self, flip, quads):
        specs = []
        operands = []
        out_specs = []
        shapes = []
        for shape, quad in quads:
            cuts = self.cuts(shape[0])
            piece = (shape[0] // cuts, shape[1])
            for values, block in quad:
                specs.append(
                    pl.BlockSpec(
                        piece, lambda i, s, block=block, cuts=cuts: (block[0] * cuts + i, block[1])
                    )
                )
                operands.append(values)
            out_specs += [pl.BlockSpec(piece, lambda i, s: (i, 0))] * 2
            shapes += [shape, shape]
        keep_a, send_a, keep_b, send_b = self.order.call(
            functools.partial(halve_kernel, flip),
            (cuts,),
            specs,
            out_specs,
            [shape_of(s, BF16) for s in shapes],
            0,
            "halve",
            operands,
            scalars=(self.scalars,),
        )
        self.kept = (keep_a, keep_b)
        self.come = (
            across(send_a, 1 << flip, self.count),
            across(send_b, 2 >> flip, self.count),
        )

    def cuts(self, rows):
        return 4 if rows % 64 == 0 else 1

    def first(self, quads):
        self.halve(0, quads)

    def second(self):
        quads = []
        for kept, come in zip(self.kept, self.come):
            shape = (kept.shape[0] // 2, kept.shape[1])
            quads.append((shape, ((kept, (0, 0)), (kept, (1, 0)), (come, (0, 0)), (come, (1, 0)))))
        self.halve(1, quads)

    def around(self, own):
        return [own[0]] + [
            across(own[offset], offset << 2, self.count) for offset in range(1, self.group)
        ]

    def share(self):
        operands = (self.kept[0], self.come[0], self.kept[1], self.come[1])
        width = operands[2].shape[1]
        shape = ((operands[0].size + operands[2].size) // (width * self.group), width)
        self.shares = self.around(
            self.order.call(
                functools.partial(share_kernel, self.group),
                (1,),
                [whole(o.shape) for o in operands],
                [whole(shape)] * self.group,
                [shape_of(shape, BF16)] * self.group,
                0,
                "share",
                operands,
                scalars=(self.scalars,),
            )
        )

    def total(self):
        shape = self.shares[0].shape
        (self.mine,) = self.order.call(
            total_kernel,
            (1,),
            [whole(shape)] * self.group,
            [whole(shape)],
            [shape_of(shape, BF16)],
            0,
            "total",
            self.shares,
        )
        offset = 4 * self.group
        while offset < self.count:
            self.mine = added(self.mine, across(self.mine, offset, self.count))
            offset *= 2

    def around_rest(self):
        self.pieces = self.around([self.mine] * self.group)

    def spread(self):
        rows, width = self.mine.shape
        shape = (self.group * rows, width)
        (quarter,) = self.order.call(
            functools.partial(spread_kernel, self.group),
            (1,),
            [whole(p.shape) for p in self.pieces],
            [whole(shape)],
            [shape_of(shape, BF16)],
            0,
            "spread",
            self.pieces,
            scalars=(self.scalars,),
        )
        self.quarters = [quarter] + [
            across(quarter, offset, self.count) for offset in (1, 2, 3)
        ]


def peers_added_kernel(*refs):
    for index in range(2):
        refs[4 + index][...] = added(refs[2 * index][...], refs[2 * index + 1][...])


def peers_added(order, up_pair, down_pair):
    cuts = 4
    width = down_pair[0].shape[1]
    up_spec = pl.BlockSpec((up_pair[0].shape[0] // cuts, width), lambda i: (i, 1))
    up_out = pl.BlockSpec((up_pair[0].shape[0] // cuts, width), lambda i: (i, 0))
    down_spec = pl.BlockSpec((down_pair[0].shape[0] // cuts, width), lambda i: (i, 0))
    return order.call(
        peers_added_kernel,
        (cuts,),
        [up_spec, up_spec, down_spec, down_spec],
        [up_out, down_spec],
        [
            shape_of((up_pair[0].shape[0], width), BF16),
            shape_of(down_pair[0].shape, BF16),
        ],
        0,
        "peers_added",
        tuple(up_pair) + tuple(down_pair),
    )


def feed_place_kernel(up_sum, down_sum, _, up_out, down_out):
    up_out[...] = up_sum[...].astype(F32)
    down_out[...] = down_sum[...].astype(F32)


def feed_place(order, up_sum, down_sum, up_grad):
    cuts = 4
    width = down_sum.shape[1]
    up_rows = up_sum.shape[0] // cuts
    down_rows = down_sum.shape[0] // cuts
    return order.call(
        feed_place_kernel,
        (cuts,),
        [
            pl.BlockSpec((up_rows, width), lambda i: (i, 0)),
            pl.BlockSpec((down_rows, width), lambda i: (i, 0)),
            pl.BlockSpec(memory_space=pl.ANY),
        ],
        [
            pl.BlockSpec((up_rows, width), lambda i: (i, 1)),
            pl.BlockSpec((down_rows, width), lambda i: (i, 0)),
        ],
        [shape_of(up_grad.shape, F32), shape_of(down_sum.shape, F32)],
        0,
        "feed_place",
        (up_sum, down_sum, up_grad),
        aliases={2: 0},
    )


def mixed_halve_kernel(scalars, *refs):
    for chunk in range(2):
        keep, send = refs[16 + 2 * chunk : 18 + 2 * chunk]
        bit = scalars[1 + chunk]

        def fill(target, half):
            own, own_more, peer, peer_more = refs[8 * chunk + 4 * half : 8 * chunk + 4 * half + 4]
            rows = own.shape[0]
            target[:rows] = added(own[...], peer[...])
            target[rows:] = added(own_more[...], peer_more[...])

        @pl.when(bit == 0)
        def _():
            fill(keep, 0)
            fill(send, 1)

        @pl.when(bit != 0)
        def _():
            fill(keep, 1)
            fill(send, 0)


class MixedSum(BatchSum):
    def first(self, dqkv, dwo, du):
        width, cols = dwo[0].shape
        part = width // 2
        specs = []
        operands = []
        for chunk in range(2):
            for half in range(2):
                main = dwo if (chunk, half) == (1, 1) else dqkv
                block = 0 if main is dwo else 2 * chunk + half
                for side in range(2):
                    specs.append(pl.BlockSpec((width, cols), lambda i, s, b=block: (b, 0)))
                    specs.append(
                        pl.BlockSpec((part, cols), lambda i, s, h=half, c=chunk: (h, c))
                    )
                    operands += [main[side], du[side]]
        shape = (width + part, cols)
        keep_a, send_a, keep_b, send_b = self.order.call(
            mixed_halve_kernel,
            (1,),
            specs,
            [whole(shape)] * 4,
            [shape_of(shape, BF16)] * 4,
            0,
            "mixed_halve",
            operands,
            scalars=(self.scalars,),
        )
        self.kept = (keep_a, keep_b)
        self.come = (across(send_a, 1, self.count), across(send_b, 2, self.count))


def mixed_place_kernel(group, scalars, *refs):
    qkv_out, up_out, wo_out = refs[-3:]
    cols = refs[0].shape[1]
    width = wo_out.shape[1]
    part = width // 2
    rows = refs[0].shape[0] // (2 * group)

    def segments(quarter, place):
        start = (quarter * group + place) * rows
        marks = [start] + [m for m in (part, width) if start < m < start + rows] + [start + rows]
        return [(a, a - start, b - a) for a, b in zip(marks, marks[1:])]

    for index in range(4):
        column = scalars[1] ^ (index % 2)
        row = scalars[2] ^ (index // 2)
        values = refs[index]
        for quarter in range(2):

            @pl.when(row == quarter)
            def _():
                for place in range(group):
                    for at, inner, size in segments(quarter, place):
                        start = 2 * place * rows + inner
                        piece = values[start : start + size].astype(F32)
                        if at < width:
                            to = pl.multiple_of(column * width + at, 16)
                            qkv_out[pl.ds(to, size), :] = piece
                        else:
                            to = pl.multiple_of(column * part + at - width, 16)
                            up_out[pl.ds(to, size), :cols] = piece

            for half in range(2):

                @pl.when((column == quarter) & (row == half))
                def _():
                    for place in range(group):
                        for at, inner, size in segments(quarter, place):
                            start = (2 * place + 1) * rows + inner
                            piece = values[start : start + size].astype(F32)
                            if at >= width:
                                to = half * part + at - width
                                up_out[to : to + size, cols:] = piece
                            elif half == 0:
                                qkv_out[2 * width + at : 2 * width + at + size] = piece
                            elif at < part:
                                wo_out[at : at + size, :cols] = piece
                            else:
                                wo_out[at - part : at - part + size, cols:] = piece


def mixed_place(order, scalars, summed, width, hidden):
    half = width // 2
    return order.call(
        functools.partial(mixed_place_kernel, summed.group),
        (1,),
        [whole(o.shape) for o in summed.quarters],
        [
            whole((3 * width, half)),
            pl.BlockSpec((width, width), lambda i, s: (0, 0)),
            whole((half, width)),
        ],
        [
            shape_of((3 * width, half), F32),
            shape_of((width, hidden), F32),
            shape_of((half, width), F32),
        ],
        0,
        "mixed_place",
        summed.quarters,
        scalars=(scalars,),
    )


def per_device(
    count,
    hidden_in,
    memory_flags,
    memory_coeffs,
    first_gain,
    first_bias,
    query_key_value_matrix,
    qv_bias,
    memory_weight,
    memory_bias,
    output_matrix,
    out_bias,
    second_gain,
    second_bias,
    up_matrix,
    up_bias_vector,
    down_matrix,
    down_bias,
    out_grad,
):
    me = lax.axis_index("mp")
    position = lax.axis_index("batch")
    width = hidden_in.shape[2]
    half = width // 2
    group = min(4, count // 4)
    place = (position >> 2) % group
    scalars = jnp.stack(
        [me, position & 1, (position >> 1) & 1] + [place ^ offset for offset in range(group)]
    ).astype(jnp.int32)

    def from_peer(values):
        return to_peer(lax.dynamic_index_in_dim(values, 1 - me, 0, keepdims=False))

    hidden_come = from_peer(hidden_in)
    w_own = jnp.transpose(query_key_value_matrix, (1, 0, 2))
    w_far = to_peer(w_own)
    coeffs_come = from_peer(memory_coeffs)
    qv_far, mw_far, mb_far, ub_far = to_peer(
        (qv_bias, memory_weight, memory_bias, up_bias_vector)
    )

    query_bias = jnp.concatenate([qv_bias, qv_far], axis=1).astype(F32)
    mem_maps = jnp.concatenate([memory_weight, mw_far], axis=1).astype(F32)
    mem_maps = jnp.transpose(mem_maps, (1, 0, 2))
    mem_biases = jnp.concatenate([memory_bias, mb_far], axis=1).astype(F32)
    vectors = jnp.stack(
        [first_gain, first_bias, out_bias, second_gain, second_bias, down_bias] + [down_bias] * 2
    )
    order = Order()
    hid, norm_t, q, k, v, mem_k, mem_v, coeffs_t = project(
        order, scalars, hidden_in, hidden_come, vectors, w_own, w_far, query_bias, memory_coeffs, coeffs_come
    )
    later, _ = lax.optimization_barrier(
        ((output_matrix, out_grad, up_matrix, down_matrix), (coeffs_t, mw_far, mb_far, ub_far))
    )
    wo_far = to_peer(later[0])
    out_grad_come = from_peer(later[1])
    up_far = to_peer(later[2])
    down_far = to_peer(later[3])
    att_t, mix_t, mix, stat = attend(
        order, scalars, memory_flags, q, k, v, mem_k, mem_v, mem_maps, mem_biases
    )
    middle, normed, normed_t, out_rows = residual(
        order, scalars, mix, hid, output_matrix, wo_far, vectors, out_grad, out_grad_come
    )
    grad_sum, du_far, du_own, dub_far, dub_own, dd_far, dd_own, block_mine, block_theirs = feed(
        order,
        scalars,
        normed,
        normed_t,
        out_rows,
        middle,
        vectors,
        up_far,
        up_matrix,
        ub_far.astype(F32)[None],
        up_bias_vector.astype(F32)[None],
        down_far,
        down_matrix,
    )
    du_peer, dd_peer = to_peer((du_far, dd_far))
    block_come = to_peer(block_theirs)
    mid_grad, mix_grad, dwo_own, dwo_far, mid_sums = branch_back(
        order, grad_sum, out_rows, middle, mix_t, output_matrix, wo_far, vectors
    )
    dwo_peer = to_peer(dwo_far)
    up_sum, down_sum = peers_added(order, (du_own, du_peer), (dd_own, dd_peer))
    up_sum, down_sum = lax.psum((up_sum, down_sum), "batch")
    back_args = (
        scalars, memory_flags, q, k, v, mem_k, mem_v, mem_maps, mix_grad, att_t, stat, norm_t, coeffs_t
    )
    pairs = width // 256
    far = attend_back(order, 1, 0, pairs, None, *back_args)
    dqkv_peer = to_peer(far[5])
    own = attend_back(order, 0, 0, pairs, None, *back_args)
    dqkv_own = own[5]
    last = MixedSum(order, scalars, count)
    last.first((dqkv_own, dqkv_peer), (dwo_own, dwo_peer), (du_own, du_peer))
    in_mine, in_theirs, coeff_mine, coeff_theirs, first_sums = input_back(
        order, scalars, hid, mid_grad, vectors, w_own, w_far, own, far
    )
    small, far_flat = pack(order, own, dub_own, far, dub_far, mid_sums, first_sums)
    last.second()
    come, in_come, coeff_come = to_peer(
        lax.optimization_barrier((far_flat, in_theirs, coeff_theirs, last.kept[0]))[:3]
    )
    block_out, input_grad, coeff_grad = tokens_place(
        order, scalars, (block_mine, in_mine, coeff_mine), (block_come, in_come, coeff_come)
    )
    last.share()
    small = small_add(order, small, come)
    small = small_add(order, small, across(small, 1, count))
    last.total()
    last.around_rest()
    small = small_add(order, small, across(small, 2, count))
    last.spread()
    offset = 4
    while offset < count:
        small = small_add(order, small, across(small, offset, count))
        offset *= 2
    query_key_value_grad, up_weight_grad, output_matrix_grad = mixed_place(
        order, scalars, last, width, up_matrix.shape[1]
    )
    query_key_value_grad = jnp.transpose(
        query_key_value_grad.reshape(3, width, half), (1, 0, 2)
    )
    up_weight_grad, down_weight_grad = feed_place(order, up_sum, down_sum, up_weight_grad)

    heads, basis = memory_weight.shape[1:]
    rows = 0

    def take(size):
        nonlocal rows
        piece = small[rows : rows + size // 128]
        rows += size // 128
        return piece

    memory_weight_grad = jnp.transpose(take(2 * heads * basis).reshape(heads, 2, basis), (1, 0, 2))
    qv_bias_grad = take(2 * half).reshape(2, half)
    up_bias_grad = take(up_bias_vector.shape[0]).reshape(-1)
    vector_grads = [take(width).reshape(-1) for _ in range(6)]
    memory_bias_grad = jnp.transpose(take(2 * heads * 128)[:, 0].reshape(heads, 2), (1, 0))
    return (
        block_out,
        input_grad,
        coeff_grad,
        vector_grads[4],
        vector_grads[5],
        query_key_value_grad,
        qv_bias_grad,
        memory_weight_grad,
        memory_bias_grad,
        output_matrix_grad,
        vector_grads[0],
        vector_grads[1],
        vector_grads[2],
        up_weight_grad,
        up_bias_grad,
        down_weight_grad,
        vector_grads[3],
    )


def solution(mesh):
    tokens = P("batch", "mp", None)
    return jax.shard_map(
        functools.partial(per_device, mesh.shape["batch"]),
        mesh=mesh,
        in_specs=(
            tokens,
            P("batch"),
            tokens,
            P(),
            P(),
            P(None, None, "mp"),
            P(None, "mp"),
            P(None, "mp", None),
            P(None, "mp"),
            P("mp", None),
            P(),
            P(),
            P(),
            P(None, "mp"),
            P("mp"),
            P("mp", None),
            P(),
            tokens,
        ),
        out_specs=(
            tokens,
            tokens,
            tokens,
            P(),
            P(),
            P(None, None, "mp"),
            P(None, "mp"),
            P(None, "mp", None),
            P(None, "mp"),
            P("mp", None),
            P(),
            P(),
            P(),
            P(None, "mp"),
            P("mp"),
            P("mp", None),
            P(),
        ),
        check_vma=False,
    )
```

```python
import functools
import math

import jax
import jax.numpy as jnp
from jax import lax
from jax.experimental import pallas as pl
from jax.experimental.pallas import tpu as pltpu
from jax.sharding import PartitionSpec as P

HD = 64
BLOCK = 256
FEED_BLOCK = 512
BF16 = jnp.bfloat16
F32 = jnp.float32
VMEM_BYTES = 56 * 2**20


def dot_nn(left, right):
    return lax.dot_general(left, right, (((1,), (0,)), ((), ())), preferred_element_type=F32)


def dot_nt(left, right):
    return lax.dot_general(left, right, (((1,), (1,)), ((), ())), preferred_element_type=F32)


def dot_tn(left, right):
    return lax.dot_general(left, right, (((0,), (0,)), ((), ())), preferred_element_type=F32)


def dot_tn_exact(left, right):
    return lax.dot_general(
        left,
        right,
        (((0,), (0,)), ((), ())),
        precision=lax.Precision.HIGHEST,
        preferred_element_type=F32,
    )


def three_parts(values):
    high = values.astype(BF16).astype(F32)
    rest = values - high
    middle = rest.astype(BF16).astype(F32)
    return jnp.concatenate([high, middle, rest - middle], axis=0).astype(BF16)


def add_parts(stacked):
    rows = stacked.shape[0] // 3
    return stacked[:rows] + stacked[rows : 2 * rows] + stacked[2 * rows :]


def scaled_rows(values):
    row_mean = jnp.mean(values, axis=-1, keepdims=True)
    centred = values - row_mean
    row_var = jnp.mean(centred * centred, axis=-1, keepdims=True)
    inverse = lax.rsqrt(row_var + 1e-05)
    return centred * inverse, inverse


def norm_back(grad_out, scaled, inverse, gain_vec):
    grad_scaled = grad_out * gain_vec
    first_mean = jnp.mean(grad_scaled, axis=-1, keepdims=True)
    second_mean = jnp.mean(grad_scaled * scaled, axis=-1, keepdims=True)
    return inverse * (grad_scaled - first_mean - scaled * second_mean)


def whole(shape):
    return pl.BlockSpec(shape, lambda *_: (0,) * len(shape))


class Order:
    def __init__(self):
        self.token = None

    def call(
        self, kernel, grid, in_specs, out_specs, out_shape, flops, name, operands, scratch=(), scalars=(),
        aliases=None,
    ):
        count = len(operands)
        prefetched = len(scalars)
        token = () if self.token is None else (self.token,)

        def body(*refs):
            kernel(*refs[: prefetched + count], *refs[prefetched + count + len(token) :])

        bytes_accessed = sum(math.prod(s.shape) * jnp.dtype(s.dtype).itemsize for s in out_shape)
        results = pl.pallas_call(
            body,
            grid_spec=pltpu.PrefetchScalarGridSpec(
                num_scalar_prefetch=prefetched,
                grid=grid,
                in_specs=list(in_specs) + [pl.BlockSpec(memory_space=pl.ANY)] * len(token),
                out_specs=list(out_specs),
                scratch_shapes=list(scratch),
            ),
            out_shape=out_shape,
            input_output_aliases=aliases or {},
            compiler_params=pltpu.CompilerParams(
                vmem_limit_bytes=VMEM_BYTES, dimension_semantics=("arbitrary",) * len(grid)
            ),
            cost_estimate=pl.CostEstimate(
                flops=int(flops), bytes_accessed=2 * bytes_accessed, transcendentals=0
            ),
            name=name,
        )(*scalars, *operands, *token)
        self.token = results[-1]
        return results


def shape_of(shape, dtype):
    return jax.ShapeDtypeStruct(shape, dtype)


def project_kernel(
    scalars, mine, theirs, vectors, w_own, w_far, qb, coeffs_mine, coeffs_theirs,
    hid, norm_t, q, k, v, mem_k, mem_v, coeffs_t,
):
    me = scalars[0]
    index = pl.program_id(0)

    @pl.when(index == me)
    def _():
        hid[...] = mine[0]

    @pl.when(index != me)
    def _():
        hid[...] = theirs[...]

    scaled, _ = scaled_rows(hid[...].astype(F32))
    normed = (scaled * vectors[0:1] + vectors[1:2]).astype(BF16)
    norm_t[...] = normed.T

    def weight(part):
        return jnp.concatenate([w_own[part], w_far[part]], axis=1)

    q[...] = (dot_nn(normed, weight(0)) + qb[0:1]).astype(BF16)
    k[...] = dot_nn(normed, weight(1)).astype(BF16)
    v[...] = (dot_nn(normed, weight(2)) + qb[1:2]).astype(BF16)

    @pl.when(index == 0)
    def _():
        first = coeffs_mine[0].astype(F32)
        second = coeffs_theirs[...].astype(F32)
        rows = jnp.concatenate(
            [jnp.where(me == 0, first, second), jnp.where(me == 0, second, first)], axis=0
        ).astype(BF16)
        coeffs_t[...] = rows.T
        mem_k[...] = dot_nn(rows, weight(1)).astype(BF16)
        mem_v[...] = dot_nn(rows, weight(2)).astype(BF16)


def project(order, scalars, hidden_in, hidden_come, vectors, w_own, w_far, qb, coeffs, coeffs_come):
    tokens, width = hidden_come.shape
    length = 2 * tokens
    part = coeffs_come.shape[0]
    basis = 2 * part
    rows = pl.BlockSpec((tokens, width), lambda i, s: (i, 0))
    return order.call(
        project_kernel,
        (2,),
        [
            pl.BlockSpec((1, tokens, width), lambda i, s: (s[0], 0, 0)),
            whole((tokens, width)),
            whole(vectors.shape),
            whole(w_own.shape),
            whole(w_far.shape),
            whole(qb.shape),
            pl.BlockSpec((1, part, width), lambda i, s: (s[0], 0, 0)),
            whole((part, width)),
        ],
        [
            rows,
            pl.BlockSpec((width, tokens), lambda i, s: (0, i)),
            rows,
            rows,
            rows,
            whole((basis, width)),
            whole((basis, width)),
            whole((width, basis)),
        ],
        [
            shape_of((length, width), BF16),
            shape_of((width, length), BF16),
            shape_of((length, width), BF16),
            shape_of((length, width), BF16),
            shape_of((length, width), BF16),
            shape_of((basis, width), BF16),
            shape_of((basis, width), BF16),
            shape_of((width, basis), BF16),
        ],
        2 * length * width * width * 3,
        "project",
        (hidden_in, hidden_come, vectors, w_own, w_far, qb, coeffs, coeffs_come),
        scalars=(scalars,),
    )


def head_rows(values_t, head):
    part = values_t[head * HD : (head + 1) * HD]
    zeros = jnp.zeros_like(part)
    return jnp.concatenate([part, zeros] if head == 0 else [zeros, part], axis=0)


def map_rows(mw, pair):
    return jnp.concatenate(
        [mw[2 * pair], mw[2 * pair + 1], jnp.zeros((4, mw.shape[2]), F32)], axis=0
    )


def pair_maps(rows, mem_k):
    maps = dot_nn(rows.astype(BF16), mem_k)
    row = lax.broadcasted_iota(jnp.int32, maps.shape, 0)
    lane = lax.broadcasted_iota(jnp.int32, maps.shape, 1)
    return jnp.where((row // 2) == (lane // HD), maps, 0.0)


def bias_rows(mb, pair):
    row = lax.broadcasted_iota(jnp.int32, (8, 1), 0)
    column = jnp.zeros((8, 1), F32)
    for head in range(2):
        for which in range(2):
            column = jnp.where(row == 2 * head + which, mb[which, 2 * pair + head], column)
    return column


def basis_of(logits, basis_count):
    centre = jax.nn.sigmoid(logits)
    softplus = jnp.maximum(logits, 0.0) + jnp.log(1.0 + jnp.exp(-jnp.abs(logits)))
    spread = 0.05 * softplus + (8.0 / basis_count) ** 2
    rate = -0.5 / spread
    level = lax.rsqrt(2.0 * math.pi * spread) / basis_count
    return centre, rate, level


def places_of(basis_count):
    steps = lax.broadcasted_iota(jnp.int32, (basis_count, BLOCK), 0).astype(F32)
    return (steps + 0.5) / basis_count


def attend_kernel(scalars, flags, q, k, v, mem_k, mem_v, mw, mb, att_t, mix_t, mix, stat):
    length = q.shape[0]
    basis = mem_k.shape[0]
    flag_value = flags[scalars[0]].astype(F32)
    q_t = (q[...].astype(F32) * 0.125).astype(BF16).T
    v_t = v[...].T
    mem_v_t = mem_v[...].T
    pair = pl.program_id(0)
    maps = pair_maps(map_rows(mw, pair), mem_k[...])
    logits = add_parts(dot_nn(three_parts(maps), q_t)) + bias_rows(mb, pair)
    centre, rate, level = basis_of(logits, basis)
    places = places_of(basis)
    allowed = lax.broadcasted_iota(jnp.int32, (BLOCK, BLOCK), 0) <= lax.broadcasted_iota(
        jnp.int32, (BLOCK, BLOCK), 1
    )
    stat[4:8, :] = logits[0:4]
    heads = []
    for head in range(2):
        rows = slice(head * HD, (head + 1) * HD)
        v_ones = jnp.concatenate([v_t[rows], jnp.ones((16, length), BF16)], axis=0)
        heads.append((rows, head_rows(q_t, head), v_ones))
    for index in range(length // BLOCK):
        start, stop = index * BLOCK, (index + 1) * BLOCK
        scores = []
        for rows, q_head, v_ones in heads:
            scores.append(dot_nn(k[:stop, :], q_head[:, start:stop]))
        for head, (rows, q_head, v_ones) in enumerate(heads):
            near = jnp.where(allowed, scores[head][start:], -1e30)
            top = jnp.max(near, axis=0, keepdims=True)
            if index:
                far = scores[head][:start]
                top = jnp.maximum(top, jnp.max(far, axis=0, keepdims=True))
                weights = jnp.concatenate([jnp.exp(far - top), jnp.exp(near - top)], axis=0)
            else:
                weights = jnp.exp(near - top)
            total = dot_nn(v_ones[:, :stop], weights.astype(BF16))
            denominator = total[HD : HD + 1]
            attended = total[:HD] / denominator
            att_t[rows, start:stop] = attended
            stat[head : head + 1, start:stop] = top + jnp.log(denominator)
            offset = places - centre[2 * head : 2 * head + 1, start:stop]
            mass = (
                jnp.exp(offset * offset * rate[2 * head + 1 : 2 * head + 2, start:stop])
                * level[2 * head + 1 : 2 * head + 2, start:stop]
            )
            recalled = dot_nn(mem_v_t[rows], mass.astype(BF16))
            mix_t[rows, start:stop] = (attended + flag_value * recalled).astype(BF16)
    mix[...] = mix_t[...].T


def attend(order, scalars, flags, q, k, v, mem_k, mem_v, mw, mb):
    length, width = q.shape
    basis = mem_k.shape[0]
    pairs = width // 128
    rows = pl.BlockSpec((length, 128), lambda p, *_: (0, p))
    mem_rows = pl.BlockSpec((basis, 128), lambda p, *_: (0, p))
    cols = pl.BlockSpec((128, length), lambda p, *_: (p, 0))
    return order.call(
        attend_kernel,
        (pairs,),
        [
            rows,
            rows,
            rows,
            mem_rows,
            mem_rows,
            whole(mw.shape),
            pl.BlockSpec(memory_space=pltpu.SMEM),
        ],
        [cols, cols, rows, pl.BlockSpec((8, length), lambda p, *_: (p, 0))],
        [
            shape_of((width, length), F32),
            shape_of((width, length), BF16),
            shape_of((length, width), BF16),
            shape_of((pairs * 8, length), F32),
        ],
        12 * length * length * width,
        "attend",
        (q, k, v, mem_k, mem_v, mw, mb),
        scalars=(scalars, flags),
    )


def attend_back_kernel(
    base, scalars, flags, q, k, v, mem_k, mem_v, mw, grad, att_t, stat, norm_t, coeffs_t, *refs
):
    dq, dk, dv, dmem_k, dmem_v, dqkv, dmw, sums = refs[-8:]
    length = q.shape[0]
    basis = mem_k.shape[0]
    flag_value = flags[scalars[0]].astype(F32)
    q_t = (q[...].astype(F32) * 0.125).astype(BF16).T
    k_t = k[...].T
    grad_t = grad[...].T
    lane = lax.broadcasted_iota(jnp.int32, (length, 128), 1)
    mem_rows = map_rows(mw, base + pl.program_id(0))
    maps = pair_maps(mem_rows, mem_k[...])
    logits = stat[4:8, :]
    logits = jnp.concatenate([logits, jnp.zeros_like(logits)], axis=0)
    centre, rate, level = basis_of(logits, basis)
    places = places_of(basis)
    allowed = lax.broadcasted_iota(jnp.int32, (BLOCK, BLOCK), 0) <= lax.broadcasted_iota(
        jnp.int32, (BLOCK, BLOCK), 1
    )
    q_lanes = []
    dk_lanes = []
    dv_lanes = []
    dmv_lanes = []
    mass_grads = []
    for head in range(2):
        rows = slice(head * HD, (head + 1) * HD)
        mine = (lane // HD) == head
        q_head_t = head_rows(q_t, head)
        grad_head_t = head_rows(grad_t, head)
        q_head = jnp.where(mine, q[...].astype(F32), 0.0).astype(BF16)
        grad_head = jnp.where(mine, grad[...].astype(F32), 0.0).astype(BF16)
        log_total = stat[head : head + 1, :]
        inner = jnp.sum(grad_t[rows].astype(F32) * att_t[rows], axis=0, keepdims=True)
        query_parts = [None] * (length // BLOCK)
        dk_parts = []
        dv_parts = []
        for index in range(length // BLOCK):
            start, stop = index * BLOCK, (index + 1) * BLOCK
            scores = dot_nn(k[start:stop, :], q_head_t[:, start:])
            weights = jnp.exp(scores - log_total[:, start:])
            diagonal = jnp.where(allowed, weights[:, :BLOCK], 0.0)
            if stop < length:
                weights = jnp.concatenate([diagonal, weights[:, BLOCK:]], axis=1)
            else:
                weights = diagonal
            weights_grad = dot_nn(v[start:stop, :], grad_head_t[:, start:])
            scores_grad = (weights * (weights_grad - inner[:, start:])).astype(BF16)
            dv_parts.append(dot_nn(weights.astype(BF16), grad_head[start:]))
            dk_parts.append(dot_nn(scores_grad, q_head[start:]))
            query = dot_nn(k_t[rows, start:stop], scores_grad)
            for later in range(index, length // BLOCK):
                piece = query[:, (later - index) * BLOCK : (later - index + 1) * BLOCK]
                kept = query_parts[later]
                query_parts[later] = piece if kept is None else kept + piece
        q_lanes.append(jnp.concatenate(query_parts, axis=1))
        dk_lanes.append(jnp.concatenate(dk_parts, axis=0))
        dv_lanes.append(jnp.concatenate(dv_parts, axis=0))
        sum_parts = []
        mem_total = None
        for index in range(length // BLOCK):
            start, stop = index * BLOCK, (index + 1) * BLOCK
            rate_row = rate[2 * head + 1 : 2 * head + 2, start:stop]
            offset = places - centre[2 * head : 2 * head + 1, start:stop]
            mass = (
                jnp.exp(offset * offset * rate_row) * level[2 * head + 1 : 2 * head + 2, start:stop]
            )
            basis_grad = dot_nn(mem_v[...], grad_head_t[:, start:stop])
            zeroth = basis_grad * mass
            first = zeroth * offset
            second = first * offset
            sum_parts.append(
                jnp.concatenate(
                    [
                        jnp.sum(first, axis=0, keepdims=True) * (-2.0 * rate_row),
                        jnp.sum(second, axis=0, keepdims=True) * (2.0 * rate_row * rate_row)
                        + jnp.sum(zeroth, axis=0, keepdims=True) * rate_row,
                    ],
                    axis=0,
                )
            )
            piece = dot_nn(mass.astype(BF16), grad_head[start:stop])
            mem_total = piece if mem_total is None else mem_total + piece
        dmv_lanes.append(mem_total)
        mass_grads.append(jnp.concatenate(sum_parts, axis=1))
    parity = lax.broadcasted_iota(jnp.int32, logits.shape, 0) % 2
    basis_grads = jnp.concatenate(
        mass_grads + [jnp.zeros((4, length), F32)], axis=0
    )
    slope = jnp.where(parity == 0, centre * (1.0 - centre), 0.05 * centre)
    logits_grad = basis_grads * slope * flag_value
    query_total = jnp.concatenate(q_lanes, axis=0) + dot_tn_exact(maps, logits_grad)
    dq[...] = (0.125 * query_total).T.astype(BF16)
    dk[...] = (0.125 * (dk_lanes[0] + dk_lanes[1])).astype(BF16)
    dv[...] = (dv_lanes[0] + dv_lanes[1]).astype(BF16)
    dmem_v[...] = (flag_value * (dmv_lanes[0] + dmv_lanes[1])).astype(BF16)
    row = lax.broadcasted_iota(jnp.int32, maps.shape, 0)
    lanes = lax.broadcasted_iota(jnp.int32, maps.shape, 1)
    outer = jnp.where(
        (row // 2) == (lanes // HD), add_parts(dot_nn(three_parts(logits_grad), q[...])) * 0.125, 0.0
    )
    dmem_k[...] = dot_tn_exact(mem_rows, outer).astype(BF16)
    dmw[0] = add_parts(dot_nt(three_parts(outer), mem_k[...]))
    ones = jnp.ones((16, length), BF16)
    sums[0, 0:8] = jnp.broadcast_to(jnp.sum(logits_grad, axis=1, keepdims=True), (8, 128))
    sums[0, 8:9] = dot_nn(ones, dq[...])[0:1]
    sums[0, 9:10] = dot_nn(ones, dv[...])[0:1]
    sums[0, 10:16] = jnp.zeros((6, 128), F32)
    width = norm_t.shape[0]
    rows_grad = dot_nn(norm_t[...], jnp.concatenate([dq[...], dk[...], dv[...]], axis=1))
    mem_grad = dot_nn(coeffs_t[...], jnp.concatenate([dmem_k[...], dmem_v[...]], axis=1))
    dqkv[:width] = rows_grad[:, :128].astype(BF16)
    dqkv[width : 2 * width] = (rows_grad[:, 128:256] + mem_grad[:, :128]).astype(BF16)
    dqkv[2 * width :] = (rows_grad[:, 256:] + mem_grad[:, 128:]).astype(BF16)


def attend_back(
    order, side, first, pairs, earlier, scalars, flags, q, k, v, mem_k, mem_v, mw, grad, att_t, stat, norm_t, coeffs_t
):
    length, width = q.shape
    basis = mem_k.shape[0]
    side_pairs = width // 256
    base = side * side_pairs + first
    half = width // 2
    rows = pl.BlockSpec((length, 128), lambda p, *_: (0, base + p))
    mem_rows = pl.BlockSpec((basis, 128), lambda p, *_: (0, base + p))
    out_rows = pl.BlockSpec((length, 128), lambda p, *_: (0, first + p))
    out_mem_rows = pl.BlockSpec((basis, 128), lambda p, *_: (0, first + p))
    operands = (q, k, v, mem_k, mem_v, mw, grad, att_t, stat, norm_t, coeffs_t)
    earlier = () if earlier is None else tuple(earlier)
    return order.call(
        functools.partial(attend_back_kernel, base),
        (pairs,),
        [
            rows,
            rows,
            rows,
            mem_rows,
            mem_rows,
            whole(mw.shape),
            rows,
            pl.BlockSpec((128, length), lambda p, *_: (base + p, 0)),
            pl.BlockSpec((8, length), lambda p, *_: (base + p, 0)),
            whole(norm_t.shape),
            whole(coeffs_t.shape),
        ]
        + [pl.BlockSpec(memory_space=pl.ANY)] * len(earlier),
        [
            out_rows,
            out_rows,
            out_rows,
            out_mem_rows,
            out_mem_rows,
            pl.BlockSpec((3 * width, 128), lambda p, *_: (0, first + p)),
            pl.BlockSpec((1, 8, basis), lambda p, *_: (first + p, 0, 0)),
            pl.BlockSpec((1, 16, 128), lambda p, *_: (first + p, 0, 0)),
        ],
        [shape_of((length, half), BF16)] * 3
        + [shape_of((basis, half), BF16)] * 2
        + [
            shape_of((3 * width, half), BF16),
            shape_of((side_pairs, 8, basis), F32),
            shape_of((side_pairs, 16, 128), F32),
        ],
        pairs * (28 * length * length * 128 + 6 * length * width * 128),
        "attend_back",
        operands + earlier,
        scalars=(scalars, flags),
        aliases={2 + len(operands) + index: index for index in range(len(earlier))},
    )


def feed_step(normed, normed_t, out_grad, up, up_bias, down, d_up, d_up_bias, d_down):
    weight_up = up[...]
    weight_down = down[...]
    before = dot_nn(normed[...], weight_up) + up_bias[...]
    out_rows = out_grad[...]
    hidden_grad = dot_nt(out_rows, weight_down)
    root = math.sqrt(2.0 / math.pi)
    square = before * before
    angle = jnp.tanh(before * (root + (root * 0.044715) * square))
    half_sum = 0.5 + 0.5 * angle
    activated = (before * half_sum).astype(BF16)
    slope = half_sum + before * (0.5 - 0.5 * angle * angle) * (
        root + (3.0 * 0.044715 * root) * square
    )
    before_grad = (hidden_grad * slope).astype(BF16)
    d_down[...] = dot_tn(activated, out_rows).astype(BF16)
    d_up[...] = dot_nn(normed_t[...], before_grad).astype(BF16)
    d_up_bias[...] = dot_nn(jnp.ones((8, before.shape[0]), BF16), before_grad)
    return dot_nn(activated, weight_down), dot_nt(before_grad, weight_up)


def residual_step(rows, mix, hid, wo, vectors, middle, normed, normed_t):
    branch = dot_nn(mix[rows, :], wo)
    values = hid[rows, :].astype(F32) + (branch + vectors[2:3])
    middle[rows, :] = values
    scaled, _ = scaled_rows(values)
    result = (scaled * vectors[3:4] + vectors[4:5]).astype(BF16)
    normed[rows, :] = result
    normed_t[:, rows] = result.T


def branch_step(rows, grad_sum, out_grad, middle, mix_t, wo, vectors, mid_grad, mix_grad):
    scaled, inverse = scaled_rows(middle[rows, :])
    grad_rows = grad_sum[rows, :]
    out_rows = out_grad[rows, :].astype(F32)
    result = out_rows + norm_back(grad_rows, scaled, inverse, vectors[3:4])
    mid_grad[rows, :] = result
    branch = result.astype(BF16)
    mix_grad[rows, :] = dot_nt(branch, wo).astype(BF16)
    sums = jnp.concatenate(
        [
            jnp.sum(branch.astype(F32), axis=0, keepdims=True),
            jnp.sum(grad_rows * scaled, axis=0, keepdims=True),
            jnp.sum(grad_rows, axis=0, keepdims=True),
            jnp.sum(out_rows, axis=0, keepdims=True),
            jnp.zeros((4, grad_rows.shape[1]), F32),
        ],
        axis=0,
    )
    return dot_nn(mix_t[:, rows], branch), sums


def feed_kernel(
    steps, scalars, mix, hid, mix_t, w_own, w_far, out_mine, out_theirs, vectors, up_far, up_own, ub_far,
    ub_own, down_far, down_own, du_far, du_own, dub_far, dub_own, dd_far, dd_own, mine, theirs, mid_grad,
    mix_grad, dw_own, dw_far, sums, middle, normed, normed_t, out_grad, out_sum, grad_sum, up, ub, down,
    du, dub, dd,
):
    index = pl.program_id(0)
    step = index - 1
    me = scalars[0]
    length = mix.shape[0]
    tokens = theirs.shape[0]
    spans = [slice(start, start + tokens) for start in range(0, length, tokens)]

    def half_at(half):
        return pl.ds(pl.multiple_of(half * tokens, tokens), tokens)

    @pl.when(index == 0)
    def _():
        out_sum[...] = jnp.zeros_like(out_sum)
        grad_sum[...] = jnp.zeros_like(grad_sum)
        out_grad[half_at(me), :] = out_mine[0]
        out_grad[half_at(1 - me), :] = out_theirs[...]
        wo = jnp.concatenate([w_own[...], w_far[...]], axis=0)
        for rows in spans:
            residual_step(rows, mix, hid, wo, vectors, middle, normed, normed_t)

    @pl.when((step >= 0) & (step < 2 * steps))
    def _():
        for side, weights in ((0, (up_far, ub_far, down_far)), (1, (up_own, ub_own, down_own))):

            @pl.when((step >= steps) == (side == 1))
            def _():
                for held, source in zip((up, ub, down), weights):
                    held[...] = source[...]

        forward, backward = feed_step(normed, normed_t, out_grad, up, ub, down, du, dub, dd)
        out_sum[...] += forward
        grad_sum[...] += backward
        for side, grads in ((0, (du_far, dub_far, dd_far)), (1, (du_own, dub_own, dd_own))):

            @pl.when((step >= steps) == (side == 1))
            def _():
                for target, held in zip(grads, (du, dub, dd)):
                    target[...] = held[...]

    @pl.when(step == 2 * steps)
    def _():
        for target, half in ((mine.at[0], me), (theirs, 1 - me)):
            at = half_at(half)
            target[...] = (middle[at, :] + out_sum[at, :] + vectors[5:6]).astype(BF16)
        wo = jnp.concatenate([w_own[...], w_far[...]], axis=0)
        total = None
        for rows in spans:
            fresh, added_sums = branch_step(
                rows, grad_sum, out_grad, middle, mix_t, wo, vectors, mid_grad, mix_grad
            )
            total = fresh if total is None else total + fresh
            sums[...] = added_sums if rows.start == 0 else sums[...] + added_sums
        half = w_own.shape[0]
        for side, out in enumerate((dw_own, dw_far)):
            rows = slice(side * half, (side + 1) * half)
            out[:half] = total[rows, :half].astype(BF16)
            out[half:] = total[rows, half:].astype(BF16)


def feed(order, scalars, mix, hid, mix_t, w_own, w_far, out_grad, out_grad_come, vectors, up_far, up_own, ub_far, ub_own, down_far, down_own):
    length, width = hid.shape
    tokens = length // 2
    hidden = up_own.shape[1]
    steps = hidden // FEED_BLOCK

    def far_block(i):
        return jnp.clip(i - 1, 0, steps - 1)

    def own_block(i):
        return jnp.clip(i - 1 - steps, 0, steps - 1)

    def up_spec(block):
        return pl.BlockSpec((width, FEED_BLOCK), lambda i, s: (0, block(i)))

    def bias_spec(block, rows):
        return pl.BlockSpec((rows, FEED_BLOCK), lambda i, s: (0, block(i)))

    def down_spec(block):
        return pl.BlockSpec((FEED_BLOCK, width), lambda i, s: (block(i), 0))

    def once(shape, place=None):
        zeros = (0,) * len(shape)
        return pl.BlockSpec(
            shape, place or (lambda i, s: zeros), pipeline_mode=pl.Buffered(1)
        )

    def mine_at(i, s):
        return (s[0], 0, 0)

    return order.call(
        functools.partial(feed_kernel, steps),
        (2 * steps + 2,),
        [
            once((length, width)),
            once((length, width)),
            once((width, length)),
            once(w_own.shape),
            once(w_far.shape),
            once((1, tokens, width), mine_at),
            once((tokens, width)),
            once(vectors.shape),
            up_spec(far_block),
            up_spec(own_block),
            bias_spec(far_block, 1),
            bias_spec(own_block, 1),
            down_spec(far_block),
            down_spec(own_block),
        ],
        [
            up_spec(far_block),
            up_spec(own_block),
            bias_spec(far_block, 8),
            bias_spec(own_block, 8),
            down_spec(far_block),
            down_spec(own_block),
            pl.BlockSpec((1, tokens, width), mine_at),
            whole((tokens, width)),
            whole((length, width)),
            whole((length, width)),
            whole((width, width // 2)),
            whole((width, width // 2)),
            whole((8, width)),
        ],
        [
            shape_of((width, hidden), BF16),
            shape_of((width, hidden), BF16),
            shape_of((8, hidden), F32),
            shape_of((8, hidden), F32),
            shape_of((hidden, width), BF16),
            shape_of((hidden, width), BF16),
            shape_of((2, tokens, width), BF16),
            shape_of((tokens, width), BF16),
            shape_of((length, width), F32),
            shape_of((length, width), BF16),
            shape_of((width, width // 2), BF16),
            shape_of((width, width // 2), BF16),
            shape_of((8, width), F32),
        ],
        24 * length * width * hidden,
        "feed",
        (mix, hid, mix_t, w_own, w_far, out_grad, out_grad_come, vectors)
        + (up_far, up_own, ub_far, ub_own, down_far, down_own),
        scratch=[
            pltpu.VMEM((length, width), F32),
            pltpu.VMEM((length, width), BF16),
            pltpu.VMEM((width, length), BF16),
            pltpu.VMEM((length, width), BF16),
            pltpu.VMEM((length, width), F32),
            pltpu.VMEM((length, width), F32),
            pltpu.VMEM((width, FEED_BLOCK), BF16),
            pltpu.VMEM((1, FEED_BLOCK), F32),
            pltpu.VMEM((FEED_BLOCK, width), BF16),
            pltpu.VMEM((width, FEED_BLOCK), BF16),
            pltpu.VMEM((8, FEED_BLOCK), F32),
            pltpu.VMEM((FEED_BLOCK, width), BF16),
        ],
        scalars=(scalars,),
    )


def input_back_kernel(
    scalars, hid, mid_grad, vectors, w_own, w_far, dq_own, dk_own, dv_own, dq_far, dk_far, dv_far,
    dmk_own, dmv_own, dmk_far, dmv_far, mine, theirs, coeff_mine, coeff_theirs, sums, total,
):
    me = scalars[0]
    index = pl.program_id(0)

    def back(own, far, part):
        return dot_nt(
            jnp.concatenate([own[...], far[...]], axis=1),
            jnp.concatenate([w_own[part], w_far[part]], axis=1),
        )

    grad_rows = back(dq_own, dq_far, 0) + back(dk_own, dk_far, 1) + back(dv_own, dv_far, 2)
    scaled, inverse = scaled_rows(hid[...].astype(F32))
    result = mid_grad[...] + norm_back(grad_rows, scaled, inverse, vectors[0:1])

    @pl.when(index == me)
    def _():
        mine[0] = result

    @pl.when(index != me)
    def _():
        theirs[...] = result.astype(BF16)

    fresh = jnp.concatenate(
        [
            jnp.sum(grad_rows * scaled, axis=0, keepdims=True),
            jnp.sum(grad_rows, axis=0, keepdims=True),
            jnp.zeros((6, grad_rows.shape[1]), F32),
        ],
        axis=0,
    )

    @pl.when(index == 0)
    def _():
        sums[...] = fresh
        total[...] = back(dmk_own, dmk_far, 1) + back(dmv_own, dmv_far, 2)
        part = coeff_theirs.shape[0]
        coeff_mine[0] = total[pl.ds(pl.multiple_of(me * part, part), part), :]
        coeff_theirs[...] = total[
            pl.ds(pl.multiple_of((1 - me) * part, part), part), :
        ].astype(BF16)

    @pl.when(index > 0)
    def _():
        sums[...] += fresh


def input_back(order, scalars, hid, mid_grad, vectors, w_own, w_far, own, far):
    length, width = hid.shape
    tokens = length // 2
    basis, half = own[3].shape
    rows = pl.BlockSpec((tokens, width), lambda i, s: (i, 0))
    half_rows = pl.BlockSpec((tokens, half), lambda i, s: (i, 0))
    return order.call(
        input_back_kernel,
        (2,),
        [rows, rows, whole(vectors.shape), whole(w_own.shape), whole(w_far.shape)]
        + [half_rows] * 6
        + [whole((basis, half))] * 4,
        [
            pl.BlockSpec((1, tokens, width), lambda i, s: (s[0], 0, 0)),
            whole((tokens, width)),
            pl.BlockSpec((1, basis // 2, width), lambda i, s: (s[0], 0, 0)),
            whole((basis // 2, width)),
            whole((8, width)),
        ],
        [
            shape_of((2, tokens, width), F32),
            shape_of((tokens, width), BF16),
            shape_of((2, basis // 2, width), F32),
            shape_of((basis // 2, width), BF16),
            shape_of((8, width), F32),
        ],
        6 * length * width * width,
        "input_back",
        (hid, mid_grad, vectors, w_own, w_far, *own[:3], *far[:3], *own[3:5], *far[3:5]),
        scratch=[pltpu.VMEM((basis, width), F32)],
        scalars=(scalars,),
    )


def tokens_place_kernel(scalars, *refs):
    for come, out in zip(refs[:3], refs[6:]):
        out[0] = come[...].astype(out.dtype)


def tokens_place(order, scalars, filled, come):
    return order.call(
        tokens_place_kernel,
        (1,),
        [whole(c.shape) for c in come] + [pl.BlockSpec(memory_space=pl.ANY)] * 3,
        [pl.BlockSpec((1,) + f.shape[1:], lambda i, s: (1 - s[0], 0, 0)) for f in filled],
        [shape_of(f.shape, f.dtype) for f in filled],
        0,
        "tokens_place",
        tuple(come) + tuple(filled),
        scalars=(scalars,),
        aliases={4 + index: index for index in range(3)},
    )


def pack_kernel(own_maps, own_sums, own_bias, far_maps, far_sums, far_bias, mid_sums, first_sums, own, far):
    for maps, sums, bias, out in (
        (own_maps, own_sums, own_bias, own),
        (far_maps, far_sums, far_bias, far),
    ):
        row = 0

        def put(values):
            nonlocal row
            for start in range(0, values.shape[1], 128):
                out[row : row + 1] = values[:, start : start + 128]
                row += 1

        for pair in range(maps.shape[0]):
            for index in range(4):
                put(maps[pair, index : index + 1])
        for index in (8, 9):
            for pair in range(maps.shape[0]):
                put(sums[pair, index : index + 1])
        put(bias[0:1])
        for index in range(4):
            put(mid_sums[index : index + 1])
        for index in range(2):
            put(first_sums[index : index + 1])
        for pair in range(maps.shape[0]):
            for index in range(4):
                put(sums[pair, index : index + 1])
        out[row:] = jnp.zeros((out.shape[0] - row, 128), F32)


def pack(order, own, own_bias, far, far_bias, mid_sums, first_sums):
    operands = (own[6], own[7], own_bias, far[6], far[7], far_bias, mid_sums, first_sums)
    pairs, _, basis = own[6].shape
    width = mid_sums.shape[1]
    count = pairs * 4 * (basis // 128) + 6 * pairs + own_bias.shape[1] // 128 + 6 * width // 128
    count += -count % 8
    return order.call(
        pack_kernel,
        (1,),
        [whole(o.shape) for o in operands],
        [whole((count, 128))] * 2,
        [shape_of((count, 128), F32)] * 2,
        0,
        "pack",
        operands,
    )


def to_peer(values):
    return jax.tree.map(lambda v: lax.ppermute(v, "mp", [(0, 1), (1, 0)]), values)


def across(values, offset, count):
    return lax.ppermute(values, "batch", [(i, i ^ offset) for i in range(count)])


def added(left, right):
    return left + right


def halve_kernel(flip, scalars, *refs):
    for chunk in range(2):
        low, high, low_more, high_more = refs[4 * chunk : 4 * chunk + 4]
        keep, send = refs[8 + 2 * chunk : 10 + 2 * chunk]
        bit = scalars[1 + (chunk ^ flip)]

        @pl.when(bit == 0)
        def _():
            keep[...] = added(low[...], low_more[...])
            send[...] = added(high[...], high_more[...])

        @pl.when(bit != 0)
        def _():
            keep[...] = added(high[...], high_more[...])
            send[...] = added(low[...], low_more[...])


def share_kernel(group, scalars, keep_a, more_a, keep_b, more_b, *outs):
    rows_a = keep_a.shape[0] // group
    rows_b = keep_b.shape[0] // group
    width = keep_b.shape[1]
    for offset in range(group):
        place = scalars[3 + offset]
        at = pl.ds(pl.multiple_of(place * rows_a, rows_a), rows_a)
        share = added(keep_a[at, :], more_a[at, :])
        for part in range(keep_a.shape[1] // width):
            outs[offset][part * rows_a : (part + 1) * rows_a] = share[
                :, part * width : (part + 1) * width
            ]
        at = pl.ds(pl.multiple_of(place * rows_b, rows_b), rows_b)
        outs[offset][outs[offset].shape[0] - rows_b :] = added(keep_b[at, :], more_b[at, :])


def total_kernel(*refs):
    total = refs[0][...].astype(F32)
    for ref in refs[1:-1]:
        total += ref[...].astype(F32)
    refs[-1][...] = total.astype(BF16)


def spread_kernel(group, scalars, *refs):
    out = refs[group]
    rows = out.shape[0] // group
    for offset in range(group):
        at = pl.ds(pl.multiple_of(scalars[3 + offset] * rows, rows), rows)
        out[at, :] = refs[offset][...]


def small_kernel(left, right, out):
    out[...] = left[...] + right[...]


def small_add(order, left, right):
    return order.call(
        small_kernel,
        (1,),
        [whole(left.shape)] * 2,
        [whole(left.shape)],
        [shape_of(left.shape, F32)],
        0,
        "small_add",
        (left, right),
    )[0]


class BatchSum:
    def __init__(self, order, scalars, count):
        self.order = order
        self.scalars = scalars
        self.count = count
        self.group = min(4, count // 4)

    def halve(self, flip, quads):
        specs = []
        operands = []
        out_specs = []
        shapes = []
        for shape, quad in quads:
            cuts = self.cuts(shape[0])
            piece = (shape[0] // cuts, shape[1])
            for values, block in quad:
                specs.append(
                    pl.BlockSpec(
                        piece, lambda i, s, block=block, cuts=cuts: (block[0] * cuts + i, block[1])
                    )
                )
                operands.append(values)
            out_specs += [pl.BlockSpec(piece, lambda i, s: (i, 0))] * 2
            shapes += [shape, shape]
        keep_a, send_a, keep_b, send_b = self.order.call(
            functools.partial(halve_kernel, flip),
            (cuts,),
            specs,
            out_specs,
            [shape_of(s, BF16) for s in shapes],
            0,
            "halve",
            operands,
            scalars=(self.scalars,),
        )
        self.kept = (keep_a, keep_b)
        self.come = (
            across(send_a, 1 << flip, self.count),
            across(send_b, 2 >> flip, self.count),
        )

    def cuts(self, rows):
        return 4 if rows % 64 == 0 else 1

    def first(self, quads):
        self.halve(0, quads)

    def second(self):
        quads = []
        for kept, come in zip(self.kept, self.come):
            shape = (kept.shape[0] // 2, kept.shape[1])
            quads.append((shape, ((kept, (0, 0)), (kept, (1, 0)), (come, (0, 0)), (come, (1, 0)))))
        self.halve(1, quads)

    def around(self, own):
        return [own[0]] + [
            across(own[offset], offset << 2, self.count) for offset in range(1, self.group)
        ]

    def share(self):
        operands = (self.kept[0], self.come[0], self.kept[1], self.come[1])
        width = operands[2].shape[1]
        shape = ((operands[0].size + operands[2].size) // (width * self.group), width)
        self.shares = self.around(
            self.order.call(
                functools.partial(share_kernel, self.group),
                (1,),
                [whole(o.shape) for o in operands],
                [whole(shape)] * self.group,
                [shape_of(shape, BF16)] * self.group,
                0,
                "share",
                operands,
                scalars=(self.scalars,),
            )
        )

    def total(self):
        shape = self.shares[0].shape
        (self.mine,) = self.order.call(
            total_kernel,
            (1,),
            [whole(shape)] * self.group,
            [whole(shape)],
            [shape_of(shape, BF16)],
            0,
            "total",
            self.shares,
        )
        offset = 4 * self.group
        while offset < self.count:
            self.mine = added(self.mine, across(self.mine, offset, self.count))
            offset *= 2

    def around_rest(self):
        self.pieces = self.around([self.mine] * self.group)

    def spread(self):
        rows, width = self.mine.shape
        shape = (self.group * rows, width)
        (quarter,) = self.order.call(
            functools.partial(spread_kernel, self.group),
            (1,),
            [whole(p.shape) for p in self.pieces],
            [whole(shape)],
            [shape_of(shape, BF16)],
            0,
            "spread",
            self.pieces,
            scalars=(self.scalars,),
        )
        self.quarters = [quarter] + [
            across(quarter, offset, self.count) for offset in (1, 2, 3)
        ]


def peers_added_kernel(*refs):
    for index in range(2):
        refs[4 + index][...] = added(refs[2 * index][...], refs[2 * index + 1][...])
    refs[6][...] = jnp.zeros_like(refs[6])


def peers_added(order, up_pair, down_pair):
    cuts = 4
    width = down_pair[0].shape[1]
    up_spec = pl.BlockSpec((up_pair[0].shape[0] // cuts, width), lambda i: (i, 1))
    up_out = pl.BlockSpec((up_pair[0].shape[0] // cuts, width), lambda i: (i, 0))
    down_spec = pl.BlockSpec((down_pair[0].shape[0] // cuts, width), lambda i: (i, 0))
    return order.call(
        peers_added_kernel,
        (cuts,),
        [up_spec, up_spec, down_spec, down_spec],
        [up_out, down_spec, whole((8, 128))],
        [
            shape_of((up_pair[0].shape[0], width), BF16),
            shape_of(down_pair[0].shape, BF16),
            shape_of((8, 128), F32),
        ],
        0,
        "peers_added",
        tuple(up_pair) + tuple(down_pair),
    )[:2]


def feed_place_kernel(up_sum, down_sum, _, up_out, down_out):
    up_out[...] = up_sum[...].astype(F32)
    down_out[...] = down_sum[...].astype(F32)


def feed_place(order, up_sum, down_sum, up_grad):
    cuts = 4
    width = down_sum.shape[1]
    up_rows = up_sum.shape[0] // cuts
    down_rows = down_sum.shape[0] // cuts
    return order.call(
        feed_place_kernel,
        (cuts,),
        [
            pl.BlockSpec((up_rows, width), lambda i: (i, 0)),
            pl.BlockSpec((down_rows, width), lambda i: (i, 0)),
            pl.BlockSpec(memory_space=pl.ANY),
        ],
        [
            pl.BlockSpec((up_rows, width), lambda i: (i, 1)),
            pl.BlockSpec((down_rows, width), lambda i: (i, 0)),
        ],
        [shape_of(up_grad.shape, F32), shape_of(down_sum.shape, F32)],
        0,
        "feed_place",
        (up_sum, down_sum, up_grad),
        aliases={2: 0},
    )


def mixed_halve_kernel(scalars, *refs):
    for chunk in range(2):
        keep, send = refs[16 + 2 * chunk : 18 + 2 * chunk]
        bit = scalars[1 + chunk]

        def fill(target, half):
            own, own_more, peer, peer_more = refs[8 * chunk + 4 * half : 8 * chunk + 4 * half + 4]
            rows = own.shape[0]
            target[:rows] = added(own[...], peer[...])
            target[rows:] = added(own_more[...], peer_more[...])

        @pl.when(bit == 0)
        def _():
            fill(keep, 0)
            fill(send, 1)

        @pl.when(bit != 0)
        def _():
            fill(keep, 1)
            fill(send, 0)


class MixedSum(BatchSum):
    def first(self, dqkv, dwo, du):
        width, cols = dwo[0].shape
        part = width // 2
        steps = cols // 128
        specs = []
        operands = []
        for chunk in range(2):
            for half in range(2):
                main = dwo if (chunk, half) == (1, 1) else dqkv
                block = 0 if main is dwo else 2 * chunk + half
                for side in range(2):
                    specs.append(pl.BlockSpec((width, 128), lambda i, s, b=block: (b, i)))
                    specs.append(
                        pl.BlockSpec((part, 128), lambda i, s, h=half, c=chunk: (h, steps * c + i))
                    )
                    operands += [main[side], du[side]]
        shape = (width + part, cols)
        keep_a, send_a, keep_b, send_b = self.order.call(
            mixed_halve_kernel,
            (steps,),
            specs,
            [pl.BlockSpec((width + part, 128), lambda i, s: (0, i))] * 4,
            [shape_of(shape, BF16)] * 4,
            0,
            "mixed_halve",
            operands,
            scalars=(self.scalars,),
        )
        self.kept = (keep_a, keep_b)
        self.come = (across(send_a, 1, self.count), across(send_b, 2, self.count))


def mixed_place_kernel(group, scalars, *refs):
    qkv_out, up_out, wo_out = refs[-3:]
    cols = refs[0].shape[1]
    width = wo_out.shape[1]
    part = width // 2
    rows = refs[0].shape[0] // (2 * group)

    def segments(quarter, place):
        start = (quarter * group + place) * rows
        marks = [start] + [m for m in (part, width) if start < m < start + rows] + [start + rows]
        return [(a, a - start, b - a) for a, b in zip(marks, marks[1:])]

    for index in range(4):
        column = scalars[1] ^ (index % 2)
        row = scalars[2] ^ (index // 2)
        values = refs[index]
        for quarter in range(2):

            @pl.when(row == quarter)
            def _():
                for place in range(group):
                    for at, inner, size in segments(quarter, place):
                        start = 2 * place * rows + inner
                        piece = values[start : start + size].astype(F32)
                        if at < width:
                            to = pl.multiple_of(column * width + at, 16)
                            qkv_out[pl.ds(to, size), :] = piece
                        else:
                            to = pl.multiple_of(column * part + at - width, 16)
                            up_out[pl.ds(to, size), :cols] = piece

            for half in range(2):

                @pl.when((column == quarter) & (row == half))
                def _():
                    for place in range(group):
                        for at, inner, size in segments(quarter, place):
                            start = (2 * place + 1) * rows + inner
                            piece = values[start : start + size].astype(F32)
                            if at >= width:
                                to = half * part + at - width
                                up_out[to : to + size, cols:] = piece
                            elif half == 0:
                                qkv_out[2 * width + at : 2 * width + at + size] = piece
                            elif at < part:
                                wo_out[at : at + size, :cols] = piece
                            else:
                                wo_out[at - part : at - part + size, cols:] = piece


def mixed_place(order, scalars, summed, width, hidden):
    half = width // 2
    return order.call(
        functools.partial(mixed_place_kernel, summed.group),
        (1,),
        [whole(o.shape) for o in summed.quarters],
        [
            whole((3 * width, half)),
            pl.BlockSpec((width, width), lambda i, s: (0, 0)),
            whole((half, width)),
        ],
        [
            shape_of((3 * width, half), F32),
            shape_of((width, hidden), F32),
            shape_of((half, width), F32),
        ],
        0,
        "mixed_place",
        summed.quarters,
        scalars=(scalars,),
    )


def per_device(
    count,
    hidden_in,
    memory_flags,
    memory_coeffs,
    first_gain,
    first_bias,
    query_key_value_matrix,
    qv_bias,
    memory_weight,
    memory_bias,
    output_matrix,
    out_bias,
    second_gain,
    second_bias,
    up_matrix,
    up_bias_vector,
    down_matrix,
    down_bias,
    out_grad,
):
    me = lax.axis_index("mp")
    position = lax.axis_index("batch")
    width = hidden_in.shape[2]
    half = width // 2
    group = min(4, count // 4)
    place = (position >> 2) % group
    scalars = jnp.stack(
        [me, position & 1, (position >> 1) & 1] + [place ^ offset for offset in range(group)]
    ).astype(jnp.int32)

    def from_peer(values):
        return to_peer(lax.dynamic_index_in_dim(values, 1 - me, 0, keepdims=False))

    hidden_come = from_peer(hidden_in)
    w_own = jnp.transpose(query_key_value_matrix, (1, 0, 2))
    w_far = to_peer(w_own)
    coeffs_come = from_peer(memory_coeffs)
    qv_far, mw_far, mb_far, ub_far = to_peer(
        (qv_bias, memory_weight, memory_bias, up_bias_vector)
    )

    query_bias = jnp.concatenate([qv_bias, qv_far], axis=1).astype(F32)
    mem_maps = jnp.concatenate([memory_weight, mw_far], axis=1).astype(F32)
    mem_maps = jnp.transpose(mem_maps, (1, 0, 2))
    mem_biases = jnp.concatenate([memory_bias, mb_far], axis=1).astype(F32)
    vectors = jnp.stack(
        [first_gain, first_bias, out_bias, second_gain, second_bias, down_bias] + [down_bias] * 2
    )
    order = Order()
    hid, norm_t, q, k, v, mem_k, mem_v, coeffs_t = project(
        order, scalars, hidden_in, hidden_come, vectors, w_own, w_far, query_bias, memory_coeffs, coeffs_come
    )
    later, _ = lax.optimization_barrier(
        ((output_matrix, out_grad, up_matrix, down_matrix), (coeffs_t, mw_far, mb_far, ub_far))
    )
    wo_far = to_peer(later[0])
    out_grad_come = from_peer(later[1])
    up_far = to_peer(later[2])
    down_far = to_peer(later[3])
    att_t, mix_t, mix, stat = attend(
        order, scalars, memory_flags, q, k, v, mem_k, mem_v, mem_maps, mem_biases
    )
    (
        du_far,
        du_own,
        dub_far,
        dub_own,
        dd_far,
        dd_own,
        block_mine,
        block_theirs,
        mid_grad,
        mix_grad,
        dwo_own,
        dwo_far,
        mid_sums,
    ) = feed(
        order,
        scalars,
        mix,
        hid,
        mix_t,
        output_matrix,
        wo_far,
        out_grad,
        out_grad_come,
        vectors,
        up_far,
        up_matrix,
        ub_far.astype(F32)[None],
        up_bias_vector.astype(F32)[None],
        down_far,
        down_matrix,
    )
    du_peer, dd_peer = to_peer((du_far, dd_far))
    dwo_peer = to_peer(dwo_far)
    back_args = (
        scalars, memory_flags, q, k, v, mem_k, mem_v, mem_maps, mix_grad, att_t, stat, norm_t, coeffs_t
    )
    pairs = width // 256
    far = attend_back(order, 1, 0, pairs, None, *back_args)
    up_sum, down_sum = peers_added(order, (du_own, du_peer), (dd_own, dd_peer))
    dqkv_peer = to_peer(far[5])
    up_sum, down_sum = lax.psum((up_sum, down_sum), "batch")
    block_come = to_peer(block_theirs)
    own = attend_back(order, 0, 0, pairs, None, *back_args)
    dqkv_own = own[5]
    last = MixedSum(order, scalars, count)
    last.first((dqkv_own, dqkv_peer), (dwo_own, dwo_peer), (du_own, du_peer))
    in_mine, in_theirs, coeff_mine, coeff_theirs, first_sums = input_back(
        order, scalars, hid, mid_grad, vectors, w_own, w_far, own, far
    )
    small, far_flat = pack(order, own, dub_own, far, dub_far, mid_sums, first_sums)
    last.second()
    come, in_come, coeff_come = to_peer(
        lax.optimization_barrier((far_flat, in_theirs, coeff_theirs, last.kept[0]))[:3]
    )
    block_out, input_grad, coeff_grad = tokens_place(
        order, scalars, (block_mine, in_mine, coeff_mine), (block_come, in_come, coeff_come)
    )
    last.share()
    small = small_add(order, small, come)
    small = small_add(order, small, across(small, 1, count))
    last.total()
    last.around_rest()
    small = small_add(order, small, across(small, 2, count))
    last.spread()
    offset = 4
    while offset < count:
        small = small_add(order, small, across(small, offset, count))
        offset *= 2
    query_key_value_grad, up_weight_grad, output_matrix_grad = mixed_place(
        order, scalars, last, width, up_matrix.shape[1]
    )
    query_key_value_grad = jnp.transpose(
        query_key_value_grad.reshape(3, width, half), (1, 0, 2)
    )
    up_weight_grad, down_weight_grad = feed_place(order, up_sum, down_sum, up_weight_grad)

    heads, basis = memory_weight.shape[1:]
    rows = 0

    def take(size):
        nonlocal rows
        piece = small[rows : rows + size // 128]
        rows += size // 128
        return piece

    memory_weight_grad = jnp.transpose(take(2 * heads * basis).reshape(heads, 2, basis), (1, 0, 2))
    qv_bias_grad = take(2 * half).reshape(2, half)
    up_bias_grad = take(up_bias_vector.shape[0]).reshape(-1)
    vector_grads = [take(width).reshape(-1) for _ in range(6)]
    memory_bias_grad = jnp.transpose(take(2 * heads * 128)[:, 0].reshape(heads, 2), (1, 0))
    return (
        block_out,
        input_grad,
        coeff_grad,
        vector_grads[4],
        vector_grads[5],
        query_key_value_grad,
        qv_bias_grad,
        memory_weight_grad,
        memory_bias_grad,
        output_matrix_grad,
        vector_grads[0],
        vector_grads[1],
        vector_grads[2],
        up_weight_grad,
        up_bias_grad,
        down_weight_grad,
        vector_grads[3],
    )


def solution(mesh):
    tokens = P("batch", "mp", None)
    return jax.shard_map(
        functools.partial(per_device, mesh.shape["batch"]),
        mesh=mesh,
        in_specs=(
            tokens,
            P("batch"),
            tokens,
            P(),
            P(),
            P(None, None, "mp"),
            P(None, "mp"),
            P(None, "mp", None),
            P(None, "mp"),
            P("mp", None),
            P(),
            P(),
            P(),
            P(None, "mp"),
            P("mp"),
            P("mp", None),
            P(),
            tokens,
        ),
        out_specs=(
            tokens,
            tokens,
            tokens,
            P(),
            P(),
            P(None, None, "mp"),
            P(None, "mp"),
            P(None, "mp", None),
            P(None, "mp"),
            P("mp", None),
            P(),
            P(),
            P(),
            P(None, "mp"),
            P("mp"),
            P("mp", None),
            P(),
        ),
        check_vma=False,
    )
```

```python
import functools
import math

import jax
import jax.numpy as jnp
from jax import lax
from jax.experimental import pallas as pl
from jax.experimental.pallas import tpu as pltpu
from jax.sharding import PartitionSpec as P

HD = 64
BLOCK = 256
FEED_BLOCK = 512
BF16 = jnp.bfloat16
F32 = jnp.float32
VMEM_BYTES = 56 * 2**20


def dot_nn(left, right):
    return lax.dot_general(left, right, (((1,), (0,)), ((), ())), preferred_element_type=F32)


def dot_nt(left, right):
    return lax.dot_general(left, right, (((1,), (1,)), ((), ())), preferred_element_type=F32)


def dot_tn(left, right):
    return lax.dot_general(left, right, (((0,), (0,)), ((), ())), preferred_element_type=F32)


def dot_tn_exact(left, right):
    return lax.dot_general(
        left,
        right,
        (((0,), (0,)), ((), ())),
        precision=lax.Precision.HIGHEST,
        preferred_element_type=F32,
    )


def three_parts(values):
    high = values.astype(BF16).astype(F32)
    rest = values - high
    middle = rest.astype(BF16).astype(F32)
    return jnp.concatenate([high, middle, rest - middle], axis=0).astype(BF16)


def add_parts(stacked):
    rows = stacked.shape[0] // 3
    return stacked[:rows] + stacked[rows : 2 * rows] + stacked[2 * rows :]


def scaled_rows(values):
    row_mean = jnp.mean(values, axis=-1, keepdims=True)
    centred = values - row_mean
    row_var = jnp.mean(centred * centred, axis=-1, keepdims=True)
    inverse = lax.rsqrt(row_var + 1e-05)
    return centred * inverse, inverse


def norm_back(grad_out, scaled, inverse, gain_vec):
    grad_scaled = grad_out * gain_vec
    first_mean = jnp.mean(grad_scaled, axis=-1, keepdims=True)
    second_mean = jnp.mean(grad_scaled * scaled, axis=-1, keepdims=True)
    return inverse * (grad_scaled - first_mean - scaled * second_mean)


def whole(shape):
    return pl.BlockSpec(shape, lambda *_: (0,) * len(shape))


class Order:
    def __init__(self):
        self.token = None

    def call(
        self, kernel, grid, in_specs, out_specs, out_shape, flops, name, operands, scratch=(), scalars=(),
        aliases=None,
    ):
        count = len(operands)
        prefetched = len(scalars)
        token = () if self.token is None else (self.token,)

        def body(*refs):
            kernel(*refs[: prefetched + count], *refs[prefetched + count + len(token) :])

        bytes_accessed = sum(math.prod(s.shape) * jnp.dtype(s.dtype).itemsize for s in out_shape)
        results = pl.pallas_call(
            body,
            grid_spec=pltpu.PrefetchScalarGridSpec(
                num_scalar_prefetch=prefetched,
                grid=grid,
                in_specs=list(in_specs) + [pl.BlockSpec(memory_space=pl.ANY)] * len(token),
                out_specs=list(out_specs),
                scratch_shapes=list(scratch),
            ),
            out_shape=out_shape,
            input_output_aliases=aliases or {},
            compiler_params=pltpu.CompilerParams(
                vmem_limit_bytes=VMEM_BYTES, dimension_semantics=("arbitrary",) * len(grid)
            ),
            cost_estimate=pl.CostEstimate(
                flops=int(flops), bytes_accessed=2 * bytes_accessed, transcendentals=0
            ),
            name=name,
        )(*scalars, *operands, *token)
        self.token = results[-1]
        return results


def shape_of(shape, dtype):
    return jax.ShapeDtypeStruct(shape, dtype)


def project_kernel(
    scalars, mine, theirs, vectors, w_own, w_far, qb, coeffs_mine, coeffs_theirs,
    hid, norm_t, q, k, v, mem_k, mem_v, coeffs_t,
):
    me = scalars[0]
    index = pl.program_id(0)

    @pl.when(index == me)
    def _():
        hid[...] = mine[0]

    @pl.when(index != me)
    def _():
        hid[...] = theirs[...]

    scaled, _ = scaled_rows(hid[...].astype(F32))
    normed = (scaled * vectors[0:1] + vectors[1:2]).astype(BF16)
    norm_t[...] = normed.T

    def weight(part):
        return jnp.concatenate([w_own[part], w_far[part]], axis=1)

    q[...] = (dot_nn(normed, weight(0)) + qb[0:1]).astype(BF16)
    k[...] = dot_nn(normed, weight(1)).astype(BF16)
    v[...] = (dot_nn(normed, weight(2)) + qb[1:2]).astype(BF16)

    @pl.when(index == 0)
    def _():
        first = coeffs_mine[0].astype(F32)
        second = coeffs_theirs[...].astype(F32)
        rows = jnp.concatenate(
            [jnp.where(me == 0, first, second), jnp.where(me == 0, second, first)], axis=0
        ).astype(BF16)
        coeffs_t[...] = rows.T
        mem_k[...] = dot_nn(rows, weight(1)).astype(BF16)
        mem_v[...] = dot_nn(rows, weight(2)).astype(BF16)


def project(order, scalars, hidden_in, hidden_come, vectors, w_own, w_far, qb, coeffs, coeffs_come):
    tokens, width = hidden_come.shape
    length = 2 * tokens
    part = coeffs_come.shape[0]
    basis = 2 * part
    rows = pl.BlockSpec((tokens, width), lambda i, s: (i, 0))
    return order.call(
        project_kernel,
        (2,),
        [
            pl.BlockSpec((1, tokens, width), lambda i, s: (s[0], 0, 0)),
            whole((tokens, width)),
            whole(vectors.shape),
            whole(w_own.shape),
            whole(w_far.shape),
            whole(qb.shape),
            pl.BlockSpec((1, part, width), lambda i, s: (s[0], 0, 0)),
            whole((part, width)),
        ],
        [
            rows,
            pl.BlockSpec((width, tokens), lambda i, s: (0, i)),
            rows,
            rows,
            rows,
            whole((basis, width)),
            whole((basis, width)),
            whole((width, basis)),
        ],
        [
            shape_of((length, width), BF16),
            shape_of((width, length), BF16),
            shape_of((length, width), BF16),
            shape_of((length, width), BF16),
            shape_of((length, width), BF16),
            shape_of((basis, width), BF16),
            shape_of((basis, width), BF16),
            shape_of((width, basis), BF16),
        ],
        2 * length * width * width * 3,
        "project",
        (hidden_in, hidden_come, vectors, w_own, w_far, qb, coeffs, coeffs_come),
        scalars=(scalars,),
    )


def head_rows(values_t, head):
    part = values_t[head * HD : (head + 1) * HD]
    zeros = jnp.zeros_like(part)
    return jnp.concatenate([part, zeros] if head == 0 else [zeros, part], axis=0)


def map_rows(mw, pair):
    return jnp.concatenate(
        [mw[2 * pair], mw[2 * pair + 1], jnp.zeros((4, mw.shape[2]), F32)], axis=0
    )


def pair_maps(rows, mem_k):
    maps = dot_nn(rows.astype(BF16), mem_k)
    row = lax.broadcasted_iota(jnp.int32, maps.shape, 0)
    lane = lax.broadcasted_iota(jnp.int32, maps.shape, 1)
    return jnp.where((row // 2) == (lane // HD), maps, 0.0)


def bias_rows(mb, pair):
    row = lax.broadcasted_iota(jnp.int32, (8, 1), 0)
    column = jnp.zeros((8, 1), F32)
    for head in range(2):
        for which in range(2):
            column = jnp.where(row == 2 * head + which, mb[which, 2 * pair + head], column)
    return column


def basis_of(logits, basis_count):
    centre = jax.nn.sigmoid(logits)
    softplus = jnp.maximum(logits, 0.0) + jnp.log(1.0 + jnp.exp(-jnp.abs(logits)))
    spread = 0.05 * softplus + (8.0 / basis_count) ** 2
    rate = -0.5 / spread
    level = lax.rsqrt(2.0 * math.pi * spread) / basis_count
    return centre, rate, level


def places_of(basis_count):
    steps = lax.broadcasted_iota(jnp.int32, (basis_count, BLOCK), 0).astype(F32)
    return (steps + 0.5) / basis_count


def attend_kernel(scalars, flags, q, k, v, mem_k, mem_v, mw, mb, att_t, mix_t, mix, stat):
    length = q.shape[0]
    basis = mem_k.shape[0]
    flag_value = flags[scalars[0]].astype(F32)
    q_t = (q[...].astype(F32) * 0.125).astype(BF16).T
    v_t = v[...].T
    mem_v_t = mem_v[...].T
    pair = pl.program_id(0)
    maps = pair_maps(map_rows(mw, pair), mem_k[...])
    logits = add_parts(dot_nn(three_parts(maps), q_t)) + bias_rows(mb, pair)
    centre, rate, level = basis_of(logits, basis)
    places = places_of(basis)
    allowed = lax.broadcasted_iota(jnp.int32, (BLOCK, BLOCK), 0) <= lax.broadcasted_iota(
        jnp.int32, (BLOCK, BLOCK), 1
    )
    stat[4:8, :] = logits[0:4]
    heads = []
    for head in range(2):
        rows = slice(head * HD, (head + 1) * HD)
        v_ones = jnp.concatenate([v_t[rows], jnp.ones((16, length), BF16)], axis=0)
        heads.append((rows, head_rows(q_t, head), v_ones))
    for index in range(length // BLOCK):
        start, stop = index * BLOCK, (index + 1) * BLOCK
        scores = []
        for rows, q_head, v_ones in heads:
            scores.append(dot_nn(k[:stop, :], q_head[:, start:stop]))
        for head, (rows, q_head, v_ones) in enumerate(heads):
            near = jnp.where(allowed, scores[head][start:], -1e30)
            top = jnp.max(near, axis=0, keepdims=True)
            if index:
                far = scores[head][:start]
                top = jnp.maximum(top, jnp.max(far, axis=0, keepdims=True))
                weights = jnp.concatenate([jnp.exp(far - top), jnp.exp(near - top)], axis=0)
            else:
                weights = jnp.exp(near - top)
            total = dot_nn(v_ones[:, :stop], weights.astype(BF16))
            denominator = total[HD : HD + 1]
            attended = total[:HD] / denominator
            att_t[rows, start:stop] = attended
            stat[head : head + 1, start:stop] = top + jnp.log(denominator)
            offset = places - centre[2 * head : 2 * head + 1, start:stop]
            mass = (
                jnp.exp(offset * offset * rate[2 * head + 1 : 2 * head + 2, start:stop])
                * level[2 * head + 1 : 2 * head + 2, start:stop]
            )
            recalled = dot_nn(mem_v_t[rows], mass.astype(BF16))
            mix_t[rows, start:stop] = (attended + flag_value * recalled).astype(BF16)
    mix[...] = mix_t[...].T


def attend(order, scalars, flags, q, k, v, mem_k, mem_v, mw, mb):
    length, width = q.shape
    basis = mem_k.shape[0]
    pairs = width // 128
    rows = pl.BlockSpec((length, 128), lambda p, *_: (0, p))
    mem_rows = pl.BlockSpec((basis, 128), lambda p, *_: (0, p))
    cols = pl.BlockSpec((128, length), lambda p, *_: (p, 0))
    return order.call(
        attend_kernel,
        (pairs,),
        [
            rows,
            rows,
            rows,
            mem_rows,
            mem_rows,
            whole(mw.shape),
            pl.BlockSpec(memory_space=pltpu.SMEM),
        ],
        [cols, cols, rows, pl.BlockSpec((8, length), lambda p, *_: (p, 0))],
        [
            shape_of((width, length), F32),
            shape_of((width, length), BF16),
            shape_of((length, width), BF16),
            shape_of((pairs * 8, length), F32),
        ],
        12 * length * length * width,
        "attend",
        (q, k, v, mem_k, mem_v, mw, mb),
        scalars=(scalars, flags),
    )


def attend_back_kernel(
    base, scalars, flags, q, k, v, mem_k, mem_v, mw, grad, att_t, stat, norm_t, coeffs_t, *refs
):
    dq, dk, dv, dmem_k, dmem_v, dqkv, dmw, sums = refs[-8:]
    length = q.shape[0]
    basis = mem_k.shape[0]
    flag_value = flags[scalars[0]].astype(F32)
    q_t = (q[...].astype(F32) * 0.125).astype(BF16).T
    k_t = k[...].T
    grad_t = grad[...].T
    lane = lax.broadcasted_iota(jnp.int32, (length, 128), 1)
    mem_rows = map_rows(mw, base + pl.program_id(0))
    maps = pair_maps(mem_rows, mem_k[...])
    logits = stat[4:8, :]
    logits = jnp.concatenate([logits, jnp.zeros_like(logits)], axis=0)
    centre, rate, level = basis_of(logits, basis)
    places = places_of(basis)
    allowed = lax.broadcasted_iota(jnp.int32, (BLOCK, BLOCK), 0) <= lax.broadcasted_iota(
        jnp.int32, (BLOCK, BLOCK), 1
    )
    q_lanes = []
    dk_lanes = []
    dv_lanes = []
    dmv_lanes = []
    mass_grads = []
    for head in range(2):
        rows = slice(head * HD, (head + 1) * HD)
        mine = (lane // HD) == head
        q_head_t = head_rows(q_t, head)
        grad_head_t = head_rows(grad_t, head)
        q_head = jnp.where(mine, q[...].astype(F32), 0.0).astype(BF16)
        grad_head = jnp.where(mine, grad[...].astype(F32), 0.0).astype(BF16)
        log_total = stat[head : head + 1, :]
        inner = jnp.sum(grad_t[rows].astype(F32) * att_t[rows], axis=0, keepdims=True)
        query_parts = [None] * (length // BLOCK)
        dk_parts = []
        dv_parts = []
        for index in range(length // BLOCK):
            start, stop = index * BLOCK, (index + 1) * BLOCK
            scores = dot_nn(k[start:stop, :], q_head_t[:, start:])
            weights = jnp.exp(scores - log_total[:, start:])
            diagonal = jnp.where(allowed, weights[:, :BLOCK], 0.0)
            if stop < length:
                weights = jnp.concatenate([diagonal, weights[:, BLOCK:]], axis=1)
            else:
                weights = diagonal
            weights_grad = dot_nn(v[start:stop, :], grad_head_t[:, start:])
            scores_grad = (weights * (weights_grad - inner[:, start:])).astype(BF16)
            dv_parts.append(dot_nn(weights.astype(BF16), grad_head[start:]))
            dk_parts.append(dot_nn(scores_grad, q_head[start:]))
            query = dot_nn(k_t[rows, start:stop], scores_grad)
            for later in range(index, length // BLOCK):
                piece = query[:, (later - index) * BLOCK : (later - index + 1) * BLOCK]
                kept = query_parts[later]
                query_parts[later] = piece if kept is None else kept + piece
        q_lanes.append(jnp.concatenate(query_parts, axis=1))
        dk_lanes.append(jnp.concatenate(dk_parts, axis=0))
        dv_lanes.append(jnp.concatenate(dv_parts, axis=0))
        sum_parts = []
        mem_total = None
        for index in range(length // BLOCK):
            start, stop = index * BLOCK, (index + 1) * BLOCK
            rate_row = rate[2 * head + 1 : 2 * head + 2, start:stop]
            offset = places - centre[2 * head : 2 * head + 1, start:stop]
            mass = (
                jnp.exp(offset * offset * rate_row) * level[2 * head + 1 : 2 * head + 2, start:stop]
            )
            basis_grad = dot_nn(mem_v[...], grad_head_t[:, start:stop])
            zeroth = basis_grad * mass
            first = zeroth * offset
            second = first * offset
            sum_parts.append(
                jnp.concatenate(
                    [
                        jnp.sum(first, axis=0, keepdims=True) * (-2.0 * rate_row),
                        jnp.sum(second, axis=0, keepdims=True) * (2.0 * rate_row * rate_row)
                        + jnp.sum(zeroth, axis=0, keepdims=True) * rate_row,
                    ],
                    axis=0,
                )
            )
            piece = dot_nn(mass.astype(BF16), grad_head[start:stop])
            mem_total = piece if mem_total is None else mem_total + piece
        dmv_lanes.append(mem_total)
        mass_grads.append(jnp.concatenate(sum_parts, axis=1))
    parity = lax.broadcasted_iota(jnp.int32, logits.shape, 0) % 2
    basis_grads = jnp.concatenate(
        mass_grads + [jnp.zeros((4, length), F32)], axis=0
    )
    slope = jnp.where(parity == 0, centre * (1.0 - centre), 0.05 * centre)
    logits_grad = basis_grads * slope * flag_value
    query_total = jnp.concatenate(q_lanes, axis=0) + dot_tn_exact(maps, logits_grad)
    dq[...] = (0.125 * query_total).T.astype(BF16)
    dk[...] = (0.125 * (dk_lanes[0] + dk_lanes[1])).astype(BF16)
    dv[...] = (dv_lanes[0] + dv_lanes[1]).astype(BF16)
    dmem_v[...] = (flag_value * (dmv_lanes[0] + dmv_lanes[1])).astype(BF16)
    row = lax.broadcasted_iota(jnp.int32, maps.shape, 0)
    lanes = lax.broadcasted_iota(jnp.int32, maps.shape, 1)
    outer = jnp.where(
        (row // 2) == (lanes // HD), add_parts(dot_nn(three_parts(logits_grad), q[...])) * 0.125, 0.0
    )
    dmem_k[...] = dot_tn_exact(mem_rows, outer).astype(BF16)
    dmw[0] = add_parts(dot_nt(three_parts(outer), mem_k[...]))
    ones = jnp.ones((16, length), BF16)
    sums[0, 0:8] = jnp.broadcast_to(jnp.sum(logits_grad, axis=1, keepdims=True), (8, 128))
    sums[0, 8:9] = dot_nn(ones, dq[...])[0:1]
    sums[0, 9:10] = dot_nn(ones, dv[...])[0:1]
    sums[0, 10:16] = jnp.zeros((6, 128), F32)
    width = norm_t.shape[0]
    rows_grad = dot_nn(norm_t[...], jnp.concatenate([dq[...], dk[...], dv[...]], axis=1))
    mem_grad = dot_nn(coeffs_t[...], jnp.concatenate([dmem_k[...], dmem_v[...]], axis=1))
    dqkv[:width] = rows_grad[:, :128].astype(BF16)
    dqkv[width : 2 * width] = (rows_grad[:, 128:256] + mem_grad[:, :128]).astype(BF16)
    dqkv[2 * width :] = (rows_grad[:, 256:] + mem_grad[:, 128:]).astype(BF16)


def attend_back(
    order, side, first, pairs, earlier, scalars, flags, q, k, v, mem_k, mem_v, mw, grad, att_t, stat, norm_t, coeffs_t
):
    length, width = q.shape
    basis = mem_k.shape[0]
    side_pairs = width // 256
    base = side * side_pairs + first
    half = width // 2
    rows = pl.BlockSpec((length, 128), lambda p, *_: (0, base + p))
    mem_rows = pl.BlockSpec((basis, 128), lambda p, *_: (0, base + p))
    out_rows = pl.BlockSpec((length, 128), lambda p, *_: (0, first + p))
    out_mem_rows = pl.BlockSpec((basis, 128), lambda p, *_: (0, first + p))
    operands = (q, k, v, mem_k, mem_v, mw, grad, att_t, stat, norm_t, coeffs_t)
    earlier = () if earlier is None else tuple(earlier)
    return order.call(
        functools.partial(attend_back_kernel, base),
        (pairs,),
        [
            rows,
            rows,
            rows,
            mem_rows,
            mem_rows,
            whole(mw.shape),
            rows,
            pl.BlockSpec((128, length), lambda p, *_: (base + p, 0)),
            pl.BlockSpec((8, length), lambda p, *_: (base + p, 0)),
            whole(norm_t.shape),
            whole(coeffs_t.shape),
        ]
        + [pl.BlockSpec(memory_space=pl.ANY)] * len(earlier),
        [
            out_rows,
            out_rows,
            out_rows,
            out_mem_rows,
            out_mem_rows,
            pl.BlockSpec((3 * width, 128), lambda p, *_: (0, first + p)),
            pl.BlockSpec((1, 8, basis), lambda p, *_: (first + p, 0, 0)),
            pl.BlockSpec((1, 16, 128), lambda p, *_: (first + p, 0, 0)),
        ],
        [shape_of((length, half), BF16)] * 3
        + [shape_of((basis, half), BF16)] * 2
        + [
            shape_of((3 * width, half), BF16),
            shape_of((side_pairs, 8, basis), F32),
            shape_of((side_pairs, 16, 128), F32),
        ],
        pairs * (28 * length * length * 128 + 6 * length * width * 128),
        "attend_back",
        operands + earlier,
        scalars=(scalars, flags),
        aliases={2 + len(operands) + index: index for index in range(len(earlier))},
    )


def feed_step(normed, normed_t, out_grad, up, up_bias, down, d_up, d_up_bias, d_down):
    weight_up = up[...]
    weight_down = down[...]
    before = dot_nn(normed[...], weight_up) + up_bias[...]
    out_rows = out_grad[...]
    hidden_grad = dot_nt(out_rows, weight_down)
    root = math.sqrt(2.0 / math.pi)
    square = before * before
    angle = jnp.tanh(before * (root + (root * 0.044715) * square))
    half_sum = 0.5 + 0.5 * angle
    activated = (before * half_sum).astype(BF16)
    slope = half_sum + before * (0.5 - 0.5 * angle * angle) * (
        root + (3.0 * 0.044715 * root) * square
    )
    before_grad = (hidden_grad * slope).astype(BF16)
    d_down[...] = dot_tn(activated, out_rows).astype(BF16)
    d_up[...] = dot_nn(normed_t[...], before_grad).astype(BF16)
    d_up_bias[...] = dot_nn(jnp.ones((8, before.shape[0]), BF16), before_grad)
    return dot_nn(activated, weight_down), dot_nt(before_grad, weight_up)


def residual_step(rows, mix, hid, wo, vectors, middle, normed, normed_t):
    branch = dot_nn(mix[rows, :], wo)
    values = hid[rows, :].astype(F32) + (branch + vectors[2:3])
    middle[rows, :] = values
    scaled, _ = scaled_rows(values)
    result = (scaled * vectors[3:4] + vectors[4:5]).astype(BF16)
    normed[rows, :] = result
    normed_t[:, rows] = result.T


def branch_step(rows, grad_sum, out_grad, middle, mix_t, wo, vectors, mid_grad, mix_grad):
    scaled, inverse = scaled_rows(middle[rows, :])
    grad_rows = grad_sum[rows, :]
    out_rows = out_grad[rows, :].astype(F32)
    result = out_rows + norm_back(grad_rows, scaled, inverse, vectors[3:4])
    mid_grad[rows, :] = result
    branch = result.astype(BF16)
    mix_grad[rows, :] = dot_nt(branch, wo).astype(BF16)
    sums = jnp.concatenate(
        [
            jnp.sum(branch.astype(F32), axis=0, keepdims=True),
            jnp.sum(grad_rows * scaled, axis=0, keepdims=True),
            jnp.sum(grad_rows, axis=0, keepdims=True),
            jnp.sum(out_rows, axis=0, keepdims=True),
            jnp.zeros((4, grad_rows.shape[1]), F32),
        ],
        axis=0,
    )
    return dot_nn(mix_t[:, rows], branch), sums


def feed_kernel(
    steps, scalars, mix, hid, mix_t, w_own, w_far, out_mine, out_theirs, vectors, up_far, up_own, ub_far,
    ub_own, down_far, down_own, du_far, du_own, dub_far, dub_own, dd_far, dd_own, mine, theirs, mid_grad,
    mix_grad, dw_own, dw_far, sums, middle, normed, normed_t, out_grad, out_sum, grad_sum, up, ub, down,
    du, dub, dd,
):
    index = pl.program_id(0)
    step = index - 1
    me = scalars[0]
    length = mix.shape[0]
    tokens = theirs.shape[0]
    spans = [slice(start, start + tokens) for start in range(0, length, tokens)]

    def half_at(half):
        return pl.ds(pl.multiple_of(half * tokens, tokens), tokens)

    @pl.when(index == 0)
    def _():
        out_sum[...] = jnp.zeros_like(out_sum)
        grad_sum[...] = jnp.zeros_like(grad_sum)
        out_grad[half_at(me), :] = out_mine[0]
        out_grad[half_at(1 - me), :] = out_theirs[...]
        wo = jnp.concatenate([w_own[...], w_far[...]], axis=0)
        for rows in spans:
            residual_step(rows, mix, hid, wo, vectors, middle, normed, normed_t)

    @pl.when((step >= 0) & (step < 2 * steps))
    def _():
        for side, weights in ((0, (up_far, ub_far, down_far)), (1, (up_own, ub_own, down_own))):

            @pl.when((step >= steps) == (side == 1))
            def _():
                up[...] = weights[0][...]
                ub[...] = weights[1][side : side + 1, :]
                down[...] = weights[2][...]

        forward, backward = feed_step(normed, normed_t, out_grad, up, ub, down, du, dub, dd)
        out_sum[...] += forward
        grad_sum[...] += backward
        for side, grads in ((0, (du_far, dub_far, dd_far)), (1, (du_own, dub_own, dd_own))):

            @pl.when((step >= steps) == (side == 1))
            def _():
                for target, held in zip(grads, (du, dub, dd)):
                    target[...] = held[...]

    @pl.when(step == 2 * steps)
    def _():
        for target, half in ((mine.at[0], me), (theirs, 1 - me)):
            at = half_at(half)
            target[...] = (middle[at, :] + out_sum[at, :] + vectors[5:6]).astype(BF16)
        wo = jnp.concatenate([w_own[...], w_far[...]], axis=0)
        total = None
        for rows in spans:
            fresh, added_sums = branch_step(
                rows, grad_sum, out_grad, middle, mix_t, wo, vectors, mid_grad, mix_grad
            )
            total = fresh if total is None else total + fresh
            sums[...] = added_sums if rows.start == 0 else sums[...] + added_sums
        half = w_own.shape[0]
        for side, out in enumerate((dw_own, dw_far)):
            rows = slice(side * half, (side + 1) * half)
            out[:half] = total[rows, :half].astype(BF16)
            out[half:] = total[rows, half:].astype(BF16)


def feed(order, scalars, mix, hid, mix_t, w_own, w_far, out_grad, out_grad_come, vectors, up_far, up_own, ub_far, ub_own, down_far, down_own):
    length, width = hid.shape
    tokens = length // 2
    hidden = up_own.shape[1]
    steps = hidden // FEED_BLOCK

    def far_block(i):
        return jnp.clip(i - 1, 0, steps - 1)

    def own_block(i):
        return jnp.clip(i - 1 - steps, 0, steps - 1)

    def up_spec(block):
        return pl.BlockSpec((width, FEED_BLOCK), lambda i, s: (0, block(i)))

    def bias_spec(block, rows):
        return pl.BlockSpec((rows, FEED_BLOCK), lambda i, s: (0, block(i)))

    def down_spec(block):
        return pl.BlockSpec((FEED_BLOCK, width), lambda i, s: (block(i), 0))

    def once(shape, place=None):
        zeros = (0,) * len(shape)
        return pl.BlockSpec(
            shape, place or (lambda i, s: zeros), pipeline_mode=pl.Buffered(1)
        )

    def mine_at(i, s):
        return (s[0], 0, 0)

    return order.call(
        functools.partial(feed_kernel, steps),
        (2 * steps + 2,),
        [
            once((length, width)),
            once((length, width)),
            once((width, length)),
            once(w_own.shape),
            once(w_far.shape),
            once((1, tokens, width), mine_at),
            once((tokens, width)),
            once(vectors.shape),
            up_spec(far_block),
            up_spec(own_block),
            bias_spec(far_block, 2),
            bias_spec(own_block, 2),
            down_spec(far_block),
            down_spec(own_block),
        ],
        [
            up_spec(far_block),
            up_spec(own_block),
            bias_spec(far_block, 8),
            bias_spec(own_block, 8),
            down_spec(far_block),
            down_spec(own_block),
            pl.BlockSpec((1, tokens, width), mine_at),
            whole((tokens, width)),
            whole((length, width)),
            whole((length, width)),
            whole((width, width // 2)),
            whole((width, width // 2)),
            whole((8, width)),
        ],
        [
            shape_of((width, hidden), BF16),
            shape_of((width, hidden), BF16),
            shape_of((8, hidden), F32),
            shape_of((8, hidden), F32),
            shape_of((hidden, width), BF16),
            shape_of((hidden, width), BF16),
            shape_of((2, tokens, width), BF16),
            shape_of((tokens, width), BF16),
            shape_of((length, width), F32),
            shape_of((length, width), BF16),
            shape_of((width, width // 2), BF16),
            shape_of((width, width // 2), BF16),
            shape_of((8, width), F32),
        ],
        24 * length * width * hidden,
        "feed",
        (mix, hid, mix_t, w_own, w_far, out_grad, out_grad_come, vectors)
        + (up_far, up_own, ub_far, ub_own, down_far, down_own),
        scratch=[
            pltpu.VMEM((length, width), F32),
            pltpu.VMEM((length, width), BF16),
            pltpu.VMEM((width, length), BF16),
            pltpu.VMEM((length, width), BF16),
            pltpu.VMEM((length, width), F32),
            pltpu.VMEM((length, width), F32),
            pltpu.VMEM((width, FEED_BLOCK), BF16),
            pltpu.VMEM((1, FEED_BLOCK), F32),
            pltpu.VMEM((FEED_BLOCK, width), BF16),
            pltpu.VMEM((width, FEED_BLOCK), BF16),
            pltpu.VMEM((8, FEED_BLOCK), F32),
            pltpu.VMEM((FEED_BLOCK, width), BF16),
        ],
        scalars=(scalars,),
    )


def input_back_kernel(
    scalars, hid, mid_grad, vectors, w_own, w_far, dq_own, dk_own, dv_own, dq_far, dk_far, dv_far,
    dmk_own, dmv_own, dmk_far, dmv_far, mine, theirs, coeff_mine, coeff_theirs, sums, total,
):
    me = scalars[0]
    index = pl.program_id(0)

    def back(own, far, part):
        return dot_nt(
            jnp.concatenate([own[...], far[...]], axis=1),
            jnp.concatenate([w_own[part], w_far[part]], axis=1),
        )

    grad_rows = back(dq_own, dq_far, 0) + back(dk_own, dk_far, 1) + back(dv_own, dv_far, 2)
    scaled, inverse = scaled_rows(hid[...].astype(F32))
    result = mid_grad[...] + norm_back(grad_rows, scaled, inverse, vectors[0:1])

    @pl.when(index == me)
    def _():
        mine[0] = result

    @pl.when(index != me)
    def _():
        theirs[...] = result.astype(BF16)

    fresh = jnp.concatenate(
        [
            jnp.sum(grad_rows * scaled, axis=0, keepdims=True),
            jnp.sum(grad_rows, axis=0, keepdims=True),
            jnp.zeros((6, grad_rows.shape[1]), F32),
        ],
        axis=0,
    )

    @pl.when(index == 0)
    def _():
        sums[...] = fresh
        total[...] = back(dmk_own, dmk_far, 1) + back(dmv_own, dmv_far, 2)
        part = coeff_theirs.shape[0]
        coeff_mine[0] = total[pl.ds(pl.multiple_of(me * part, part), part), :]
        coeff_theirs[...] = total[
            pl.ds(pl.multiple_of((1 - me) * part, part), part), :
        ].astype(BF16)

    @pl.when(index > 0)
    def _():
        sums[...] += fresh


def input_back(order, scalars, hid, mid_grad, vectors, w_own, w_far, own, far):
    length, width = hid.shape
    tokens = length // 2
    basis, half = own[3].shape
    rows = pl.BlockSpec((tokens, width), lambda i, s: (i, 0))
    half_rows = pl.BlockSpec((tokens, half), lambda i, s: (i, 0))
    return order.call(
        input_back_kernel,
        (2,),
        [rows, rows, whole(vectors.shape), whole(w_own.shape), whole(w_far.shape)]
        + [half_rows] * 6
        + [whole((basis, half))] * 4,
        [
            pl.BlockSpec((1, tokens, width), lambda i, s: (s[0], 0, 0)),
            whole((tokens, width)),
            pl.BlockSpec((1, basis // 2, width), lambda i, s: (s[0], 0, 0)),
            whole((basis // 2, width)),
            whole((8, width)),
        ],
        [
            shape_of((2, tokens, width), F32),
            shape_of((tokens, width), BF16),
            shape_of((2, basis // 2, width), F32),
            shape_of((basis // 2, width), BF16),
            shape_of((8, width), F32),
        ],
        6 * length * width * width,
        "input_back",
        (hid, mid_grad, vectors, w_own, w_far, *own[:3], *far[:3], *own[3:5], *far[3:5]),
        scratch=[pltpu.VMEM((basis, width), F32)],
        scalars=(scalars,),
    )


def tokens_place_kernel(scalars, *refs):
    for come, out in zip(refs[:3], refs[6:]):
        out[0] = come[...].astype(out.dtype)


def tokens_place(order, scalars, filled, come):
    return order.call(
        tokens_place_kernel,
        (1,),
        [whole(c.shape) for c in come] + [pl.BlockSpec(memory_space=pl.ANY)] * 3,
        [pl.BlockSpec((1,) + f.shape[1:], lambda i, s: (1 - s[0], 0, 0)) for f in filled],
        [shape_of(f.shape, f.dtype) for f in filled],
        0,
        "tokens_place",
        tuple(come) + tuple(filled),
        scalars=(scalars,),
        aliases={4 + index: index for index in range(3)},
    )


def pack_kernel(own_maps, own_sums, own_bias, far_maps, far_sums, far_bias, mid_sums, first_sums, own, far):
    for maps, sums, bias, out in (
        (own_maps, own_sums, own_bias, own),
        (far_maps, far_sums, far_bias, far),
    ):
        row = 0

        def put(values):
            nonlocal row
            for start in range(0, values.shape[1], 128):
                out[row : row + 1] = values[:, start : start + 128]
                row += 1

        for pair in range(maps.shape[0]):
            for index in range(4):
                put(maps[pair, index : index + 1])
        for index in (8, 9):
            for pair in range(maps.shape[0]):
                put(sums[pair, index : index + 1])
        put(bias[0:1])
        for index in range(4):
            put(mid_sums[index : index + 1])
        for index in range(2):
            put(first_sums[index : index + 1])
        for pair in range(maps.shape[0]):
            for index in range(4):
                put(sums[pair, index : index + 1])
        out[row:] = jnp.zeros((out.shape[0] - row, 128), F32)


def pack(order, own, own_bias, far, far_bias, mid_sums, first_sums):
    operands = (own[6], own[7], own_bias, far[6], far[7], far_bias, mid_sums, first_sums)
    pairs, _, basis = own[6].shape
    width = mid_sums.shape[1]
    count = pairs * 4 * (basis // 128) + 6 * pairs + own_bias.shape[1] // 128 + 6 * width // 128
    count += -count % 8
    return order.call(
        pack_kernel,
        (1,),
        [whole(o.shape) for o in operands],
        [whole((count, 128))] * 2,
        [shape_of((count, 128), F32)] * 2,
        0,
        "pack",
        operands,
    )


def to_peer(values):
    return jax.tree.map(lambda v: lax.ppermute(v, "mp", [(0, 1), (1, 0)]), values)


def across(values, offset, count):
    return lax.ppermute(values, "batch", [(i, i ^ offset) for i in range(count)])


def added(left, right):
    return left + right


def halve_kernel(flip, scalars, *refs):
    for chunk in range(2):
        low, high, low_more, high_more = refs[4 * chunk : 4 * chunk + 4]
        keep, send = refs[8 + 2 * chunk : 10 + 2 * chunk]
        bit = scalars[1 + (chunk ^ flip)]

        @pl.when(bit == 0)
        def _():
            keep[...] = added(low[...], low_more[...])
            send[...] = added(high[...], high_more[...])

        @pl.when(bit != 0)
        def _():
            keep[...] = added(high[...], high_more[...])
            send[...] = added(low[...], low_more[...])


def share_kernel(group, scalars, keep_a, more_a, keep_b, more_b, *outs):
    rows_a = keep_a.shape[0] // group
    rows_b = keep_b.shape[0] // group
    width = keep_b.shape[1]
    for offset in range(group):
        place = scalars[3 + offset]
        at = pl.ds(pl.multiple_of(place * rows_a, rows_a), rows_a)
        share = added(keep_a[at, :], more_a[at, :])
        for part in range(keep_a.shape[1] // width):
            outs[offset][part * rows_a : (part + 1) * rows_a] = share[
                :, part * width : (part + 1) * width
            ]
        at = pl.ds(pl.multiple_of(place * rows_b, rows_b), rows_b)
        outs[offset][outs[offset].shape[0] - rows_b :] = added(keep_b[at, :], more_b[at, :])


def total_kernel(*refs):
    total = refs[0][...].astype(F32)
    for ref in refs[1:-1]:
        total += ref[...].astype(F32)
    refs[-1][...] = total.astype(BF16)


def spread_kernel(group, scalars, *refs):
    out = refs[group]
    rows = out.shape[0] // group
    for offset in range(group):
        at = pl.ds(pl.multiple_of(scalars[3 + offset] * rows, rows), rows)
        out[at, :] = refs[offset][...]


def small_kernel(left, right, out):
    out[...] = left[...] + right[...]


def small_add(order, left, right):
    return order.call(
        small_kernel,
        (1,),
        [whole(left.shape)] * 2,
        [whole(left.shape)],
        [shape_of(left.shape, F32)],
        0,
        "small_add",
        (left, right),
    )[0]


class BatchSum:
    def __init__(self, order, scalars, count):
        self.order = order
        self.scalars = scalars
        self.count = count
        self.group = min(4, count // 4)

    def halve(self, flip, quads):
        specs = []
        operands = []
        out_specs = []
        shapes = []
        for shape, quad in quads:
            cuts = self.cuts(shape[0])
            piece = (shape[0] // cuts, shape[1])
            for values, block in quad:
                specs.append(
                    pl.BlockSpec(
                        piece, lambda i, s, block=block, cuts=cuts: (block[0] * cuts + i, block[1])
                    )
                )
                operands.append(values)
            out_specs += [pl.BlockSpec(piece, lambda i, s: (i, 0))] * 2
            shapes += [shape, shape]
        keep_a, send_a, keep_b, send_b = self.order.call(
            functools.partial(halve_kernel, flip),
            (cuts,),
            specs,
            out_specs,
            [shape_of(s, BF16) for s in shapes],
            0,
            "halve",
            operands,
            scalars=(self.scalars,),
        )
        self.kept = (keep_a, keep_b)
        self.come = (
            across(send_a, 1 << flip, self.count),
            across(send_b, 2 >> flip, self.count),
        )

    def cuts(self, rows):
        return 2 if rows % 32 == 0 else 1

    def first(self, quads):
        self.halve(0, quads)

    def second(self):
        quads = []
        for kept, come in zip(self.kept, self.come):
            shape = (kept.shape[0] // 2, kept.shape[1])
            quads.append((shape, ((kept, (0, 0)), (kept, (1, 0)), (come, (0, 0)), (come, (1, 0)))))
        self.halve(1, quads)

    def around(self, own):
        return [own[0]] + [
            across(own[offset], offset << 2, self.count) for offset in range(1, self.group)
        ]

    def share(self):
        operands = (self.kept[0], self.come[0], self.kept[1], self.come[1])
        width = operands[2].shape[1]
        shape = ((operands[0].size + operands[2].size) // (width * self.group), width)
        self.shares = self.around(
            self.order.call(
                functools.partial(share_kernel, self.group),
                (1,),
                [whole(o.shape) for o in operands],
                [whole(shape)] * self.group,
                [shape_of(shape, BF16)] * self.group,
                0,
                "share",
                operands,
                scalars=(self.scalars,),
            )
        )

    def total(self):
        shape = self.shares[0].shape
        (self.mine,) = self.order.call(
            total_kernel,
            (1,),
            [whole(shape)] * self.group,
            [whole(shape)],
            [shape_of(shape, BF16)],
            0,
            "total",
            self.shares,
        )
        offset = 4 * self.group
        while offset < self.count:
            self.mine = added(self.mine, across(self.mine, offset, self.count))
            offset *= 2

    def around_rest(self):
        self.pieces = self.around([self.mine] * self.group)

    def spread(self):
        rows, width = self.mine.shape
        shape = (self.group * rows, width)
        (quarter,) = self.order.call(
            functools.partial(spread_kernel, self.group),
            (1,),
            [whole(p.shape) for p in self.pieces],
            [whole(shape)],
            [shape_of(shape, BF16)],
            0,
            "spread",
            self.pieces,
            scalars=(self.scalars,),
        )
        self.quarters = [quarter] + [
            across(quarter, offset, self.count) for offset in (1, 2, 3)
        ]


def peers_added_kernel(*refs):
    for index in range(2):
        refs[4 + index][...] = added(refs[2 * index][...], refs[2 * index + 1][...])
    refs[6][...] = jnp.zeros_like(refs[6])


def peers_added(order, up_pair, down_pair):
    cuts = 4
    width = down_pair[0].shape[1]
    up_spec = pl.BlockSpec((up_pair[0].shape[0] // cuts, width), lambda i: (i, 1))
    up_out = pl.BlockSpec((up_pair[0].shape[0] // cuts, width), lambda i: (i, 0))
    down_spec = pl.BlockSpec((down_pair[0].shape[0] // cuts, width), lambda i: (i, 0))
    return order.call(
        peers_added_kernel,
        (cuts,),
        [up_spec, up_spec, down_spec, down_spec],
        [up_out, down_spec, whole((8, 128))],
        [
            shape_of((up_pair[0].shape[0], width), BF16),
            shape_of(down_pair[0].shape, BF16),
            shape_of((8, 128), F32),
        ],
        0,
        "peers_added",
        tuple(up_pair) + tuple(down_pair),
    )[:2]


def feed_place_kernel(up_sum, down_sum, _, up_out, down_out):
    up_out[...] = up_sum[...].astype(F32)
    down_out[...] = down_sum[...].astype(F32)


def feed_place(order, up_sum, down_sum, up_grad):
    cuts = 4
    width = down_sum.shape[1]
    up_rows = up_sum.shape[0] // cuts
    down_rows = down_sum.shape[0] // cuts
    return order.call(
        feed_place_kernel,
        (cuts,),
        [
            pl.BlockSpec((up_rows, width), lambda i: (i, 0)),
            pl.BlockSpec((down_rows, width), lambda i: (i, 0)),
            pl.BlockSpec(memory_space=pl.ANY),
        ],
        [
            pl.BlockSpec((up_rows, width), lambda i: (i, 1)),
            pl.BlockSpec((down_rows, width), lambda i: (i, 0)),
        ],
        [shape_of(up_grad.shape, F32), shape_of(down_sum.shape, F32)],
        0,
        "feed_place",
        (up_sum, down_sum, up_grad),
        aliases={2: 0},
    )


def mixed_halve_kernel(scalars, *refs):
    for chunk in range(2):
        keep, send = refs[16 + 2 * chunk : 18 + 2 * chunk]
        bit = scalars[1 + chunk]

        def fill(target, half):
            own, own_more, peer, peer_more = refs[8 * chunk + 4 * half : 8 * chunk + 4 * half + 4]
            rows = own.shape[0]
            target[:rows] = added(own[...], peer[...])
            target[rows:] = added(own_more[...], peer_more[...])

        @pl.when(bit == 0)
        def _():
            fill(keep, 0)
            fill(send, 1)

        @pl.when(bit != 0)
        def _():
            fill(keep, 1)
            fill(send, 0)


class MixedSum(BatchSum):
    def first(self, dqkv, dwo, du):
        width, cols = dwo[0].shape
        part = width // 2
        steps = cols // 128
        specs = []
        operands = []
        for chunk in range(2):
            for half in range(2):
                main = dwo if (chunk, half) == (1, 1) else dqkv
                block = 0 if main is dwo else 2 * chunk + half
                for side in range(2):
                    specs.append(pl.BlockSpec((width, 128), lambda i, s, b=block: (b, i)))
                    specs.append(
                        pl.BlockSpec((part, 128), lambda i, s, h=half, c=chunk: (h, steps * c + i))
                    )
                    operands += [main[side], du[side]]
        shape = (width + part, cols)
        keep_a, send_a, keep_b, send_b = self.order.call(
            mixed_halve_kernel,
            (steps,),
            specs,
            [pl.BlockSpec((width + part, 128), lambda i, s: (0, i))] * 4,
            [shape_of(shape, BF16)] * 4,
            0,
            "mixed_halve",
            operands,
            scalars=(self.scalars,),
        )
        self.kept = (keep_a, keep_b)
        self.come = (across(send_a, 1, self.count), across(send_b, 2, self.count))


def mixed_place_kernel(group, scalars, *refs):
    qkv_out, up_out, wo_out = refs[-3:]
    cols = refs[0].shape[1]
    width = wo_out.shape[1]
    part = width // 2
    rows = refs[0].shape[0] // (2 * group)

    def segments(quarter, place):
        start = (quarter * group + place) * rows
        marks = [start] + [m for m in (part, width) if start < m < start + rows] + [start + rows]
        return [(a, a - start, b - a) for a, b in zip(marks, marks[1:])]

    for index in range(4):
        column = scalars[1] ^ (index % 2)
        row = scalars[2] ^ (index // 2)
        values = refs[index]
        for quarter in range(2):

            @pl.when(row == quarter)
            def _():
                for place in range(group):
                    for at, inner, size in segments(quarter, place):
                        start = 2 * place * rows + inner
                        piece = values[start : start + size].astype(F32)
                        if at < width:
                            to = pl.multiple_of(column * width + at, 16)
                            qkv_out[pl.ds(to, size), :] = piece
                        else:
                            to = pl.multiple_of(column * part + at - width, 16)
                            up_out[pl.ds(to, size), :cols] = piece

            for half in range(2):

                @pl.when((column == quarter) & (row == half))
                def _():
                    for place in range(group):
                        for at, inner, size in segments(quarter, place):
                            start = (2 * place + 1) * rows + inner
                            piece = values[start : start + size].astype(F32)
                            if at >= width:
                                to = half * part + at - width
                                up_out[to : to + size, cols:] = piece
                            elif half == 0:
                                qkv_out[2 * width + at : 2 * width + at + size] = piece
                            elif at < part:
                                wo_out[at : at + size, :cols] = piece
                            else:
                                wo_out[at - part : at - part + size, cols:] = piece


def mixed_place(order, scalars, summed, width, hidden):
    half = width // 2
    return order.call(
        functools.partial(mixed_place_kernel, summed.group),
        (1,),
        [whole(o.shape) for o in summed.quarters],
        [
            whole((3 * width, half)),
            pl.BlockSpec((width, width), lambda i, s: (0, 0)),
            whole((half, width)),
        ],
        [
            shape_of((3 * width, half), F32),
            shape_of((width, hidden), F32),
            shape_of((half, width), F32),
        ],
        0,
        "mixed_place",
        summed.quarters,
        scalars=(scalars,),
    )


def per_device(
    count,
    hidden_in,
    memory_flags,
    memory_coeffs,
    first_gain,
    first_bias,
    query_key_value_matrix,
    qv_bias,
    memory_weight,
    memory_bias,
    output_matrix,
    out_bias,
    second_gain,
    second_bias,
    up_matrix,
    up_bias_vector,
    down_matrix,
    down_bias,
    out_grad,
):
    me = lax.axis_index("mp")
    position = lax.axis_index("batch")
    width = hidden_in.shape[2]
    half = width // 2
    group = min(4, count // 4)
    place = (position >> 2) % group
    scalars = jnp.stack(
        [me, position & 1, (position >> 1) & 1] + [place ^ offset for offset in range(group)]
    ).astype(jnp.int32)

    def from_peer(values):
        return to_peer(lax.dynamic_index_in_dim(values, 1 - me, 0, keepdims=False))

    hidden_come = from_peer(hidden_in)
    w_own = jnp.transpose(query_key_value_matrix, (1, 0, 2))
    w_far = to_peer(w_own)
    coeffs_come = from_peer(memory_coeffs)
    qv_far, mw_far, mb_far, ub_far = to_peer(
        (qv_bias, memory_weight, memory_bias, up_bias_vector)
    )

    query_bias = jnp.concatenate([qv_bias, qv_far], axis=1).astype(F32)
    mem_maps = jnp.concatenate([memory_weight, mw_far], axis=1).astype(F32)
    mem_maps = jnp.transpose(mem_maps, (1, 0, 2))
    mem_biases = jnp.concatenate([memory_bias, mb_far], axis=1).astype(F32)
    vectors = jnp.stack(
        [first_gain, first_bias, out_bias, second_gain, second_bias, down_bias] + [down_bias] * 2
    )
    up_biases = jnp.stack([ub_far, up_bias_vector]).astype(F32)
    order = Order()
    hid, norm_t, q, k, v, mem_k, mem_v, coeffs_t = project(
        order, scalars, hidden_in, hidden_come, vectors, w_own, w_far, query_bias, memory_coeffs, coeffs_come
    )
    later, _ = lax.optimization_barrier(
        ((output_matrix, out_grad, up_matrix, down_matrix), (coeffs_t, mw_far, mb_far, ub_far))
    )
    wo_far = to_peer(later[0])
    out_grad_come = from_peer(later[1])
    up_far = to_peer(later[2])
    down_far = to_peer(later[3])
    att_t, mix_t, mix, stat = attend(
        order, scalars, memory_flags, q, k, v, mem_k, mem_v, mem_maps, mem_biases
    )
    (
        du_far,
        du_own,
        dub_far,
        dub_own,
        dd_far,
        dd_own,
        block_mine,
        block_theirs,
        mid_grad,
        mix_grad,
        dwo_own,
        dwo_far,
        mid_sums,
    ) = feed(
        order,
        scalars,
        mix,
        hid,
        mix_t,
        output_matrix,
        wo_far,
        out_grad,
        out_grad_come,
        vectors,
        up_far,
        up_matrix,
        up_biases,
        up_biases,
        down_far,
        down_matrix,
    )
    du_peer, dd_peer = to_peer((du_far, dd_far))
    dwo_peer = to_peer(dwo_far)
    back_args = (
        scalars, memory_flags, q, k, v, mem_k, mem_v, mem_maps, mix_grad, att_t, stat, norm_t, coeffs_t
    )
    pairs = width // 256
    far = attend_back(order, 1, 0, pairs, None, *back_args)
    up_sum, down_sum = peers_added(order, (du_own, du_peer), (dd_own, dd_peer))
    dqkv_peer = to_peer(far[5])
    up_sum, down_sum = lax.psum((up_sum, down_sum), "batch")
    block_come = to_peer(block_theirs)
    own = attend_back(order, 0, 0, pairs, None, *back_args)
    dqkv_own = own[5]
    last = MixedSum(order, scalars, count)
    last.first((dqkv_own, dqkv_peer), (dwo_own, dwo_peer), (du_own, du_peer))
    in_mine, in_theirs, coeff_mine, coeff_theirs, first_sums = input_back(
        order, scalars, hid, mid_grad, vectors, w_own, w_far, own, far
    )
    small, far_flat = pack(order, own, dub_own, far, dub_far, mid_sums, first_sums)
    last.second()
    come, in_come, coeff_come = to_peer(
        lax.optimization_barrier((far_flat, in_theirs, coeff_theirs, last.kept[0]))[:3]
    )
    block_out, input_grad, coeff_grad = tokens_place(
        order, scalars, (block_mine, in_mine, coeff_mine), (block_come, in_come, coeff_come)
    )
    last.share()
    small = small_add(order, small, come)
    small = small_add(order, small, across(small, 1, count))
    last.total()
    last.around_rest()
    small = small_add(order, small, across(small, 2, count))
    last.spread()
    offset = 4
    while offset < count:
        small = small_add(order, small, across(small, offset, count))
        offset *= 2
    query_key_value_grad, up_weight_grad, output_matrix_grad = mixed_place(
        order, scalars, last, width, up_matrix.shape[1]
    )
    query_key_value_grad = jnp.transpose(
        query_key_value_grad.reshape(3, width, half), (1, 0, 2)
    )
    up_weight_grad, down_weight_grad = feed_place(order, up_sum, down_sum, up_weight_grad)

    heads, basis = memory_weight.shape[1:]
    rows = 0

    def take(size):
        nonlocal rows
        piece = small[rows : rows + size // 128]
        rows += size // 128
        return piece

    memory_weight_grad = jnp.transpose(take(2 * heads * basis).reshape(heads, 2, basis), (1, 0, 2))
    qv_bias_grad = take(2 * half).reshape(2, half)
    up_bias_grad = take(up_bias_vector.shape[0]).reshape(-1)
    vector_grads = [take(width).reshape(-1) for _ in range(6)]
    memory_bias_grad = jnp.transpose(take(2 * heads * 128)[:, 0].reshape(heads, 2), (1, 0))
    return (
        block_out,
        input_grad,
        coeff_grad,
        vector_grads[4],
        vector_grads[5],
        query_key_value_grad,
        qv_bias_grad,
        memory_weight_grad,
        memory_bias_grad,
        output_matrix_grad,
        vector_grads[0],
        vector_grads[1],
        vector_grads[2],
        up_weight_grad,
        up_bias_grad,
        down_weight_grad,
        vector_grads[3],
    )


def solution(mesh):
    tokens = P("batch", "mp", None)
    return jax.shard_map(
        functools.partial(per_device, mesh.shape["batch"]),
        mesh=mesh,
        in_specs=(
            tokens,
            P("batch"),
            tokens,
            P(),
            P(),
            P(None, None, "mp"),
            P(None, "mp"),
            P(None, "mp", None),
            P(None, "mp"),
            P("mp", None),
            P(),
            P(),
            P(),
            P(None, "mp"),
            P("mp"),
            P("mp", None),
            P(),
            tokens,
        ),
        out_specs=(
            tokens,
            tokens,
            tokens,
            P(),
            P(),
            P(None, None, "mp"),
            P(None, "mp"),
            P(None, "mp", None),
            P(None, "mp"),
            P("mp", None),
            P(),
            P(),
            P(),
            P(None, "mp"),
            P("mp"),
            P("mp", None),
            P(),
        ),
        check_vma=False,
    )
```

```python
import functools
import math

import jax
import jax.numpy as jnp
from jax import lax
from jax.experimental import pallas as pl
from jax.experimental.pallas import tpu as pltpu
from jax.sharding import PartitionSpec as P

HD = 64
BLOCK = 256
FEED_BLOCK = 512
BF16 = jnp.bfloat16
F32 = jnp.float32
VMEM_BYTES = 56 * 2**20


def dot_nn(left, right):
    return lax.dot_general(left, right, (((1,), (0,)), ((), ())), preferred_element_type=F32)


def dot_nt(left, right):
    return lax.dot_general(left, right, (((1,), (1,)), ((), ())), preferred_element_type=F32)


def dot_tn(left, right):
    return lax.dot_general(left, right, (((0,), (0,)), ((), ())), preferred_element_type=F32)


def dot_tn_exact(left, right):
    return lax.dot_general(
        left,
        right,
        (((0,), (0,)), ((), ())),
        precision=lax.Precision.HIGHEST,
        preferred_element_type=F32,
    )


def three_parts(values):
    high = values.astype(BF16).astype(F32)
    rest = values - high
    middle = rest.astype(BF16).astype(F32)
    return jnp.concatenate([high, middle, rest - middle], axis=0).astype(BF16)


def add_parts(stacked):
    rows = stacked.shape[0] // 3
    return stacked[:rows] + stacked[rows : 2 * rows] + stacked[2 * rows :]


def scaled_rows(values):
    row_mean = jnp.mean(values, axis=-1, keepdims=True)
    centred = values - row_mean
    row_var = jnp.mean(centred * centred, axis=-1, keepdims=True)
    inverse = lax.rsqrt(row_var + 1e-05)
    return centred * inverse, inverse


def norm_back(grad_out, scaled, inverse, gain_vec):
    grad_scaled = grad_out * gain_vec
    first_mean = jnp.mean(grad_scaled, axis=-1, keepdims=True)
    second_mean = jnp.mean(grad_scaled * scaled, axis=-1, keepdims=True)
    return inverse * (grad_scaled - first_mean - scaled * second_mean)


def whole(shape):
    return pl.BlockSpec(shape, lambda *_: (0,) * len(shape))


class Order:
    def __init__(self):
        self.token = None

    def call(
        self, kernel, grid, in_specs, out_specs, out_shape, flops, name, operands, scratch=(), scalars=(),
        aliases=None,
    ):
        count = len(operands)
        prefetched = len(scalars)
        token = () if self.token is None else (self.token,)

        def body(*refs):
            kernel(*refs[: prefetched + count], *refs[prefetched + count + len(token) :])

        bytes_accessed = sum(math.prod(s.shape) * jnp.dtype(s.dtype).itemsize for s in out_shape)
        results = pl.pallas_call(
            body,
            grid_spec=pltpu.PrefetchScalarGridSpec(
                num_scalar_prefetch=prefetched,
                grid=grid,
                in_specs=list(in_specs) + [pl.BlockSpec(memory_space=pl.ANY)] * len(token),
                out_specs=list(out_specs),
                scratch_shapes=list(scratch),
            ),
            out_shape=out_shape,
            input_output_aliases=aliases or {},
            compiler_params=pltpu.CompilerParams(
                vmem_limit_bytes=VMEM_BYTES, dimension_semantics=("arbitrary",) * len(grid)
            ),
            cost_estimate=pl.CostEstimate(
                flops=int(flops), bytes_accessed=2 * bytes_accessed, transcendentals=0
            ),
            name=name,
        )(*scalars, *operands, *token)
        self.token = results[-1]
        return results


def shape_of(shape, dtype):
    return jax.ShapeDtypeStruct(shape, dtype)


def project_kernel(
    scalars, mine, theirs, vectors, w_own, w_far, qb, coeffs_mine, coeffs_theirs,
    hid, norm_t, q, k, v, mem_k, mem_v, coeffs_t,
):
    me = scalars[0]
    index = pl.program_id(0)

    @pl.when(index == me)
    def _():
        hid[...] = mine[0]

    @pl.when(index != me)
    def _():
        hid[...] = theirs[...]

    scaled, _ = scaled_rows(hid[...].astype(F32))
    normed = (scaled * vectors[0:1] + vectors[1:2]).astype(BF16)
    norm_t[...] = normed.T

    def weight(part):
        return jnp.concatenate([w_own[part], w_far[part]], axis=1)

    q[...] = (dot_nn(normed, weight(0)) + qb[0:1]).astype(BF16)
    k[...] = dot_nn(normed, weight(1)).astype(BF16)
    v[...] = (dot_nn(normed, weight(2)) + qb[1:2]).astype(BF16)

    @pl.when(index == 0)
    def _():
        first = coeffs_mine[0].astype(F32)
        second = coeffs_theirs[...].astype(F32)
        rows = jnp.concatenate(
            [jnp.where(me == 0, first, second), jnp.where(me == 0, second, first)], axis=0
        ).astype(BF16)
        coeffs_t[...] = rows.T
        mem_k[...] = dot_nn(rows, weight(1)).astype(BF16)
        mem_v[...] = dot_nn(rows, weight(2)).astype(BF16)


def project(order, scalars, hidden_in, hidden_come, vectors, w_own, w_far, qb, coeffs, coeffs_come):
    tokens, width = hidden_come.shape
    length = 2 * tokens
    part = coeffs_come.shape[0]
    basis = 2 * part
    rows = pl.BlockSpec((tokens, width), lambda i, s: (i, 0))
    return order.call(
        project_kernel,
        (2,),
        [
            pl.BlockSpec((1, tokens, width), lambda i, s: (s[0], 0, 0)),
            whole((tokens, width)),
            whole(vectors.shape),
            whole(w_own.shape),
            whole(w_far.shape),
            whole(qb.shape),
            pl.BlockSpec((1, part, width), lambda i, s: (s[0], 0, 0)),
            whole((part, width)),
        ],
        [
            rows,
            pl.BlockSpec((width, tokens), lambda i, s: (0, i)),
            rows,
            rows,
            rows,
            whole((basis, width)),
            whole((basis, width)),
            whole((width, basis)),
        ],
        [
            shape_of((length, width), BF16),
            shape_of((width, length), BF16),
            shape_of((length, width), BF16),
            shape_of((length, width), BF16),
            shape_of((length, width), BF16),
            shape_of((basis, width), BF16),
            shape_of((basis, width), BF16),
            shape_of((width, basis), BF16),
        ],
        2 * length * width * width * 3,
        "project",
        (hidden_in, hidden_come, vectors, w_own, w_far, qb, coeffs, coeffs_come),
        scalars=(scalars,),
    )


def head_rows(values_t, head):
    part = values_t[head * HD : (head + 1) * HD]
    zeros = jnp.zeros_like(part)
    return jnp.concatenate([part, zeros] if head == 0 else [zeros, part], axis=0)


def map_rows(mw, pair):
    return jnp.concatenate(
        [mw[2 * pair], mw[2 * pair + 1], jnp.zeros((4, mw.shape[2]), F32)], axis=0
    )


def pair_maps(rows, mem_k):
    maps = dot_nn(rows.astype(BF16), mem_k)
    row = lax.broadcasted_iota(jnp.int32, maps.shape, 0)
    lane = lax.broadcasted_iota(jnp.int32, maps.shape, 1)
    return jnp.where((row // 2) == (lane // HD), maps, 0.0)


def bias_rows(mb, pair):
    row = lax.broadcasted_iota(jnp.int32, (8, 1), 0)
    column = jnp.zeros((8, 1), F32)
    for head in range(2):
        for which in range(2):
            column = jnp.where(row == 2 * head + which, mb[which, 2 * pair + head], column)
    return column


def basis_of(logits, basis_count):
    centre = jax.nn.sigmoid(logits)
    softplus = jnp.maximum(logits, 0.0) + jnp.log(1.0 + jnp.exp(-jnp.abs(logits)))
    spread = 0.05 * softplus + (8.0 / basis_count) ** 2
    rate = -0.5 / spread
    level = lax.rsqrt(2.0 * math.pi * spread) / basis_count
    return centre, rate, level


def places_of(basis_count):
    steps = lax.broadcasted_iota(jnp.int32, (basis_count, BLOCK), 0).astype(F32)
    return (steps + 0.5) / basis_count


def attend_kernel(scalars, flags, q, k, v, mem_k, mem_v, mw, mb, att_t, mix_t, mix, stat):
    length = q.shape[0]
    basis = mem_k.shape[0]
    flag_value = flags[scalars[0]].astype(F32)
    q_t = (q[...].astype(F32) * 0.125).astype(BF16).T
    v_t = v[...].T
    mem_v_t = mem_v[...].T
    pair = pl.program_id(0)
    maps = pair_maps(map_rows(mw, pair), mem_k[...])
    logits = add_parts(dot_nn(three_parts(maps), q_t)) + bias_rows(mb, pair)
    centre, rate, level = basis_of(logits, basis)
    places = places_of(basis)
    allowed = lax.broadcasted_iota(jnp.int32, (BLOCK, BLOCK), 0) <= lax.broadcasted_iota(
        jnp.int32, (BLOCK, BLOCK), 1
    )
    stat[4:8, :] = logits[0:4]
    heads = []
    for head in range(2):
        rows = slice(head * HD, (head + 1) * HD)
        v_ones = jnp.concatenate([v_t[rows], jnp.ones((16, length), BF16)], axis=0)
        heads.append((rows, head_rows(q_t, head), v_ones))
    for index in range(length // BLOCK):
        start, stop = index * BLOCK, (index + 1) * BLOCK
        scores = []
        for rows, q_head, v_ones in heads:
            scores.append(dot_nn(k[:stop, :], q_head[:, start:stop]))
        for head, (rows, q_head, v_ones) in enumerate(heads):
            near = jnp.where(allowed, scores[head][start:], -1e30)
            top = jnp.max(near, axis=0, keepdims=True)
            if index:
                far = scores[head][:start]
                top = jnp.maximum(top, jnp.max(far, axis=0, keepdims=True))
                weights = jnp.concatenate([jnp.exp(far - top), jnp.exp(near - top)], axis=0)
            else:
                weights = jnp.exp(near - top)
            total = dot_nn(v_ones[:, :stop], weights.astype(BF16))
            denominator = total[HD : HD + 1]
            attended = total[:HD] / denominator
            att_t[rows, start:stop] = attended
            stat[head : head + 1, start:stop] = top + jnp.log(denominator)
            offset = places - centre[2 * head : 2 * head + 1, start:stop]
            mass = (
                jnp.exp(offset * offset * rate[2 * head + 1 : 2 * head + 2, start:stop])
                * level[2 * head + 1 : 2 * head + 2, start:stop]
            )
            recalled = dot_nn(mem_v_t[rows], mass.astype(BF16))
            mix_t[rows, start:stop] = (attended + flag_value * recalled).astype(BF16)
    mix[...] = mix_t[...].T


def attend(order, scalars, flags, q, k, v, mem_k, mem_v, mw, mb):
    length, width = q.shape
    basis = mem_k.shape[0]
    pairs = width // 128
    rows = pl.BlockSpec((length, 128), lambda p, *_: (0, p))
    mem_rows = pl.BlockSpec((basis, 128), lambda p, *_: (0, p))
    cols = pl.BlockSpec((128, length), lambda p, *_: (p, 0))
    return order.call(
        attend_kernel,
        (pairs,),
        [
            rows,
            rows,
            rows,
            mem_rows,
            mem_rows,
            whole(mw.shape),
            pl.BlockSpec(memory_space=pltpu.SMEM),
        ],
        [cols, cols, rows, pl.BlockSpec((8, length), lambda p, *_: (p, 0))],
        [
            shape_of((width, length), F32),
            shape_of((width, length), BF16),
            shape_of((length, width), BF16),
            shape_of((pairs * 8, length), F32),
        ],
        12 * length * length * width,
        "attend",
        (q, k, v, mem_k, mem_v, mw, mb),
        scalars=(scalars, flags),
    )


def attend_back_kernel(
    base, scalars, flags, q, k, v, mem_k, mem_v, mw, grad, att_t, stat, norm_t, coeffs_t, *refs
):
    dq, dk, dv, dmem_k, dmem_v, dqkv, dmw, sums = refs[-8:]
    length = q.shape[0]
    basis = mem_k.shape[0]
    flag_value = flags[scalars[0]].astype(F32)
    q_t = (q[...].astype(F32) * 0.125).astype(BF16).T
    k_t = k[...].T
    grad_t = grad[...].T
    lane = lax.broadcasted_iota(jnp.int32, (length, 128), 1)
    mem_rows = map_rows(mw, base + pl.program_id(0))
    maps = pair_maps(mem_rows, mem_k[...])
    logits = stat[4:8, :]
    logits = jnp.concatenate([logits, jnp.zeros_like(logits)], axis=0)
    centre, rate, level = basis_of(logits, basis)
    places = places_of(basis)
    allowed = lax.broadcasted_iota(jnp.int32, (BLOCK, BLOCK), 0) <= lax.broadcasted_iota(
        jnp.int32, (BLOCK, BLOCK), 1
    )
    q_lanes = []
    dk_lanes = []
    dv_lanes = []
    dmv_lanes = []
    mass_grads = []
    for head in range(2):
        rows = slice(head * HD, (head + 1) * HD)
        mine = (lane // HD) == head
        q_head_t = head_rows(q_t, head)
        grad_head_t = head_rows(grad_t, head)
        q_head = jnp.where(mine, q[...].astype(F32), 0.0).astype(BF16)
        grad_head = jnp.where(mine, grad[...].astype(F32), 0.0).astype(BF16)
        log_total = stat[head : head + 1, :]
        inner = jnp.sum(grad_t[rows].astype(F32) * att_t[rows], axis=0, keepdims=True)
        query_parts = [None] * (length // BLOCK)
        dk_parts = []
        dv_parts = []
        for index in range(length // BLOCK):
            start, stop = index * BLOCK, (index + 1) * BLOCK
            scores = dot_nn(k[start:stop, :], q_head_t[:, start:])
            weights = jnp.exp(scores - log_total[:, start:])
            diagonal = jnp.where(allowed, weights[:, :BLOCK], 0.0)
            if stop < length:
                weights = jnp.concatenate([diagonal, weights[:, BLOCK:]], axis=1)
            else:
                weights = diagonal
            weights_grad = dot_nn(v[start:stop, :], grad_head_t[:, start:])
            scores_grad = (weights * (weights_grad - inner[:, start:])).astype(BF16)
            dv_parts.append(dot_nn(weights.astype(BF16), grad_head[start:]))
            dk_parts.append(dot_nn(scores_grad, q_head[start:]))
            query = dot_nn(k_t[rows, start:stop], scores_grad)
            for later in range(index, length // BLOCK):
                piece = query[:, (later - index) * BLOCK : (later - index + 1) * BLOCK]
                kept = query_parts[later]
                query_parts[later] = piece if kept is None else kept + piece
        q_lanes.append(jnp.concatenate(query_parts, axis=1))
        dk_lanes.append(jnp.concatenate(dk_parts, axis=0))
        dv_lanes.append(jnp.concatenate(dv_parts, axis=0))
        sum_parts = []
        mem_total = None
        for index in range(length // BLOCK):
            start, stop = index * BLOCK, (index + 1) * BLOCK
            rate_row = rate[2 * head + 1 : 2 * head + 2, start:stop]
            offset = places - centre[2 * head : 2 * head + 1, start:stop]
            mass = (
                jnp.exp(offset * offset * rate_row) * level[2 * head + 1 : 2 * head + 2, start:stop]
            )
            basis_grad = dot_nn(mem_v[...], grad_head_t[:, start:stop])
            zeroth = basis_grad * mass
            first = zeroth * offset
            second = first * offset
            sum_parts.append(
                jnp.concatenate(
                    [
                        jnp.sum(first, axis=0, keepdims=True) * (-2.0 * rate_row),
                        jnp.sum(second, axis=0, keepdims=True) * (2.0 * rate_row * rate_row)
                        + jnp.sum(zeroth, axis=0, keepdims=True) * rate_row,
                    ],
                    axis=0,
                )
            )
            piece = dot_nn(mass.astype(BF16), grad_head[start:stop])
            mem_total = piece if mem_total is None else mem_total + piece
        dmv_lanes.append(mem_total)
        mass_grads.append(jnp.concatenate(sum_parts, axis=1))
    parity = lax.broadcasted_iota(jnp.int32, logits.shape, 0) % 2
    basis_grads = jnp.concatenate(
        mass_grads + [jnp.zeros((4, length), F32)], axis=0
    )
    slope = jnp.where(parity == 0, centre * (1.0 - centre), 0.05 * centre)
    logits_grad = basis_grads * slope * flag_value
    query_total = jnp.concatenate(q_lanes, axis=0) + dot_tn_exact(maps, logits_grad)
    dq[...] = (0.125 * query_total).T.astype(BF16)
    dk[...] = (0.125 * (dk_lanes[0] + dk_lanes[1])).astype(BF16)
    dv[...] = (dv_lanes[0] + dv_lanes[1]).astype(BF16)
    dmem_v[...] = (flag_value * (dmv_lanes[0] + dmv_lanes[1])).astype(BF16)
    row = lax.broadcasted_iota(jnp.int32, maps.shape, 0)
    lanes = lax.broadcasted_iota(jnp.int32, maps.shape, 1)
    outer = jnp.where(
        (row // 2) == (lanes // HD), add_parts(dot_nn(three_parts(logits_grad), q[...])) * 0.125, 0.0
    )
    dmem_k[...] = dot_tn_exact(mem_rows, outer).astype(BF16)
    dmw[0] = add_parts(dot_nt(three_parts(outer), mem_k[...]))
    ones = jnp.ones((16, length), BF16)
    sums[0, 0:8] = jnp.broadcast_to(jnp.sum(logits_grad, axis=1, keepdims=True), (8, 128))
    sums[0, 8:9] = dot_nn(ones, dq[...])[0:1]
    sums[0, 9:10] = dot_nn(ones, dv[...])[0:1]
    sums[0, 10:16] = jnp.zeros((6, 128), F32)
    width = norm_t.shape[0]
    rows_grad = dot_nn(norm_t[...], jnp.concatenate([dq[...], dk[...], dv[...]], axis=1))
    mem_grad = dot_nn(coeffs_t[...], jnp.concatenate([dmem_k[...], dmem_v[...]], axis=1))
    dqkv[:width] = rows_grad[:, :128].astype(BF16)
    dqkv[width : 2 * width] = (rows_grad[:, 128:256] + mem_grad[:, :128]).astype(BF16)
    dqkv[2 * width :] = (rows_grad[:, 256:] + mem_grad[:, 128:]).astype(BF16)


def attend_back(
    order, side, first, pairs, earlier, scalars, flags, q, k, v, mem_k, mem_v, mw, grad, att_t, stat, norm_t, coeffs_t
):
    length, width = q.shape
    basis = mem_k.shape[0]
    side_pairs = width // 256
    base = side * side_pairs + first
    half = width // 2
    rows = pl.BlockSpec((length, 128), lambda p, *_: (0, base + p))
    mem_rows = pl.BlockSpec((basis, 128), lambda p, *_: (0, base + p))
    out_rows = pl.BlockSpec((length, 128), lambda p, *_: (0, first + p))
    out_mem_rows = pl.BlockSpec((basis, 128), lambda p, *_: (0, first + p))
    operands = (q, k, v, mem_k, mem_v, mw, grad, att_t, stat, norm_t, coeffs_t)
    earlier = () if earlier is None else tuple(earlier)
    return order.call(
        functools.partial(attend_back_kernel, base),
        (pairs,),
        [
            rows,
            rows,
            rows,
            mem_rows,
            mem_rows,
            whole(mw.shape),
            rows,
            pl.BlockSpec((128, length), lambda p, *_: (base + p, 0)),
            pl.BlockSpec((8, length), lambda p, *_: (base + p, 0)),
            whole(norm_t.shape),
            whole(coeffs_t.shape),
        ]
        + [pl.BlockSpec(memory_space=pl.ANY)] * len(earlier),
        [
            out_rows,
            out_rows,
            out_rows,
            out_mem_rows,
            out_mem_rows,
            pl.BlockSpec((3 * width, 128), lambda p, *_: (0, first + p)),
            pl.BlockSpec((1, 8, basis), lambda p, *_: (first + p, 0, 0)),
            pl.BlockSpec((1, 16, 128), lambda p, *_: (first + p, 0, 0)),
        ],
        [shape_of((length, half), BF16)] * 3
        + [shape_of((basis, half), BF16)] * 2
        + [
            shape_of((3 * width, half), BF16),
            shape_of((side_pairs, 8, basis), F32),
            shape_of((side_pairs, 16, 128), F32),
        ],
        pairs * (28 * length * length * 128 + 6 * length * width * 128),
        "attend_back",
        operands + earlier,
        scalars=(scalars, flags),
        aliases={2 + len(operands) + index: index for index in range(len(earlier))},
    )


def feed_step(normed, normed_t, out_grad, up, up_bias, down, d_up, d_up_bias, d_down):
    weight_up = up[...]
    weight_down = down[...]
    before = dot_nn(normed[...], weight_up) + up_bias[...]
    out_rows = out_grad[...]
    hidden_grad = dot_nt(out_rows, weight_down)
    root = math.sqrt(2.0 / math.pi)
    square = before * before
    angle = jnp.tanh(before * (root + (root * 0.044715) * square))
    half_sum = 0.5 + 0.5 * angle
    activated = (before * half_sum).astype(BF16)
    slope = half_sum + before * (0.5 - 0.5 * angle * angle) * (
        root + (3.0 * 0.044715 * root) * square
    )
    before_grad = (hidden_grad * slope).astype(BF16)
    d_down[...] = dot_tn(activated, out_rows).astype(BF16)
    d_up[...] = dot_nn(normed_t[...], before_grad).astype(BF16)
    d_up_bias[...] = dot_nn(jnp.ones((8, before.shape[0]), BF16), before_grad)
    return dot_nn(activated, weight_down), dot_nt(before_grad, weight_up)


def residual_step(rows, mix, hid, wo, vectors, middle, normed, normed_t):
    branch = dot_nn(mix[rows, :], wo)
    values = hid[rows, :].astype(F32) + (branch + vectors[2:3])
    middle[rows, :] = values
    scaled, _ = scaled_rows(values)
    result = (scaled * vectors[3:4] + vectors[4:5]).astype(BF16)
    normed[rows, :] = result
    normed_t[:, rows] = result.T


def branch_step(rows, grad_sum, out_grad, middle, mix_t, wo, vectors, mid_grad, mix_grad):
    scaled, inverse = scaled_rows(middle[rows, :])
    grad_rows = grad_sum[rows, :]
    out_rows = out_grad[rows, :].astype(F32)
    result = out_rows + norm_back(grad_rows, scaled, inverse, vectors[3:4])
    mid_grad[rows, :] = result
    branch = result.astype(BF16)
    mix_grad[rows, :] = dot_nt(branch, wo).astype(BF16)
    sums = jnp.concatenate(
        [
            jnp.sum(branch.astype(F32), axis=0, keepdims=True),
            jnp.sum(grad_rows * scaled, axis=0, keepdims=True),
            jnp.sum(grad_rows, axis=0, keepdims=True),
            jnp.sum(out_rows, axis=0, keepdims=True),
            jnp.zeros((4, grad_rows.shape[1]), F32),
        ],
        axis=0,
    )
    return dot_nn(mix_t[:, rows], branch), sums


def feed_kernel(
    steps, scalars, mix, hid, mix_t, w_own, w_far, out_mine, out_theirs, vectors, up_far, up_own, ub_far,
    ub_own, down_far, down_own, du_far, du_own, dub_far, dub_own, dd_far, dd_own, mine, theirs, mid_grad,
    mix_grad, dw_own, dw_far, sums, middle, normed, normed_t, out_grad, out_sum, grad_sum, up, ub, down,
    du, dub, dd,
):
    index = pl.program_id(0)
    step = index - 1
    me = scalars[0]
    length = mix.shape[0]
    tokens = theirs.shape[0]
    spans = [slice(start, start + tokens) for start in range(0, length, tokens)]

    def half_at(half):
        return pl.ds(pl.multiple_of(half * tokens, tokens), tokens)

    @pl.when(index == 0)
    def _():
        out_sum[...] = jnp.zeros_like(out_sum)
        grad_sum[...] = jnp.zeros_like(grad_sum)
        out_grad[half_at(me), :] = out_mine[0]
        out_grad[half_at(1 - me), :] = out_theirs[...]
        wo = jnp.concatenate([w_own[...], w_far[...]], axis=0)
        for rows in spans:
            residual_step(rows, mix, hid, wo, vectors, middle, normed, normed_t)

    @pl.when((step >= 0) & (step < 2 * steps))
    def _():
        for side, weights in ((0, (up_far, ub_far, down_far)), (1, (up_own, ub_own, down_own))):

            @pl.when((step >= steps) == (side == 1))
            def _():
                up[...] = weights[0][...]
                ub[...] = weights[1][side : side + 1, :]
                down[...] = weights[2][...]

        forward, backward = feed_step(normed, normed_t, out_grad, up, ub, down, du, dub, dd)
        out_sum[...] += forward
        grad_sum[...] += backward
        for side, grads in ((0, (du_far, dub_far, dd_far)), (1, (du_own, dub_own, dd_own))):

            @pl.when((step >= steps) == (side == 1))
            def _():
                for target, held in zip(grads, (du, dub, dd)):
                    target[...] = held[...]

    @pl.when(step == 2 * steps)
    def _():
        for target, half in ((mine.at[0], me), (theirs, 1 - me)):
            at = half_at(half)
            target[...] = (middle[at, :] + out_sum[at, :] + vectors[5:6]).astype(BF16)
        wo = jnp.concatenate([w_own[...], w_far[...]], axis=0)
        total = None
        for rows in spans:
            fresh, added_sums = branch_step(
                rows, grad_sum, out_grad, middle, mix_t, wo, vectors, mid_grad, mix_grad
            )
            total = fresh if total is None else total + fresh
            sums[...] = added_sums if rows.start == 0 else sums[...] + added_sums
        half = w_own.shape[0]
        for side, out in enumerate((dw_own, dw_far)):
            rows = slice(side * half, (side + 1) * half)
            out[:half] = total[rows, :half].astype(BF16)
            out[half:] = total[rows, half:].astype(BF16)


def feed(order, scalars, mix, hid, mix_t, w_own, w_far, out_grad, out_grad_come, vectors, up_far, up_own, ub_far, ub_own, down_far, down_own):
    length, width = hid.shape
    tokens = length // 2
    hidden = up_own.shape[1]
    steps = hidden // FEED_BLOCK

    def far_block(i):
        return jnp.clip(i - 1, 0, steps - 1)

    def own_block(i):
        return jnp.clip(i - 1 - steps, 0, steps - 1)

    def up_spec(block):
        return pl.BlockSpec((width, FEED_BLOCK), lambda i, s: (0, block(i)))

    def bias_spec(block, rows):
        return pl.BlockSpec((rows, FEED_BLOCK), lambda i, s: (0, block(i)))

    def down_spec(block):
        return pl.BlockSpec((FEED_BLOCK, width), lambda i, s: (block(i), 0))

    def once(shape, place=None):
        zeros = (0,) * len(shape)
        return pl.BlockSpec(
            shape, place or (lambda i, s: zeros), pipeline_mode=pl.Buffered(1)
        )

    def mine_at(i, s):
        return (s[0], 0, 0)

    return order.call(
        functools.partial(feed_kernel, steps),
        (2 * steps + 2,),
        [
            once((length, width)),
            once((length, width)),
            once((width, length)),
            once(w_own.shape),
            once(w_far.shape),
            once((1, tokens, width), mine_at),
            once((tokens, width)),
            once(vectors.shape),
            up_spec(far_block),
            up_spec(own_block),
            bias_spec(far_block, 2),
            bias_spec(own_block, 2),
            down_spec(far_block),
            down_spec(own_block),
        ],
        [
            up_spec(far_block),
            up_spec(own_block),
            bias_spec(far_block, 8),
            bias_spec(own_block, 8),
            down_spec(far_block),
            down_spec(own_block),
            pl.BlockSpec((1, tokens, width), mine_at),
            whole((tokens, width)),
            whole((length, width)),
            whole((length, width)),
            whole((width, width // 2)),
            whole((width, width // 2)),
            whole((8, width)),
        ],
        [
            shape_of((width, hidden), BF16),
            shape_of((width, hidden), BF16),
            shape_of((8, hidden), F32),
            shape_of((8, hidden), F32),
            shape_of((hidden, width), BF16),
            shape_of((hidden, width), BF16),
            shape_of((2, tokens, width), BF16),
            shape_of((tokens, width), BF16),
            shape_of((length, width), F32),
            shape_of((length, width), BF16),
            shape_of((width, width // 2), BF16),
            shape_of((width, width // 2), BF16),
            shape_of((8, width), F32),
        ],
        24 * length * width * hidden,
        "feed",
        (mix, hid, mix_t, w_own, w_far, out_grad, out_grad_come, vectors)
        + (up_far, up_own, ub_far, ub_own, down_far, down_own),
        scratch=[
            pltpu.VMEM((length, width), F32),
            pltpu.VMEM((length, width), BF16),
            pltpu.VMEM((width, length), BF16),
            pltpu.VMEM((length, width), BF16),
            pltpu.VMEM((length, width), F32),
            pltpu.VMEM((length, width), F32),
            pltpu.VMEM((width, FEED_BLOCK), BF16),
            pltpu.VMEM((1, FEED_BLOCK), F32),
            pltpu.VMEM((FEED_BLOCK, width), BF16),
            pltpu.VMEM((width, FEED_BLOCK), BF16),
            pltpu.VMEM((8, FEED_BLOCK), F32),
            pltpu.VMEM((FEED_BLOCK, width), BF16),
        ],
        scalars=(scalars,),
    )


def input_back_kernel(
    scalars, hid, mid_grad, vectors, w_own, w_far, dq_own, dk_own, dv_own, dq_far, dk_far, dv_far,
    dmk_own, dmv_own, dmk_far, dmv_far, mine, theirs, coeff_mine, coeff_theirs, sums, total,
):
    me = scalars[0]
    index = pl.program_id(0)

    def back(own, far, part):
        return dot_nt(
            jnp.concatenate([own[...], far[...]], axis=1),
            jnp.concatenate([w_own[part], w_far[part]], axis=1),
        )

    grad_rows = back(dq_own, dq_far, 0) + back(dk_own, dk_far, 1) + back(dv_own, dv_far, 2)
    scaled, inverse = scaled_rows(hid[...].astype(F32))
    result = mid_grad[...] + norm_back(grad_rows, scaled, inverse, vectors[0:1])

    @pl.when(index == me)
    def _():
        mine[0] = result

    @pl.when(index != me)
    def _():
        theirs[...] = result.astype(BF16)

    fresh = jnp.concatenate(
        [
            jnp.sum(grad_rows * scaled, axis=0, keepdims=True),
            jnp.sum(grad_rows, axis=0, keepdims=True),
            jnp.zeros((6, grad_rows.shape[1]), F32),
        ],
        axis=0,
    )

    @pl.when(index == 0)
    def _():
        sums[...] = fresh
        total[...] = back(dmk_own, dmk_far, 1) + back(dmv_own, dmv_far, 2)
        part = coeff_theirs.shape[0]
        coeff_mine[0] = total[pl.ds(pl.multiple_of(me * part, part), part), :]
        coeff_theirs[...] = total[
            pl.ds(pl.multiple_of((1 - me) * part, part), part), :
        ].astype(BF16)

    @pl.when(index > 0)
    def _():
        sums[...] += fresh


def input_back(order, scalars, hid, mid_grad, vectors, w_own, w_far, own, far):
    length, width = hid.shape
    tokens = length // 2
    basis, half = own[3].shape
    rows = pl.BlockSpec((tokens, width), lambda i, s: (i, 0))
    half_rows = pl.BlockSpec((tokens, half), lambda i, s: (i, 0))
    return order.call(
        input_back_kernel,
        (2,),
        [rows, rows, whole(vectors.shape), whole(w_own.shape), whole(w_far.shape)]
        + [half_rows] * 6
        + [whole((basis, half))] * 4,
        [
            pl.BlockSpec((1, tokens, width), lambda i, s: (s[0], 0, 0)),
            whole((tokens, width)),
            pl.BlockSpec((1, basis // 2, width), lambda i, s: (s[0], 0, 0)),
            whole((basis // 2, width)),
            whole((8, width)),
        ],
        [
            shape_of((2, tokens, width), F32),
            shape_of((tokens, width), BF16),
            shape_of((2, basis // 2, width), F32),
            shape_of((basis // 2, width), BF16),
            shape_of((8, width), F32),
        ],
        6 * length * width * width,
        "input_back",
        (hid, mid_grad, vectors, w_own, w_far, *own[:3], *far[:3], *own[3:5], *far[3:5]),
        scratch=[pltpu.VMEM((basis, width), F32)],
        scalars=(scalars,),
    )


def tokens_place_kernel(scalars, *refs):
    for come, out in zip(refs[:3], refs[6:]):
        out[0] = come[...].astype(out.dtype)


def tokens_place(order, scalars, filled, come):
    return order.call(
        tokens_place_kernel,
        (1,),
        [whole(c.shape) for c in come] + [pl.BlockSpec(memory_space=pl.ANY)] * 3,
        [pl.BlockSpec((1,) + f.shape[1:], lambda i, s: (1 - s[0], 0, 0)) for f in filled],
        [shape_of(f.shape, f.dtype) for f in filled],
        0,
        "tokens_place",
        tuple(come) + tuple(filled),
        scalars=(scalars,),
        aliases={4 + index: index for index in range(3)},
    )


def pack_kernel(own_maps, own_sums, own_bias, far_maps, far_sums, far_bias, mid_sums, first_sums, own, far):
    for maps, sums, bias, out in (
        (own_maps, own_sums, own_bias, own),
        (far_maps, far_sums, far_bias, far),
    ):
        row = 0

        def put(values):
            nonlocal row
            for start in range(0, values.shape[1], 128):
                out[row : row + 1] = values[:, start : start + 128]
                row += 1

        for pair in range(maps.shape[0]):
            for index in range(4):
                put(maps[pair, index : index + 1])
        for index in (8, 9):
            for pair in range(maps.shape[0]):
                put(sums[pair, index : index + 1])
        put(bias[0:1])
        for index in range(4):
            put(mid_sums[index : index + 1])
        for index in range(2):
            put(first_sums[index : index + 1])
        for pair in range(maps.shape[0]):
            for index in range(4):
                put(sums[pair, index : index + 1])
        out[row:] = jnp.zeros((out.shape[0] - row, 128), F32)


def pack(order, own, own_bias, far, far_bias, mid_sums, first_sums):
    operands = (own[6], own[7], own_bias, far[6], far[7], far_bias, mid_sums, first_sums)
    pairs, _, basis = own[6].shape
    width = mid_sums.shape[1]
    count = pairs * 4 * (basis // 128) + 6 * pairs + own_bias.shape[1] // 128 + 6 * width // 128
    count += -count % 8
    return order.call(
        pack_kernel,
        (1,),
        [whole(o.shape) for o in operands],
        [whole((count, 128))] * 2,
        [shape_of((count, 128), F32)] * 2,
        0,
        "pack",
        operands,
    )


def to_peer(values):
    return jax.tree.map(lambda v: lax.ppermute(v, "mp", [(0, 1), (1, 0)]), values)


def across(values, offset, count):
    return lax.ppermute(values, "batch", [(i, i ^ offset) for i in range(count)])


def added(left, right):
    return left + right


def halve_kernel(flip, scalars, *refs):
    for chunk in range(2):
        low, high, low_more, high_more = refs[4 * chunk : 4 * chunk + 4]
        keep, send = refs[8 + 2 * chunk : 10 + 2 * chunk]
        bit = scalars[1 + (chunk ^ flip)]

        @pl.when(bit == 0)
        def _():
            keep[...] = added(low[...], low_more[...])
            send[...] = added(high[...], high_more[...])

        @pl.when(bit != 0)
        def _():
            keep[...] = added(high[...], high_more[...])
            send[...] = added(low[...], low_more[...])


def share_kernel(group, scalars, keep_a, more_a, keep_b, more_b, *outs):
    rows_a = keep_a.shape[0] // group
    rows_b = keep_b.shape[0] // group
    width = keep_b.shape[1]
    for offset in range(group):
        place = scalars[3 + offset]
        at = pl.ds(pl.multiple_of(place * rows_a, rows_a), rows_a)
        share = added(keep_a[at, :], more_a[at, :])
        for part in range(keep_a.shape[1] // width):
            outs[offset][part * rows_a : (part + 1) * rows_a] = share[
                :, part * width : (part + 1) * width
            ]
        at = pl.ds(pl.multiple_of(place * rows_b, rows_b), rows_b)
        outs[offset][outs[offset].shape[0] - rows_b :] = added(keep_b[at, :], more_b[at, :])


def total_kernel(*refs):
    total = refs[0][...].astype(F32)
    for ref in refs[1:-1]:
        total += ref[...].astype(F32)
    refs[-1][...] = total.astype(BF16)


def spread_kernel(group, scalars, *refs):
    out = refs[group]
    rows = out.shape[0] // group
    for offset in range(group):
        at = pl.ds(pl.multiple_of(scalars[3 + offset] * rows, rows), rows)
        out[at, :] = refs[offset][...]


def small_kernel(left, right, out):
    out[...] = left[...] + right[...]


def small_add(order, left, right):
    return order.call(
        small_kernel,
        (1,),
        [whole(left.shape)] * 2,
        [whole(left.shape)],
        [shape_of(left.shape, F32)],
        0,
        "small_add",
        (left, right),
    )[0]


class BatchSum:
    def __init__(self, order, scalars, count):
        self.order = order
        self.scalars = scalars
        self.count = count
        self.group = min(4, count // 4)

    def halve(self, flip, quads):
        specs = []
        operands = []
        out_specs = []
        shapes = []
        for shape, quad in quads:
            cuts = self.cuts(shape[0])
            piece = (shape[0] // cuts, shape[1])
            for values, block in quad:
                specs.append(
                    pl.BlockSpec(
                        piece, lambda i, s, block=block, cuts=cuts: (block[0] * cuts + i, block[1])
                    )
                )
                operands.append(values)
            out_specs += [pl.BlockSpec(piece, lambda i, s: (i, 0))] * 2
            shapes += [shape, shape]
        keep_a, send_a, keep_b, send_b = self.order.call(
            functools.partial(halve_kernel, flip),
            (cuts,),
            specs,
            out_specs,
            [shape_of(s, BF16) for s in shapes],
            0,
            "halve",
            operands,
            scalars=(self.scalars,),
        )
        self.kept = (keep_a, keep_b)
        self.come = (
            across(send_a, 1 << flip, self.count),
            across(send_b, 2 >> flip, self.count),
        )

    def cuts(self, rows):
        return 1

    def first(self, quads):
        self.halve(0, quads)

    def second(self):
        quads = []
        for kept, come in zip(self.kept, self.come):
            shape = (kept.shape[0] // 2, kept.shape[1])
            quads.append((shape, ((kept, (0, 0)), (kept, (1, 0)), (come, (0, 0)), (come, (1, 0)))))
        self.halve(1, quads)

    def around(self, own):
        return [own[0]] + [
            across(own[offset], offset << 2, self.count) for offset in range(1, self.group)
        ]

    def share(self):
        operands = (self.kept[0], self.come[0], self.kept[1], self.come[1])
        width = operands[2].shape[1]
        shape = ((operands[0].size + operands[2].size) // (width * self.group), width)
        self.shares = self.around(
            self.order.call(
                functools.partial(share_kernel, self.group),
                (1,),
                [whole(o.shape) for o in operands],
                [whole(shape)] * self.group,
                [shape_of(shape, BF16)] * self.group,
                0,
                "share",
                operands,
                scalars=(self.scalars,),
            )
        )

    def total(self):
        shape = self.shares[0].shape
        (self.mine,) = self.order.call(
            total_kernel,
            (1,),
            [whole(shape)] * self.group,
            [whole(shape)],
            [shape_of(shape, BF16)],
            0,
            "total",
            self.shares,
        )
        offset = 4 * self.group
        while offset < self.count:
            self.mine = added(self.mine, across(self.mine, offset, self.count))
            offset *= 2

    def around_rest(self):
        self.pieces = self.around([self.mine] * self.group)

    def spread(self):
        rows, width = self.mine.shape
        shape = (self.group * rows, width)
        (quarter,) = self.order.call(
            functools.partial(spread_kernel, self.group),
            (1,),
            [whole(p.shape) for p in self.pieces],
            [whole(shape)],
            [shape_of(shape, BF16)],
            0,
            "spread",
            self.pieces,
            scalars=(self.scalars,),
        )
        self.quarters = [quarter] + [
            across(quarter, offset, self.count) for offset in (1, 2, 3)
        ]


def peers_added_kernel(*refs):
    for index in range(2):
        refs[4 + index][...] = added(refs[2 * index][...], refs[2 * index + 1][...])
    refs[6][...] = jnp.zeros_like(refs[6])


def peers_added(order, up_pair, down_pair):
    cuts = 2
    width = down_pair[0].shape[1]
    up_spec = pl.BlockSpec((up_pair[0].shape[0] // cuts, width), lambda i: (i, 1))
    up_out = pl.BlockSpec((up_pair[0].shape[0] // cuts, width), lambda i: (i, 0))
    down_spec = pl.BlockSpec((down_pair[0].shape[0] // cuts, width), lambda i: (i, 0))
    return order.call(
        peers_added_kernel,
        (cuts,),
        [up_spec, up_spec, down_spec, down_spec],
        [up_out, down_spec, whole((8, 128))],
        [
            shape_of((up_pair[0].shape[0], width), BF16),
            shape_of(down_pair[0].shape, BF16),
            shape_of((8, 128), F32),
        ],
        0,
        "peers_added",
        tuple(up_pair) + tuple(down_pair),
    )[:2]


def feed_place_kernel(up_sum, down_sum, _, up_out, down_out):
    up_out[...] = up_sum[...].astype(F32)
    down_out[...] = down_sum[...].astype(F32)


def feed_place(order, up_sum, down_sum, up_grad):
    cuts = 4
    width = down_sum.shape[1]
    up_rows = up_sum.shape[0] // cuts
    down_rows = down_sum.shape[0] // cuts
    return order.call(
        feed_place_kernel,
        (cuts,),
        [
            pl.BlockSpec((up_rows, width), lambda i: (i, 0)),
            pl.BlockSpec((down_rows, width), lambda i: (i, 0)),
            pl.BlockSpec(memory_space=pl.ANY),
        ],
        [
            pl.BlockSpec((up_rows, width), lambda i: (i, 1)),
            pl.BlockSpec((down_rows, width), lambda i: (i, 0)),
        ],
        [shape_of(up_grad.shape, F32), shape_of(down_sum.shape, F32)],
        0,
        "feed_place",
        (up_sum, down_sum, up_grad),
        aliases={2: 0},
    )


def mixed_halve_kernel(scalars, *refs):
    for chunk in range(2):
        keep, send = refs[16 + 2 * chunk : 18 + 2 * chunk]
        bit = scalars[1 + chunk]

        def fill(target, half):
            own, own_more, peer, peer_more = refs[8 * chunk + 4 * half : 8 * chunk + 4 * half + 4]
            rows = own.shape[0]
            target[:rows] = added(own[...], peer[...])
            target[rows:] = added(own_more[...], peer_more[...])

        @pl.when(bit == 0)
        def _():
            fill(keep, 0)
            fill(send, 1)

        @pl.when(bit != 0)
        def _():
            fill(keep, 1)
            fill(send, 0)


class MixedSum(BatchSum):
    def first(self, dqkv, dwo, du):
        width, cols = dwo[0].shape
        part = width // 2
        steps = cols // 128
        specs = []
        operands = []
        for chunk in range(2):
            for half in range(2):
                main = dwo if (chunk, half) == (1, 1) else dqkv
                block = 0 if main is dwo else 2 * chunk + half
                for side in range(2):
                    specs.append(pl.BlockSpec((width, 128), lambda i, s, b=block: (b, i)))
                    specs.append(
                        pl.BlockSpec((part, 128), lambda i, s, h=half, c=chunk: (h, steps * c + i))
                    )
                    operands += [main[side], du[side]]
        shape = (width + part, cols)
        keep_a, send_a, keep_b, send_b = self.order.call(
            mixed_halve_kernel,
            (steps,),
            specs,
            [pl.BlockSpec((width + part, 128), lambda i, s: (0, i))] * 4,
            [shape_of(shape, BF16)] * 4,
            0,
            "mixed_halve",
            operands,
            scalars=(self.scalars,),
        )
        self.kept = (keep_a, keep_b)
        self.come = (across(send_a, 1, self.count), across(send_b, 2, self.count))


def mixed_place_kernel(group, scalars, *refs):
    qkv_out, up_out, wo_out = refs[-3:]
    cols = refs[0].shape[1]
    width = wo_out.shape[1]
    part = width // 2
    rows = refs[0].shape[0] // (2 * group)

    def segments(quarter, place):
        start = (quarter * group + place) * rows
        marks = [start] + [m for m in (part, width) if start < m < start + rows] + [start + rows]
        return [(a, a - start, b - a) for a, b in zip(marks, marks[1:])]

    for index in range(4):
        column = scalars[1] ^ (index % 2)
        row = scalars[2] ^ (index // 2)
        values = refs[index]
        for quarter in range(2):

            @pl.when(row == quarter)
            def _():
                for place in range(group):
                    for at, inner, size in segments(quarter, place):
                        start = 2 * place * rows + inner
                        piece = values[start : start + size].astype(F32)
                        if at < width:
                            to = pl.multiple_of(column * width + at, 16)
                            qkv_out[pl.ds(to, size), :] = piece
                        else:
                            to = pl.multiple_of(column * part + at - width, 16)
                            up_out[pl.ds(to, size), :cols] = piece

            for half in range(2):

                @pl.when((column == quarter) & (row == half))
                def _():
                    for place in range(group):
                        for at, inner, size in segments(quarter, place):
                            start = (2 * place + 1) * rows + inner
                            piece = values[start : start + size].astype(F32)
                            if at >= width:
                                to = half * part + at - width
                                up_out[to : to + size, cols:] = piece
                            elif half == 0:
                                qkv_out[2 * width + at : 2 * width + at + size] = piece
                            elif at < part:
                                wo_out[at : at + size, :cols] = piece
                            else:
                                wo_out[at - part : at - part + size, cols:] = piece


def mixed_place(order, scalars, summed, width, hidden):
    half = width // 2
    return order.call(
        functools.partial(mixed_place_kernel, summed.group),
        (1,),
        [whole(o.shape) for o in summed.quarters],
        [
            whole((3 * width, half)),
            pl.BlockSpec((width, width), lambda i, s: (0, 0)),
            whole((half, width)),
        ],
        [
            shape_of((3 * width, half), F32),
            shape_of((width, hidden), F32),
            shape_of((half, width), F32),
        ],
        0,
        "mixed_place",
        summed.quarters,
        scalars=(scalars,),
    )


def per_device(
    count,
    hidden_in,
    memory_flags,
    memory_coeffs,
    first_gain,
    first_bias,
    query_key_value_matrix,
    qv_bias,
    memory_weight,
    memory_bias,
    output_matrix,
    out_bias,
    second_gain,
    second_bias,
    up_matrix,
    up_bias_vector,
    down_matrix,
    down_bias,
    out_grad,
):
    me = lax.axis_index("mp")
    position = lax.axis_index("batch")
    width = hidden_in.shape[2]
    half = width // 2
    group = min(4, count // 4)
    place = (position >> 2) % group
    scalars = jnp.stack(
        [me, position & 1, (position >> 1) & 1] + [place ^ offset for offset in range(group)]
    ).astype(jnp.int32)

    def from_peer(values):
        return to_peer(lax.dynamic_index_in_dim(values, 1 - me, 0, keepdims=False))

    hidden_come = from_peer(hidden_in)
    w_own = jnp.transpose(query_key_value_matrix, (1, 0, 2))
    w_far = to_peer(w_own)
    coeffs_come = from_peer(memory_coeffs)
    qv_far, mw_far, mb_far, ub_far = to_peer(
        (qv_bias, memory_weight, memory_bias, up_bias_vector)
    )

    query_bias = jnp.concatenate([qv_bias, qv_far], axis=1).astype(F32)
    mem_maps = jnp.concatenate([memory_weight, mw_far], axis=1).astype(F32)
    mem_maps = jnp.transpose(mem_maps, (1, 0, 2))
    mem_biases = jnp.concatenate([memory_bias, mb_far], axis=1).astype(F32)
    vectors = jnp.stack(
        [first_gain, first_bias, out_bias, second_gain, second_bias, down_bias] + [down_bias] * 2
    )
    up_biases = jnp.stack([ub_far, up_bias_vector]).astype(F32)
    order = Order()
    hid, norm_t, q, k, v, mem_k, mem_v, coeffs_t = project(
        order, scalars, hidden_in, hidden_come, vectors, w_own, w_far, query_bias, memory_coeffs, coeffs_come
    )
    later, _ = lax.optimization_barrier(
        ((output_matrix, out_grad, up_matrix, down_matrix), (coeffs_t, mw_far, mb_far, ub_far))
    )
    wo_far = to_peer(later[0])
    out_grad_come = from_peer(later[1])
    up_far = to_peer(later[2])
    down_far = to_peer(later[3])
    att_t, mix_t, mix, stat = attend(
        order, scalars, memory_flags, q, k, v, mem_k, mem_v, mem_maps, mem_biases
    )
    (
        du_far,
        du_own,
        dub_far,
        dub_own,
        dd_far,
        dd_own,
        block_mine,
        block_theirs,
        mid_grad,
        mix_grad,
        dwo_own,
        dwo_far,
        mid_sums,
    ) = feed(
        order,
        scalars,
        mix,
        hid,
        mix_t,
        output_matrix,
        wo_far,
        out_grad,
        out_grad_come,
        vectors,
        up_far,
        up_matrix,
        up_biases,
        up_biases,
        down_far,
        down_matrix,
    )
    du_peer, dd_peer = to_peer((du_far, dd_far))
    dwo_peer = to_peer(dwo_far)
    back_args = (
        scalars, memory_flags, q, k, v, mem_k, mem_v, mem_maps, mix_grad, att_t, stat, norm_t, coeffs_t
    )
    pairs = width // 256
    far = attend_back(order, 1, 0, pairs, None, *back_args)
    up_sum, down_sum = peers_added(order, (du_own, du_peer), (dd_own, dd_peer))
    dqkv_peer = to_peer(far[5])
    up_sum, down_sum = lax.psum((up_sum, down_sum), "batch")
    block_come = to_peer(block_theirs)
    own = attend_back(order, 0, 0, pairs, None, *back_args)
    dqkv_own = own[5]
    last = MixedSum(order, scalars, count)
    last.first((dqkv_own, dqkv_peer), (dwo_own, dwo_peer), (du_own, du_peer))
    in_mine, in_theirs, coeff_mine, coeff_theirs, first_sums = input_back(
        order, scalars, hid, mid_grad, vectors, w_own, w_far, own, far
    )
    small, far_flat = pack(order, own, dub_own, far, dub_far, mid_sums, first_sums)
    last.second()
    come, in_come, coeff_come = to_peer(
        lax.optimization_barrier((far_flat, in_theirs, coeff_theirs, last.kept[0]))[:3]
    )
    block_out, input_grad, coeff_grad = tokens_place(
        order, scalars, (block_mine, in_mine, coeff_mine), (block_come, in_come, coeff_come)
    )
    last.share()
    small = small_add(order, small, come)
    small = small_add(order, small, across(small, 1, count))
    last.total()
    last.around_rest()
    small = small_add(order, small, across(small, 2, count))
    last.spread()
    offset = 4
    while offset < count:
        small = small_add(order, small, across(small, offset, count))
        offset *= 2
    query_key_value_grad, up_weight_grad, output_matrix_grad = mixed_place(
        order, scalars, last, width, up_matrix.shape[1]
    )
    query_key_value_grad = jnp.transpose(
        query_key_value_grad.reshape(3, width, half), (1, 0, 2)
    )
    up_weight_grad, down_weight_grad = feed_place(order, up_sum, down_sum, up_weight_grad)

    heads, basis = memory_weight.shape[1:]
    rows = 0

    def take(size):
        nonlocal rows
        piece = small[rows : rows + size // 128]
        rows += size // 128
        return piece

    memory_weight_grad = jnp.transpose(take(2 * heads * basis).reshape(heads, 2, basis), (1, 0, 2))
    qv_bias_grad = take(2 * half).reshape(2, half)
    up_bias_grad = take(up_bias_vector.shape[0]).reshape(-1)
    vector_grads = [take(width).reshape(-1) for _ in range(6)]
    memory_bias_grad = jnp.transpose(take(2 * heads * 128)[:, 0].reshape(heads, 2), (1, 0))
    return (
        block_out,
        input_grad,
        coeff_grad,
        vector_grads[4],
        vector_grads[5],
        query_key_value_grad,
        qv_bias_grad,
        memory_weight_grad,
        memory_bias_grad,
        output_matrix_grad,
        vector_grads[0],
        vector_grads[1],
        vector_grads[2],
        up_weight_grad,
        up_bias_grad,
        down_weight_grad,
        vector_grads[3],
    )


def solution(mesh):
    tokens = P("batch", "mp", None)
    return jax.shard_map(
        functools.partial(per_device, mesh.shape["batch"]),
        mesh=mesh,
        in_specs=(
            tokens,
            P("batch"),
            tokens,
            P(),
            P(),
            P(None, None, "mp"),
            P(None, "mp"),
            P(None, "mp", None),
            P(None, "mp"),
            P("mp", None),
            P(),
            P(),
            P(),
            P(None, "mp"),
            P("mp"),
            P("mp", None),
            P(),
            tokens,
        ),
        out_specs=(
            tokens,
            tokens,
            tokens,
            P(),
            P(),
            P(None, None, "mp"),
            P(None, "mp"),
            P(None, "mp", None),
            P(None, "mp"),
            P("mp", None),
            P(),
            P(),
            P(),
            P(None, "mp"),
            P("mp"),
            P("mp", None),
            P(),
        ),
        check_vma=False,
    )
```
